32 devices in a mesh: rows: 8 (over y, x, core), heads: 4 (over z).
Axes of the slice: x: 2, y: 2, z: 4, core: 2. Of those that a mesh axis runs over, the one named last changes fastest.
Arguments:
- tokens: bfloat16 [8, 2048, 768], P('rows', 'heads'), may hold values from -6 to 6
- segment_ids: int32 [8, 2048], P('rows'), may hold values from 0 to 7, as said below
- w_qkv: bfloat16 [768, 3, 768], P(None, None, 'heads'), may hold values from -0.21875 to 0.21875
- b_qkv: float32 [3, 768], P(None, 'heads'), may hold values from -3 to 3
- w_out: bfloat16 [768, 768], P('heads'), may hold values from -0.75 to 0.75
- b_out: float32 [768], replicated, may hold values from -3 to 3
- gain_one: float32 [768], replicated, may hold values from 0.25 to 1.75
- bias_one: float32 [768], replicated, may hold values from -3 to 3
- w_up: bfloat16 [768, 3072], P(None, 'heads'), may hold values from -0.21875 to 0.21875
- b_up: float32 [3072], P('heads'), may hold values from -3 to 3
- w_down: bfloat16 [3072, 768], P('heads'), may hold values from -0.109375 to 0.109375
- b_down: float32 [768], replicated, may hold values from -3 to 3
- gain_two: float32 [768], replicated, may hold values from 0.25 to 1.75
- bias_two: float32 [768], replicated, may hold values from -3 to 3
- omega: bfloat16 [64, 256], replicated, may hold values from -4 to 4
- cotangent: bfloat16 [8, 2048, 768], P('rows', 'heads'), may hold values from -6 to 6
Outputs:
- layer_output: bfloat16 [8, 2048, 768], P('rows', 'heads')
- grad_tokens: float32 [8, 2048, 768], P('rows', 'heads')
- grad_w_qkv: float32 [768, 3, 768], P(None, None, 'heads')
- grad_b_qkv: float32 [3, 768], P(None, 'heads')
- grad_w_out: float32 [768, 768], P('heads')
- grad_b_out: float32 [768], replicated
- grad_gain_one: float32 [768], replicated
- grad_bias_one: float32 [768], replicated
- grad_w_up: float32 [768, 3072], P(None, 'heads')
- grad_b_up: float32 [3072], P('heads')
- grad_w_down: float32 [3072, 768], P('heads')
- grad_b_down: float32 [768], replicated
- grad_gain_two: float32 [768], replicated
- grad_bias_two: float32 [768], replicated
The draws below stay inside these ranges and needn't reach their ends.
Inputs may be any that keep to these rules, and one draw needn't show every extreme that they name: `segment_ids`: every row holds all 8 documents, numbered in order of position; each document has at least one position.
All inputs are finite; a program needn't handle non-finite values.
Results may differ from the reference program's by a relative error of at most 0.025.
Values may be sent and summed in bfloat16 or wider, within the bound.
No kernel may reach another device: no remote copies, remote signals or barrier semaphores. Data moves between devices by JAX's collectives and lax.ppermute only.
A program may use at most 192 MiB of HBM per device.

```python
import jax
import jax.numpy as jnp
from jax import lax

D = 768
HEADS = 12
HD = 64
FF = 3072
FEATS = 256
SEGS = 8
L = 2048
ROWS = 8


def draw_segment_ids(key, part):
    key = jax.random.fold_in(key, 7)

    def one_row(row_key):
        cuts = (1 + jax.random.permutation(row_key, L - 1)[:SEGS - 1]).astype(jnp.int32)
        positions = jnp.arange(L, dtype=jnp.int32)
        return jnp.sum((positions[:, None] >= cuts[None, :]).astype(jnp.int32), axis=1)
    return jax.vmap(one_row)(jax.random.split(key, ROWS)).astype(jnp.int32)


def level_of(stream_key, extent, cuts, least, high):
    level, own = 1.0, jax.random.fold_in(stream_key, 6)
    for dim, shards_of in cuts:
        heights = jnp.exp(jax.random.uniform(jax.random.fold_in(own, dim), (shards_of,), jnp.float32, least / len(cuts), high / len(cuts)))
        level = level * jnp.repeat(heights, extent[dim] // shards_of).reshape([-1 if axis == dim else 1 for axis in range(len(extent))])
    return level


def noise(own_key, extent, scale, limit, cuts=(), held_as=jnp.bfloat16):
    values = scale * jax.random.normal(own_key, extent, jnp.float32)
    if cuts:
        values = values * level_of(own_key, extent, cuts, -0.22, 0.18)
    return jnp.clip(values, -limit, limit).astype(held_as)


def setup_inputs(seed: int = 0) -> dict:
    key_list = jax.random.split(jax.random.key(seed), 17)
    return {
        "tokens": noise(key_list[0], (ROWS, L, D), 1.0, 6.0, ((0, 8), (1, 4))),
        "segment_ids": draw_segment_ids(jax.random.fold_in(key_list[16], 71), 0),
        "w_qkv": noise(key_list[2], (D, 3, D), D ** -0.5, 0.21875, ((2, 4),)),
        "b_qkv": noise(key_list[3], (3, D), 0.3, 3.0, ((1, 4),), jnp.float32),
        "w_out": noise(key_list[4], (D, D), HD ** -0.5, 0.75, ((0, 4),)),
        "b_out": noise(key_list[5], (D,), 0.5, 3.0, (), jnp.float32),
        "gain_one": jnp.clip(1.0 + 0.15 * jax.random.normal(key_list[6], (D,), jnp.float32), 0.25, 1.75),
        "bias_one": noise(key_list[7], (D,), 0.5, 3.0, (), jnp.float32),
        "w_up": noise(key_list[8], (D, FF), D ** -0.5, 0.21875, ((1, 4),)),
        "b_up": noise(key_list[9], (FF,), 0.5, 3.0, ((0, 4),), jnp.float32),
        "w_down": noise(key_list[10], (FF, D), FF ** -0.5, 0.109375, ((0, 4),)),
        "b_down": noise(key_list[11], (D,), 0.5, 3.0, (), jnp.float32),
        "gain_two": jnp.clip(1.0 + 0.15 * jax.random.normal(key_list[12], (D,), jnp.float32), 0.25, 1.75),
        "bias_two": noise(key_list[13], (D,), 0.5, 3.0, (), jnp.float32),
        "omega": noise(key_list[14], (HD, FEATS), 1.0, 4.0),
        "cotangent": noise(key_list[15], (ROWS, L, D), 1.0, 6.0, ((0, 8), (1, 4))),
    }


PRECISE = lax.Precision.HIGHEST
EPSILON = 1e-05

@jax.custom_vjp
def low(v):
    return lax.optimization_barrier(v.astype(jnp.bfloat16)).astype(jnp.float32)

@jax.custom_vjp
def low_back(v):
    return v

def low_keep(v):
    return (low(v), None)

def low_pass(kept, grad):
    return (grad,)

def back_keep(v):
    return (v, None)

def back_low(kept, grad):
    return (low(grad),)
low.defvjp(low_keep, low_pass)
low_back.defvjp(back_keep, back_low)

def layer_norm(hidden, gain, bias):
    average = lax.optimization_barrier(jnp.mean(hidden, axis=-1, keepdims=True))
    centred = hidden - average
    variance = lax.optimization_barrier(jnp.mean(centred * centred, axis=-1, keepdims=True))
    return centred * lax.rsqrt(variance + EPSILON) * gain + bias

def feature_map(vectors, omega):
    feat_scale = HD ** (-0.25)
    projected = feat_scale * low_back(jnp.dot(vectors, omega, precision=PRECISE))
    half_norm = 0.5 * feat_scale * feat_scale * lax.optimization_barrier(jnp.sum(vectors * vectors, axis=-1, keepdims=True))
    return low(jnp.exp(projected - half_norm) * FEATS ** (-0.5))

def favor(queries, key_rows, values, omega, onehot):
    feat_q = feature_map(queries, omega)
    feat_k = feature_map(key_rows, omega)
    spread = (onehot[:, :, None] * values[:, None, :]).reshape(L, SEGS * HD)
    state_sums = low(low_back(jnp.dot(feat_k.T, spread, precision=PRECISE)))
    state_norms = low(low_back(jnp.dot(feat_k.T, onehot, precision=PRECISE)))
    blocks = jnp.dot(feat_q, state_sums, precision=PRECISE).reshape(L, SEGS, HD)
    numerator = lax.optimization_barrier(jnp.sum(onehot[:, :, None] * blocks, axis=1))
    denominator = lax.optimization_barrier(jnp.sum(onehot * jnp.dot(feat_q, state_norms, precision=PRECISE), axis=1, keepdims=True))
    return low_back(numerator) / low_back(denominator)

def layer(tokens_in, w_qkv, b_qkv, w_out, b_out, gain_one, bias_one, w_up, b_up, w_down, b_down, gain_two, bias_two, omega, onehot):
    projected = jnp.dot(tokens_in, w_qkv.reshape(D, 3 * D), precision=PRECISE)
    triple = low(low_back(projected) + b_qkv.reshape(3 * D))
    pieces = triple.reshape(L, 3, HEADS, HD)
    attend = jax.vmap(lambda a, b, c: favor(a, b, c, omega, onehot), in_axes=1, out_axes=1)
    attended = low(attend(pieces[:, 0], pieces[:, 1], pieces[:, 2]).reshape(L, D))
    mixed = low_back(jnp.dot(attended, w_out, precision=PRECISE)) + b_out
    first_out = layer_norm(tokens_in + mixed, gain_one, bias_one)
    hidden_pre = low_back(jnp.dot(low(first_out), w_up, precision=PRECISE)) + b_up
    activated = low(jax.nn.gelu(hidden_pre, approximate=False))
    ffn_branch = low_back(jnp.dot(activated, w_down, precision=PRECISE)) + b_down
    return layer_norm(first_out + ffn_branch, gain_two, bias_two)

def reference(tokens, segment_ids, w_qkv, b_qkv, w_out, b_out, gain_one, bias_one, w_up, b_up, w_down, b_down, gain_two, bias_two, omega, cotangent):
    params = tuple((p.astype(jnp.float32) for p in (w_qkv, b_qkv, w_out, b_out, gain_one, bias_one, w_up, b_up, w_down, b_down, gain_two, bias_two)))
    omega_wide = omega.astype(jnp.float32)

    def one_row(totals, row):
        tokens_row, seg_row, cot_row = row
        onehot = (seg_row[:, None] == jnp.arange(SEGS, dtype=jnp.int32)[None, :]).astype(jnp.float32)

        def forward(tokens_in, *weights):
            return layer(tokens_in, *weights, omega_wide, onehot)
        layer_out, pullback = jax.vjp(forward, tokens_row.astype(jnp.float32), *params)
        gradients = pullback(cot_row.astype(jnp.float32))
        totals = tuple((t + g for t, g in zip(totals, gradients[1:])))
        return (totals, (layer_out.astype(jnp.bfloat16), gradients[0]))
    zeros_init = tuple((jnp.zeros_like(p) for p in params))
    totals, (layer_output, grad_tokens) = lax.scan(one_row, zeros_init, (tokens, segment_ids, cotangent))
    return (layer_output, grad_tokens, totals[0], totals[1], totals[2], totals[3], totals[4], totals[5], totals[6], totals[7], totals[8], totals[9], totals[10], totals[11])
```

```python
import functools

import jax
import jax.numpy as jnp
from jax import lax
from jax.experimental import pallas as pl
from jax.experimental.pallas import tpu as pltpu
from jax.sharding import PartitionSpec as P

EPSILON = 1e-05
PLANE = 8
VMEM_LIMIT = 48 * 1024 * 1024
BF = jnp.bfloat16
F32 = jnp.float32


def dot(a, b, dims=((1,), (0,))):
    return lax.dot_general(a, b, (dims, ((), ())), preferred_element_type=F32)


def dot_nt(a, b):
    return dot(a, b, ((1,), (1,)))


def dot_tn(a, b):
    return dot(a, b, ((0,), (0,)))


def estimate(us):
    return pl.CostEstimate(flops=int(us * 1.1e9), bytes_accessed=0, transcendentals=0)


def call(kernel, grid, in_specs, out_specs, out_shape, args, us, scratch=()):
    return pl.pallas_call(
        kernel,
        grid=grid,
        in_specs=in_specs,
        out_specs=out_specs,
        out_shape=out_shape,
        scratch_shapes=list(scratch),
        compiler_params=pltpu.CompilerParams(vmem_limit_bytes=VMEM_LIMIT),
        cost_estimate=estimate(us),
    )(*args)


def whole(*shape):
    return pl.BlockSpec(shape, lambda g: (0,) * len(shape))


def part(*shape):
    return pl.BlockSpec((None, *shape), lambda g: (g,) + (0,) * len(shape))


def struct(shape, dtype):
    return jax.ShapeDtypeStruct(shape, dtype)


def permute(array, axis, size, partner):
    return lax.ppermute(array, axis, [(i, partner(i)) for i in range(size)])


def first_partner(i):
    return i ^ (4 if i & 1 else 2)


def second_partner(i):
    return i ^ (2 if i & 1 else 4)


def core_partner(i):
    return i ^ 1


def plane_gather(piece, rows):
    p0 = piece
    p1 = permute(p0, "rows", rows, first_partner)
    p2 = permute(p0, "rows", rows, second_partner)
    p3 = permute(p1, "rows", rows, second_partner)
    own = [p0, p1, p2, p3]
    return own + [permute(p, "rows", rows, core_partner) for p in own]


def plane_slots(rank):
    me = rank & (PLANE - 1)
    core = rank & 1
    first = jnp.where(core == 1, 4, 2)
    second = jnp.where(core == 1, 2, 4)
    return [
        me,
        me ^ first,
        me ^ second,
        me ^ 6,
        me ^ 1,
        me ^ 1 ^ second,
        me ^ 1 ^ first,
        me ^ 7,
    ]


def to_heads(array):
    return lax.all_to_all(array, "heads", 0, 0, tiled=True)


def reduce_grads(sent, kept, rank, rows):
    came = permute(sent, "rows", rows, core_partner)
    core = rank & 1
    mine = (rank & (PLANE - 1)) >> 1
    first = jnp.where(core == 1, 2, 1)
    second = jnp.where(core == 1, 1, 2)

    def pick(slot):
        a = lax.dynamic_index_in_dim(kept, slot, 1, keepdims=False)
        b = lax.dynamic_index_in_dim(came, slot, 1, keepdims=False)
        return a.astype(F32) + b.astype(F32)

    sent = jnp.stack([pick(mine ^ second), pick(mine ^ 3)]).astype(BF)
    came2 = permute(sent, "rows", rows, second_partner)
    sent = (pick(mine ^ first) + came2[1].astype(F32)).astype(BF)
    came3 = permute(sent, "rows", rows, first_partner)
    total = pick(mine) + came2[0].astype(F32) + came3.astype(F32)
    mask = PLANE
    while mask < rows:
        total = total + permute(
            total.astype(BF), "rows", rows, lambda i, m=mask: i ^ m
        ).astype(F32)
        mask *= 2
    total = to_heads(total.astype(BF)).astype(F32)
    return plane_gather(jnp.sum(total, axis=0).astype(BF), rows)


SMEM_SPEC = pl.BlockSpec(memory_space=pltpu.SMEM)
VMEM_SPEC = pl.BlockSpec(memory_space=pltpu.VMEM)


def place_weights_kernel(count, parts, info_ref, *refs):
    owns = refs[:parts]
    pieces = refs[parts : parts + count]
    outs = refs[parts + count :]
    step = pieces[0].shape[0] // parts
    mine = pl.program_id(0) == info_ref[count]

    @pl.when(mine)
    def _():
        for own, out in zip(owns, outs):
            out[...] = own[...]

    @pl.when(jnp.logical_not(mine))
    def _():
        for n in range(count):
            start = pl.multiple_of(info_ref[n] * step, 16)
            for p, out in enumerate(outs):
                out[pl.ds(start, step), :] = pieces[n][p * step : (p + 1) * step, :]


def place_weights(owns, pieces, info):
    count, parts = len(pieces), len(owns)
    others, rows, cols = pieces[0].shape
    height = owns[0].shape[0]

    def piece_index(g, info_ref):
        return (jnp.maximum((g ^ info_ref[count]) - 1, 0), 0, 0)

    return pl.pallas_call(
        functools.partial(place_weights_kernel, count, parts),
        grid_spec=pltpu.PrefetchScalarGridSpec(
            num_scalar_prefetch=1,
            grid=(others + 1,),
            in_specs=[pl.BlockSpec((height, cols), lambda g, s: (0, 0))] * parts
            + [pl.BlockSpec((None, rows, cols), piece_index)] * count,
            out_specs=[pl.BlockSpec((None, height, cols), lambda g, s: (g, 0, 0))] * parts,
        ),
        out_shape=[struct((others + 1, height, cols), BF)] * parts,
        compiler_params=pltpu.CompilerParams(vmem_limit_bytes=VMEM_LIMIT),
        cost_estimate=estimate(3 * parts),
    )(info, *owns, *pieces)


def place_ffn_kernel(count, info_ref, *refs):
    up, down = refs[count], refs[count + 1]
    step = refs[0].shape[0] // 2
    for n in range(count):
        start = pl.multiple_of(info_ref[n] * step, 16)
        up[pl.ds(start, step), :] = refs[n][:step, :].astype(F32)
        down[pl.ds(start, step), :] = refs[n][step:, :].astype(F32)


def place_ffn(pieces, info):
    rows, cols = pieces[0].shape
    count = len(pieces)
    return pl.pallas_call(
        functools.partial(place_ffn_kernel, count),
        in_specs=[SMEM_SPEC] + [VMEM_SPEC] * count,
        out_specs=[VMEM_SPEC] * 2,
        out_shape=[struct((count * rows // 2, cols), F32)] * 2,
        compiler_params=pltpu.CompilerParams(vmem_limit_bytes=VMEM_LIMIT),
        cost_estimate=estimate(4),
    )(info, *pieces)


def place_attention_kernel(count, cols, width, info_ref, *refs):
    qo, kv = refs[:count], refs[count : 2 * count]
    out_qkv, out_o, bias = refs[2 * count :]
    step = qo[0].shape[0]
    for n in range(count):
        start = pl.multiple_of(info_ref[n] * step, 16)
        wide = qo[n][...].astype(F32)

        @pl.when(start < cols)
        def _():
            out_qkv[pl.ds(start, step), :] = wide[:, :width]
            bias[pl.ds(start, step), :] = wide[:, width:]

        @pl.when(start >= cols)
        def _():
            out_o[pl.ds(pl.multiple_of(start - cols, 16), step), :] = wide[:, :width]

        wide = kv[n][...].astype(F32)
        out_qkv[pl.ds(cols + start, step), :] = wide[:, :width]
        bias[pl.ds(cols + start, step), :] = wide[:, width:]


def place_attention(qo, kv, info, cols, width):
    count = len(qo)
    return pl.pallas_call(
        functools.partial(place_attention_kernel, count, cols, width),
        in_specs=[SMEM_SPEC] + [VMEM_SPEC] * (2 * count),
        out_specs=[VMEM_SPEC] * 3,
        out_shape=[struct((3 * cols, width), F32), struct((cols, width), F32), struct((3 * cols, 128), F32)],
        compiler_params=pltpu.CompilerParams(vmem_limit_bytes=VMEM_LIMIT),
        cost_estimate=estimate(3),
    )(info, *qo, *kv)


def phi_of(raw, vectors, head, hd, feats, scale):
    wide = vectors[:, head * hd : (head + 1) * hd].astype(F32)
    half = 0.5 * scale * scale * jnp.sum(wide * wide, axis=-1, keepdims=True)
    part_raw = raw[:, head * feats : (head + 1) * feats]
    return jnp.exp(scale * part_raw - half) * feats ** (-0.5)


def edge_rows(first, last, head):
    lane = lax.broadcasted_iota(jnp.int32, (first.shape[0], 32), 1)
    return jnp.where(lane == head, first, 0.0) + jnp.where(lane == 16 + head, last, 0.0)


def edge_left(value, norm, first, last, head):
    return jnp.concatenate(
        [value * first, value * last, edge_rows(norm * first, norm * last, head)], axis=1
    ).astype(BF)


def put_edges(edge_ref, states, heads, hd, level):
    cols = heads * hd
    norms = states[0][2 * hd :]
    for state in states[1:]:
        norms = norms + state[2 * hd :]
    firsts = jnp.concatenate([s[:hd] for s in states] + [norms[:16]], axis=0).astype(BF)
    lasts = jnp.concatenate([s[hd : 2 * hd] for s in states] + [norms[16:]], axis=0).astype(BF)
    for m in range(edge_ref.shape[0]):

        @pl.when(m > level)
        def _():
            edge_ref[m] = lasts

        @pl.when(m <= level)
        def _():
            edge_ref[m] = firsts


def take_edges(came_ref, match_ref):
    left = right = None
    count = came_ref.shape[0]
    for m in range(count):
        wide = came_ref[m].astype(F32)
        a, b = wide * match_ref[m], wide * match_ref[count + m]
        left = a if left is None else left + a
        right = b if right is None else right + b
    return left.astype(BF), right.astype(BF)


def stack_edges(f, l, h, hd, cols):
    return jnp.concatenate(
        [f[h * hd : (h + 1) * hd], l[h * hd : (h + 1) * hd], f[cols:], l[cols:]], axis=0
    )


def with_one(value):
    lane = lax.broadcasted_iota(jnp.int32, value.shape, 1)
    return jnp.concatenate([value, jnp.where(lane == 0, 1.0, 0.0).astype(value.dtype)], axis=1)


def keys_kernel(heads, hd, feats, info_ref, x_ref, w_ref, b_ref, om_ref, ends_ref, kv_ref, phi_ref, edge_ref):
    cols = heads * hd
    scale = hd ** (-0.25)
    kv = (dot_nt(x_ref[...], w_ref[...]) + b_ref[...]).astype(BF)
    kv_ref[...] = kv
    raw = dot(kv[:, :cols], om_ref[...])
    first, last = ends_ref[:, 0:1], ends_ref[:, 1:2]
    states = []
    for h in range(heads):
        phi = phi_of(raw, kv, h, hd, feats, scale).astype(BF)
        phi_ref[:, h * feats : (h + 1) * feats] = phi
        value = kv[:, cols + h * hd : cols + (h + 1) * hd].astype(F32)
        states.append(dot_tn(edge_left(value, 1.0, first, last, h), phi))
    put_edges(edge_ref, states, heads, hd, info_ref[PLANE])


def queries_kernel(
    heads, hd, feats, x_ref, w_ref, b_ref, om_ref, same_ref, kv_ref, phik_ref, q_ref, phi_ref, nd_ref
):
    cols = heads * hd
    scale = hd ** (-0.25)
    q = (dot_nt(x_ref[...], w_ref[:cols, :]) + b_ref[...]).astype(BF)
    q_ref[...] = q
    raw = dot(q, om_ref[...])
    same = same_ref[...]
    for h in range(heads):
        phi = phi_of(raw, q, h, hd, feats, scale).astype(BF)
        phi_ref[:, h * feats : (h + 1) * feats] = phi
        scores = dot_nt(phi, phik_ref[:, h * feats : (h + 1) * feats]).astype(BF) * same
        value = kv_ref[:, cols + h * hd : cols + (h + 1) * hd]
        nd_ref[:, 2 * h * hd : 2 * (h + 1) * hd] = dot(scores, with_one(value))


def attend_kernel(
    heads, hd, feats, match_ref, phi_ref, nd_ref, came_ref, ends_ref, w_ref, x_ref, bias_ref, vec_ref,
    att_ref, den_ref, cf_ref, cl_ref, normed_ref, inverse_ref, low_ref, acc_ref,
):
    g = pl.program_id(0)
    cols = heads * hd
    first, last = ends_ref[:, 0:1], ends_ref[:, 1:2]
    lane = lax.broadcasted_iota(jnp.int32, den_ref.shape, 1)
    dens = jnp.zeros(den_ref.shape, F32)
    outs = []
    cf, cl = take_edges(came_ref, match_ref)
    cf_ref[...] = cf
    cl_ref[...] = cl
    for h in range(heads):
        far = dot_nt(phi_ref[:, h * feats : (h + 1) * feats], stack_edges(cf, cl, h, hd, cols))
        nd = nd_ref[:, 2 * h * hd : 2 * (h + 1) * hd]
        num = nd[:, :hd] + first * far[:, :hd] + last * far[:, hd : 2 * hd]
        den = (
            nd[:, hd : hd + 1]
            + first * far[:, 2 * hd + h : 2 * hd + h + 1]
            + last * far[:, 2 * hd + 16 + h : 2 * hd + 17 + h]
        )
        outs.append(num / den)
        dens = dens + jnp.where(lane == h, den, 0.0)
    att = jnp.concatenate(outs, axis=1).astype(BF)
    att_ref[...] = att
    den_ref[...] = dens
    mixed = dot(att, w_ref[cols:, :])

    @pl.when(g == 0)
    def _():
        acc_ref[...] = x_ref[...].astype(F32) + bias_ref[...] + mixed

    @pl.when(g > 0)
    def _():
        acc_ref[...] += mixed

    @pl.when(g == pl.num_programs(0) - 1)
    def _():
        normed, inverse = norm_of(acc_ref[...])
        normed_ref[...] = normed
        inverse_ref[...] = jnp.broadcast_to(inverse, inverse_ref.shape)
        low_ref[...] = (normed * vec_ref[0:1, :] + vec_ref[1:2, :]).astype(BF)


def attend_back_kernel(
    heads, hd, feats, info_ref, dh_ref, w_ref, att_ref, den_ref, phi_ref, ends_ref, dnd_ref, edge_ref
):
    cols = heads * hd
    first, last = ends_ref[:, 0:1], ends_ref[:, 1:2]
    datt = dot_nt(dh_ref[...], w_ref[cols:, :])
    lane = lax.broadcasted_iota(jnp.int32, (datt.shape[0], hd), 1)
    states = []
    for h in range(heads):
        inverse = 1.0 / den_ref[:, h : h + 1]
        part_datt = datt[:, h * hd : (h + 1) * hd]
        att = att_ref[:, h * hd : (h + 1) * hd].astype(F32)
        dnum = part_datt * inverse
        dden = -jnp.sum(part_datt * att, axis=-1, keepdims=True) * inverse
        dnd_ref[:, 2 * h * hd : 2 * (h + 1) * hd] = jnp.concatenate(
            [dnum, jnp.where(lane == 0, dden, 0.0)], axis=1
        ).astype(BF)
        states.append(
            dot_tn(edge_left(dnum, dden, first, last, h), phi_ref[:, h * feats : (h + 1) * feats])
        )
    put_edges(edge_ref, states, heads, hd, info_ref[PLANE])


def feature_back(dphi, phi, vectors, om, heads, hd, feats, scale):
    lows, sums = [], []
    for h in range(heads):
        grad_raw = dphi[h] * phi[:, h * feats : (h + 1) * feats].astype(F32)
        lows.append((scale * grad_raw).astype(BF))
        total = jnp.sum(grad_raw, axis=-1, keepdims=True)
        sums.append(total * vectors[:, h * hd : (h + 1) * hd].astype(F32))
    through = dot_nt(jnp.concatenate(lows, axis=1), om)
    return through - scale * scale * jnp.concatenate(sums, axis=1)


def put_slices(source_ref, base, sent_ref, kept_ref, core):
    step = source_ref.shape[0] // PLANE
    for i in range(PLANE // 2):
        other = pl.multiple_of((2 * i + 1 - core) * step, 16)
        own = pl.multiple_of((2 * i + core) * step, 16)
        sent_ref[i, base : base + step, :] = source_ref[pl.ds(other, step), :]
        kept_ref[i, base : base + step, :] = source_ref[pl.ds(own, step), :]


def queries_back_kernel(
    heads, hd, feats, info_ref, dnd_ref, q_ref, phiq_ref, kv_ref, phik_ref, cf_ref, cl_ref, om_ref, same_ref,
    ends_ref, att_ref, x_ref, one_ref, dq_ref, dphik_ref, dv_ref, sent_ref, kept_ref, grad_ref,
):
    cols = heads * hd
    scale = hd ** (-0.25)
    first, last = ends_ref[:, 0:1], ends_ref[:, 1:2]
    same = same_ref[...]
    dphis, dvs = [], []
    for h in range(heads):
        phiq = phiq_ref[:, h * feats : (h + 1) * feats]
        phik = phik_ref[:, h * feats : (h + 1) * feats]
        value = with_one(kv_ref[:, cols + h * hd : cols + (h + 1) * hd])
        dnd = dnd_ref[:, 2 * h * hd : 2 * (h + 1) * hd]
        dscore = dot_nt(dnd, value).astype(BF) * same
        dscore_t = dot_nt(value, dnd).astype(BF) * same
        score_t = dot_nt(phik, phiq).astype(BF) * same
        wide = dnd.astype(F32)
        left = edge_left(wide[:, :hd], wide[:, hd : hd + 1], first, last, h)
        stack = stack_edges(cf_ref[...], cl_ref[...], h, hd, cols)
        dphis.append(dot(dscore, phik) + dot(left, stack))
        dphik_ref[:, h * feats : (h + 1) * feats] = dot(dscore_t, phiq)
        dvs.append(dot(score_t, dnd)[:, :hd])
    dv_ref[...] = jnp.concatenate(dvs, axis=1)
    dq = feature_back(dphis, phiq_ref[...], q_ref[...], om_ref[...], heads, hd, feats, scale)
    dq = dq.astype(BF)
    dq_ref[...] = dq
    grad_ref[:cols, :] = dot_tn(dq, x_ref[...]).astype(BF)
    grad_ref[cols:, :] = dot_tn(att_ref[...], one_ref[...]).astype(BF)
    put_slices(grad_ref, 0, sent_ref, kept_ref, info_ref[0] & 1)


def keys_back_kernel(
    heads, hd, feats, info_ref, match_ref, kv_ref, phik_ref, dphik_ref, dv_ref, came_ref, om_ref, ends_ref, x_ref,
    dkv_ref, sent_ref, kept_ref, grad_ref,
):
    cols = heads * hd
    scale = hd ** (-0.25)
    first, last = ends_ref[:, 0:1], ends_ref[:, 1:2]
    rf, rl = take_edges(came_ref, match_ref)
    dphis, dvs = [], []
    for h in range(heads):
        phik = phik_ref[:, h * feats : (h + 1) * feats]
        value = kv_ref[:, cols + h * hd : cols + (h + 1) * hd].astype(F32)
        stack = stack_edges(rf, rl, h, hd, cols)
        dphis.append(
            dphik_ref[:, h * feats : (h + 1) * feats] + dot(edge_left(value, 1.0, first, last, h), stack)
        )
        far = dot_nt(phik, stack[: 2 * hd])
        dvs.append(dv_ref[:, h * hd : (h + 1) * hd] + first * far[:, :hd] + last * far[:, hd:])
    dk = feature_back(dphis, phik_ref[...], kv_ref[:, :cols], om_ref[...], heads, hd, feats, scale)
    dkv = jnp.concatenate([dk] + dvs, axis=1).astype(BF)
    dkv_ref[...] = dkv
    grad_ref[...] = dot_tn(dkv, x_ref[...]).astype(BF)
    put_slices(grad_ref, 0, sent_ref, kept_ref, info_ref[0] & 1)


def tokens_kernel(cols, dq_ref, dkv_ref, qo_ref, kv_ref, one_ref, out_ref):
    back = dot(dq_ref[...], qo_ref[:cols, :]) + dot(dkv_ref[...], kv_ref[...])

    @pl.when(pl.program_id(0) == 0)
    def _():
        out_ref[...] = one_ref[...] + back

    @pl.when(pl.program_id(0) > 0)
    def _():
        out_ref[...] += back


def norm_of(hidden):
    average = jnp.mean(hidden, axis=-1, keepdims=True)
    centred = hidden - average
    inverse = lax.rsqrt(jnp.mean(centred * centred, axis=-1, keepdims=True) + EPSILON)
    return centred * inverse, inverse


def norm_back(grad_in, normed, inverse, gain):
    scaled = grad_in * gain
    centred = (
        scaled
        - jnp.mean(scaled, axis=-1, keepdims=True)
        - normed * jnp.mean(scaled * normed, axis=-1, keepdims=True)
    )
    return centred * inverse


def column_sums(arrays, rows):
    sums = [jnp.sum(a, axis=0, keepdims=True) for a in arrays]
    return jnp.concatenate(sums + [jnp.zeros((rows - len(sums), sums[0].shape[1]), F32)], axis=0)


def gelu_both(v):
    t = 1.0 / (1.0 + (0.3275911 * 0.5**0.5) * jnp.abs(v))
    tail = 1.061405429 * 0.5
    for c in (-1.453152027, 1.421413741, -0.284496736, 0.254829592):
        tail = tail * t + 0.5 * c
    bell = jnp.exp(-0.5 * v * v)
    tail = tail * t * bell
    gate = jnp.where(v < 0.0, tail, 1.0 - tail)
    return v * gate, gate + v * bell * (2.0 * jnp.pi) ** (-0.5)


def ffn_kernel(
    first_ref, up_ref, down_ref, bup_ref, normed_ref, cot_ref, vec_ref,
    act_ref, slope_ref, out_ref, two_ref, low_ref, sums_ref, acc_ref,
):
    g = pl.program_id(0)
    act, slope = gelu_both(dot(first_ref[...], up_ref[...]) + bup_ref[...])
    act = act.astype(BF)
    act_ref[...] = act
    slope_ref[...] = slope.astype(BF)
    branch = dot(act, down_ref[...])

    @pl.when(g == 0)
    def _():
        acc_ref[...] = normed_ref[...] * vec_ref[0:1, :] + vec_ref[1:2, :] + vec_ref[2:3, :] + branch

    @pl.when(g > 0)
    def _():
        acc_ref[...] += branch

    @pl.when(g == pl.num_programs(0) - 1)
    def _():
        normed, inverse = norm_of(acc_ref[...])
        gain = vec_ref[3:4, :]
        out_ref[...] = (normed * gain + vec_ref[4:5, :]).astype(BF)
        grad_in = cot_ref[...].astype(F32)
        two = norm_back(grad_in, normed, inverse, gain)
        two_ref[...] = two
        low_ref[...] = two.astype(BF)
        sums_ref[...] = column_sums([grad_in * normed, grad_in, two], 8)


def ffn_back_kernel(
    info_ref, low_ref, act_ref, slope_ref, up_ref, down_ref, first_ref, two_ref, normed_ref, inverse_ref, vec_ref,
    sent_ref, kept_ref, bup_ref, one_ref, onelow_ref, sums_ref, acc_ref, grad_ref,
):
    g = pl.program_id(0)
    core = info_ref[0] & 1
    step = up_ref.shape[0] // PLANE
    low = low_ref[...]
    dpre = dot_nt(low, down_ref[...]) * slope_ref[...].astype(F32)
    bup_ref[...] = jnp.sum(dpre, axis=0, keepdims=True)
    pre_low = dpre.astype(BF)
    grad_ref[...] = dot_tn(first_ref[...], pre_low).astype(BF)
    put_slices(grad_ref, 0, sent_ref, kept_ref, core)
    grad_ref[...] = dot_tn(act_ref[...], low).astype(BF)
    put_slices(grad_ref, step, sent_ref, kept_ref, core)
    through = dot_nt(pre_low, up_ref[...])

    @pl.when(g == 0)
    def _():
        acc_ref[...] = two_ref[...] + through

    @pl.when(g > 0)
    def _():
        acc_ref[...] += through

    @pl.when(g == pl.num_programs(0) - 1)
    def _():
        grad_in = acc_ref[...]
        normed = normed_ref[...]
        one = norm_back(grad_in, normed, inverse_ref[:, 0:1], vec_ref[0:1, :])
        one_ref[...] = one
        onelow_ref[...] = one.astype(BF)
        sums_ref[...] = column_sums([grad_in * normed, grad_in, one], 8)


def body(
    rows, heads,
    tokens, segment_ids, w_qkv, b_qkv, w_out, b_out, gain_one, bias_one, w_up, b_up, w_down, b_down,
    gain_two, bias_two, omega, cotangent,
):
    rank = lax.axis_index("rows")
    level = lax.axis_index("heads")
    hd, feats = omega.shape
    _, length, width = tokens.shape
    cols = w_qkv.shape[2]
    nh = cols // hd
    hidden = w_up.shape[1]
    slots = plane_slots(rank)
    me = slots[0]
    info = jnp.stack(slots + [level]).astype(jnp.int32)
    x = tokens[0]

    def slice_of(array):
        step = array.shape[0] // PLANE
        return lax.dynamic_slice_in_dim(array, me * step, step, 0)

    def gather_weights(*owns):
        piece = jnp.concatenate([slice_of(own) for own in owns], axis=0)
        near = [permute(piece, "heads", heads, lambda i, m=m: i ^ m) for m in range(1, heads)]
        return place_weights(owns, plane_gather(jnp.stack(near), rows), info)

    wt = jnp.transpose(w_qkv, (1, 2, 0)).reshape(3 * cols, width)
    own_qo = jnp.concatenate([wt[:cols], w_out], axis=0)
    (kv_w,) = gather_weights(wt[cols:])
    biases = jnp.concatenate([b_qkv.reshape(-1), b_up])
    biases = to_heads(jnp.broadcast_to(biases[None, None], (heads, 1, biases.size)))
    (qo_w,) = gather_weights(own_qo)
    up_w, down_w = gather_weights(w_up, w_down)
    bias_q = biases[:, :, :cols]
    bias_kv = biases[:, :, cols : 3 * cols]
    bias_up = biases[:, :, 3 * cols :]

    segments = lax.dynamic_slice_in_dim(segment_ids[0], level * length, length, 0)
    by_level = segment_ids[0].reshape(heads, length)
    firsts, lasts = by_level[:, 0], by_level[:, -1]
    my_first, my_last = segments[0], segments[-1]
    ends = jnp.stack([segments == my_first, segments == my_last], axis=1).astype(F32)
    same = (segments[:, None] == segments[None, :]).astype(BF)
    index = jnp.arange(heads)
    match = jnp.concatenate(
        [(index < level) & (lasts == my_first), (index > level) & (firsts == my_last)]
    ).astype(F32)

    eye = jnp.eye(nh, dtype=BF)
    om = (eye[:, None, :, None] * omega[None, :, None, :]).reshape(cols, nh * feats)
    edge = cols + 16
    dims = (nh, hd, feats)
    t = length
    aug = width + 128
    ones = jnp.ones((t, 1), BF)
    blank = jnp.zeros((t, 127), BF)
    x_aug = jnp.concatenate([x, ones, blank], axis=1)
    edge_spec = pl.BlockSpec((heads, None, edge, feats), lambda g: (0, g, 0, 0))
    half = PLANE // 2

    kv, phi_k, edges = call(
        functools.partial(keys_kernel, *dims),
        (heads,),
        [
            SMEM_SPEC, whole(t, width), part(2 * cols, width), part(1, 2 * cols), whole(cols, nh * feats),
            whole(t, 2),
        ],
        [part(t, 2 * cols), part(t, nh * feats), edge_spec],
        [
            struct((heads, t, 2 * cols), BF),
            struct((heads, t, nh * feats), BF),
            struct((heads, heads, edge, feats), BF),
        ],
        (info, x, kv_w, bias_kv, om, ends),
        us=12,
    )
    came = to_heads(edges)
    q, phi_q, near = call(
        functools.partial(queries_kernel, *dims),
        (heads,),
        [
            whole(t, width), part(2 * cols, width), part(1, cols), whole(cols, nh * feats), whole(t, t),
            part(t, 2 * cols), part(t, nh * feats),
        ],
        [part(t, cols), part(t, nh * feats), part(t, 2 * cols)],
        [
            struct((heads, t, cols), BF),
            struct((heads, t, nh * feats), BF),
            struct((heads, t, 2 * cols), F32),
        ],
        (x, qo_w, bias_q, om, same, kv, phi_k),
        us=12,
    )
    vec_one = jnp.stack([gain_one, bias_one])
    att, den, far_f, far_l, normed_one, inverse_one, first_low = call(
        functools.partial(attend_kernel, *dims),
        (heads,),
        [
            SMEM_SPEC, part(t, nh * feats), part(t, 2 * cols), edge_spec, whole(t, 2), part(2 * cols, width),
            whole(t, width), whole(1, width), whole(2, width),
        ],
        [
            part(t, cols), part(t, 128), part(edge, feats), part(edge, feats), whole(t, width), whole(t, 128),
            whole(t, width),
        ],
        [
            struct((heads, t, cols), BF),
            struct((heads, t, 128), F32),
            struct((heads, edge, feats), BF),
            struct((heads, edge, feats), BF),
            struct((t, width), F32),
            struct((t, 128), F32),
            struct((t, width), BF),
        ],
        (match, phi_q, near, came, ends, qo_w, x, b_out[None], vec_one),
        us=10,
        scratch=[pltpu.VMEM((t, width), F32)],
    )

    vec_two = jnp.stack([gain_one, bias_one, b_down, gain_two, bias_two])
    act, slope, layer_output, grad_two, two_low, sums_two = call(
        ffn_kernel,
        (heads,),
        [
            whole(t, width), part(width, hidden), part(hidden, width), part(1, hidden), whole(t, width),
            whole(t, width), whole(5, width),
        ],
        [part(t, hidden), part(t, hidden), whole(t, width), whole(t, width), whole(t, width), whole(8, width)],
        [
            struct((heads, t, hidden), BF),
            struct((heads, t, hidden), BF),
            struct((t, width), BF),
            struct((t, width), F32),
            struct((t, width), BF),
            struct((8, width), F32),
        ],
        (first_low, up_w, down_w, bias_up, normed_one, cotangent[0], vec_two),
        us=12,
        scratch=[pltpu.VMEM((t, width), F32)],
    )
    step = width // PLANE
    ffn_sent, ffn_kept, grad_b_up, grad_one, one_low, sums_one = call(
        ffn_back_kernel,
        (heads,),
        [
            SMEM_SPEC, whole(t, width), part(t, hidden), part(t, hidden), part(width, hidden), part(hidden, width),
            whole(t, width), whole(t, width), whole(t, width), whole(t, 128), whole(2, width),
        ],
        [
            part(half, 2 * step, width), part(half, 2 * step, width), part(1, hidden), whole(t, width),
            whole(t, width), whole(8, width),
        ],
        [
            struct((heads, half, 2 * step, width), BF),
            struct((heads, half, 2 * step, width), BF),
            struct((heads, 1, hidden), F32),
            struct((t, width), F32),
            struct((t, width), BF),
            struct((8, width), F32),
        ],
        (info, two_low, act, slope, up_w, down_w, first_low, grad_two, normed_one, inverse_one, vec_one),
        us=16,
        scratch=[pltpu.VMEM((t, width), F32), pltpu.VMEM((width, hidden), BF)],
    )
    ffn_pieces = reduce_grads(ffn_sent, ffn_kept, rank, rows)

    dnd, edges = call(
        functools.partial(attend_back_kernel, *dims),
        (heads,),
        [
            SMEM_SPEC, whole(t, width), part(2 * cols, width), part(t, cols), part(t, 128), part(t, nh * feats),
            whole(t, 2),
        ],
        [part(t, 2 * cols), edge_spec],
        [struct((heads, t, 2 * cols), BF), struct((heads, heads, edge, feats), BF)],
        (info, one_low, qo_w, att, den, phi_q, ends),
        us=13,
    )
    back = to_heads(edges)
    one_aug = jnp.concatenate([one_low, ones, blank], axis=1)
    slice_rows = 2 * cols // PLANE
    dq, dphi_k, dv, qo_sent, qo_kept = call(
        functools.partial(queries_back_kernel, *dims),
        (heads,),
        [
            SMEM_SPEC, part(t, 2 * cols), part(t, cols), part(t, nh * feats), part(t, 2 * cols),
            part(t, nh * feats), part(edge, feats), part(edge, feats), whole(cols, nh * feats), whole(t, t),
            whole(t, 2), part(t, cols), whole(t, aug), whole(t, aug),
        ],
        [
            part(t, cols), part(t, nh * feats), part(t, cols), part(half, slice_rows, aug),
            part(half, slice_rows, aug),
        ],
        [
            struct((heads, t, cols), BF),
            struct((heads, t, nh * feats), F32),
            struct((heads, t, cols), F32),
            struct((heads, half, slice_rows, aug), BF),
            struct((heads, half, slice_rows, aug), BF),
        ],
        (info, dnd, q, phi_q, kv, phi_k, far_f, far_l, om, same, ends, att, x_aug, one_aug),
        us=20,
        scratch=[pltpu.VMEM((2 * cols, aug), BF)],
    )
    qo_pieces = reduce_grads(qo_sent, qo_kept, rank, rows)
    dkv, kv_sent, kv_kept = call(
        functools.partial(keys_back_kernel, *dims),
        (heads,),
        [
            SMEM_SPEC, SMEM_SPEC, part(t, 2 * cols), part(t, nh * feats), part(t, nh * feats), part(t, cols),
            edge_spec, whole(cols, nh * feats), whole(t, 2), whole(t, aug),
        ],
        [part(t, 2 * cols), part(half, slice_rows, aug), part(half, slice_rows, aug)],
        [
            struct((heads, t, 2 * cols), BF),
            struct((heads, half, slice_rows, aug), BF),
            struct((heads, half, slice_rows, aug), BF),
        ],
        (info, match, kv, phi_k, dphi_k, dv, back, om, ends, x_aug),
        us=12,
        scratch=[pltpu.VMEM((2 * cols, aug), BF)],
    )
    kv_pieces = reduce_grads(kv_sent, kv_kept, rank, rows)
    grad_tokens = call(
        functools.partial(tokens_kernel, cols),
        (heads,),
        [part(t, cols), part(t, 2 * cols), part(2 * cols, width), part(2 * cols, width), whole(t, width)],
        whole(t, width),
        struct((t, width), F32),
        (dq, dkv, qo_w, kv_w, grad_one),
        us=5,
    )

    shared = jnp.concatenate([sums_one[:3], sums_two[:3]], axis=0).reshape(1, 6 * width)
    shared = jnp.broadcast_to(shared, (heads, 6 * width))
    vectors = jnp.concatenate([shared, grad_b_up[:, 0]], axis=1)
    vectors = lax.all_to_all(
        jnp.broadcast_to(vectors[None], (rows, *vectors.shape)), "rows", 0, 0, tiled=True
    )
    vectors = jnp.sum(vectors, axis=0)
    vectors = jnp.sum(to_heads(vectors[:, None, :]), axis=0)[0]
    outs = [vectors[n * width : (n + 1) * width] for n in range(6)]
    out_b_up = vectors[6 * width :]

    out_up, out_down = place_ffn(ffn_pieces, info)
    out_qkv, out_o, out_b = place_attention(qo_pieces, kv_pieces, info, cols, width)
    out_qkv = jnp.transpose(out_qkv.reshape(3, cols, width), (2, 0, 1))
    return (
        layer_output[None],
        grad_tokens[None],
        out_qkv,
        out_b[:, 0].reshape(3, cols),
        out_o,
        outs[2],
        outs[0],
        outs[1],
        out_up,
        out_b_up,
        out_down,
        outs[5],
        outs[3],
        outs[4],
    )


def solution(mesh):
    return jax.shard_map(
        functools.partial(body, mesh.shape["rows"], mesh.shape["heads"]),
        mesh=mesh,
        in_specs=(
            P("rows", "heads", None),
            P("rows", None),
            P(None, None, "heads"),
            P(None, "heads"),
            P("heads", None),
            P(),
            P(),
            P(),
            P(None, "heads"),
            P("heads"),
            P("heads", None),
            P(),
            P(),
            P(),
            P(),
            P("rows", "heads", None),
        ),
        out_specs=(
            P("rows", "heads", None),
            P("rows", "heads", None),
            P(None, None, "heads"),
            P(None, "heads"),
            P("heads", None),
            P(),
            P(),
            P(),
            P(None, "heads"),
            P("heads"),
            P("heads", None),
            P(),
            P(),
            P(),
        ),
        check_vma=False,
    )
```

```python
import functools

import jax
import jax.numpy as jnp
from jax import lax
from jax.experimental import pallas as pl
from jax.experimental.pallas import tpu as pltpu
from jax.sharding import PartitionSpec as P

EPSILON = 1e-05
PLANE = 8
VMEM_LIMIT = 48 * 1024 * 1024
BF = jnp.bfloat16
F32 = jnp.float32


def dot(a, b, dims=((1,), (0,))):
    return lax.dot_general(a, b, (dims, ((), ())), preferred_element_type=F32)


def dot_nt(a, b):
    return dot(a, b, ((1,), (1,)))


def dot_tn(a, b):
    return dot(a, b, ((0,), (0,)))


def estimate(us):
    return pl.CostEstimate(flops=int(us * 1e3), bytes_accessed=0, transcendentals=0)


def call_prefetch(kernel, grid, in_specs, out_specs, out_shape, args, us, scratch=()):
    return pl.pallas_call(
        kernel,
        grid_spec=pltpu.PrefetchScalarGridSpec(
            num_scalar_prefetch=1, grid=grid, in_specs=in_specs, out_specs=out_specs, scratch_shapes=list(scratch)
        ),
        out_shape=out_shape,
        compiler_params=pltpu.CompilerParams(vmem_limit_bytes=VMEM_LIMIT),
        cost_estimate=estimate(us),
    )(*args)


def call(kernel, grid, in_specs, out_specs, out_shape, args, us, scratch=(), aliases=None, limit=VMEM_LIMIT):
    return pl.pallas_call(
        kernel,
        grid=grid,
        input_output_aliases=aliases or {},
        in_specs=in_specs,
        out_specs=out_specs,
        out_shape=out_shape,
        scratch_shapes=list(scratch),
        compiler_params=pltpu.CompilerParams(vmem_limit_bytes=limit),
        cost_estimate=estimate(us),
    )(*args)


def whole(*shape):
    return pl.BlockSpec(shape, lambda g: (0,) * len(shape))


def part(*shape, base=0, flip=0):
    return pl.BlockSpec((None, *shape), lambda g: ((g + base) ^ flip,) + (0,) * len(shape))


def other(*shape):
    return pl.BlockSpec((None, *shape), lambda g: (jnp.maximum(g - 1, 0),) + (0,) * len(shape))


ANY_SPEC = pl.BlockSpec(memory_space=pl.ANY)


def struct(shape, dtype):
    return jax.ShapeDtypeStruct(shape, dtype)


def permute(array, axis, size, partner):
    return lax.ppermute(array, axis, [(i, partner(i)) for i in range(size)])


def first_partner(i):
    return i ^ (4 if i & 1 else 2)


def second_partner(i):
    return i ^ (2 if i & 1 else 4)


def core_partner(i):
    return i ^ 1


def after(array, *others):
    return lax.optimization_barrier((array, others))[0]


def gather_chips(piece, rows, *others):
    p1 = permute(piece, "rows", rows, first_partner)
    p2 = permute(piece, "rows", rows, second_partner)
    return [piece, p1, p2, permute(after(p1, *others), "rows", rows, second_partner)]


def gather_cores(own, rows):
    return own + [permute(p, "rows", rows, core_partner) for p in own]


def plane_gather(piece, rows):
    return gather_cores(gather_chips(piece, rows), rows)


def plane_slots(rank):
    me = rank & (PLANE - 1)
    core = rank & 1
    first = jnp.where(core == 1, 4, 2)
    second = jnp.where(core == 1, 2, 4)
    return [
        me,
        me ^ first,
        me ^ second,
        me ^ 6,
        me ^ 1,
        me ^ 1 ^ second,
        me ^ 1 ^ first,
        me ^ 7,
    ]


def to_levels(arrays):
    size = len(arrays) + 1
    return [permute(a, "heads", size, lambda i, m=m: i ^ m) for m, a in enumerate(arrays, 1)]


def sum_kernel(*refs):
    *ins, out = refs
    total = ins[0][...].astype(F32)
    for ref in ins[1:]:
        total = total + ref[...].astype(F32)
    out[...] = total.astype(BF)


def sums(*jobs):
    tail = jobs[0][0][0].shape[1:]
    zeros = (0,) * len(tail)
    counts = [len(job) for job in jobs]

    def kernel(*refs):
        base = 0
        for n, count in enumerate(counts):
            sum_kernel(*refs[base : base + count], refs[-1].at[n])
            base += count

    return call(
        kernel,
        (1,),
        [
            pl.BlockSpec((None, *tail), lambda g, slot=slot: (slot, *zeros)) for job in jobs for _, slot in job
        ],
        whole(len(jobs), *tail),
        struct((len(jobs), *tail), BF),
        [array for job in jobs for array, _ in job],
        us=2,
    )


class Reduction:
    def __init__(self, sent, kept, rows):
        self.rows = rows
        self.kept = kept
        self.came = [permute(a, "rows", rows, core_partner) for a in sent]

    def near(self, slot):
        if len(self.came) == 1:
            return [(self.kept, slot), (self.came[0], slot)]
        return [(self.kept, slot), (self.came[slot], 0)]

    def second(self, *others):
        self.came = after(self.came, *others)
        sent = [sums(self.near(2)), sums(self.near(3))]
        self.close, self.far = [permute(a, "rows", self.rows, second_partner) for a in sent]
        return sent

    def first(self, *others):
        sent = sums([*self.near(1), (after(self.far, *others), 0)])
        self.last = permute(sent, "rows", self.rows, first_partner)
        return sent

    def parts(self, *others):
        last = after(self.last, *others)
        mask = PLANE
        while mask < self.rows:
            total = sums([*self.near(0), (self.close, 0), (last, 0)])
            other = permute(total, "rows", self.rows, lambda i, m=mask: i ^ m)
            last = (last.astype(F32) + other.astype(F32)).astype(BF)
            mask *= 2
        return [self.kept, self.came[0], self.close, last]


def total_kernel(sets, stacked, info_ref, *refs):
    outs = refs[4 * sets :]
    groups = refs[0].shape[0]
    base = 0
    for n in range(sets):
        arrays = refs[4 * n : 4 * n + 4]
        rows = arrays[0].shape[1]
        for k in range(groups):
            total = arrays[0][k].astype(F32)
            for array in arrays[1:]:
                total = total + array[k].astype(F32)
            if stacked:
                outs[0][info_ref[PLANE] ^ k, base : base + rows, :] = total.astype(BF)
            else:
                outs[k][base : base + rows, :] = total.astype(BF)
        base += rows


def totals(sets, info, stacked):
    heads, rows, cols = sets[0][0].shape[1:]
    rows *= len(sets)
    spec = pl.BlockSpec((None, heads, rows // len(sets), cols), lambda g: (0, 0, 0, 0))
    shapes = [struct((heads, rows, cols), BF)] if stacked else [struct((rows, cols), BF)] * heads
    return call(
        functools.partial(total_kernel, len(sets), stacked),
        (1,),
        [SMEM_SPEC] + [spec] * (4 * len(sets)),
        [whole(*shape.shape) for shape in shapes],
        shapes,
        [info] + [array for arrays in sets for array in arrays],
        us=2,
    )


def others_first(array, info, split):
    heads, rows, cols = array.shape
    shapes = [(heads - 1, split, cols), (heads - 1, rows - split, cols)]

    def kernel(info_ref, in_ref, head_ref, tail_ref):
        for k in range(1, heads):
            place = info_ref[PLANE] ^ k
            head_ref[k - 1] = in_ref[place, :split, :]
            tail_ref[k - 1] = in_ref[place, split:, :]

    return call(
        kernel, (1,), [SMEM_SPEC, whole(*array.shape)], [whole(*shape) for shape in shapes],
        [struct(shape, array.dtype) for shape in shapes], (info, array), us=2,
    )


def to_heads(array):
    return lax.all_to_all(array, "heads", 0, 0, tiled=True)


def sum_levels(array):
    return sums([(array, n) for n in range(array.shape[0])])[0]


SMEM_SPEC = pl.BlockSpec(memory_space=pltpu.SMEM)
VMEM_SPEC = pl.BlockSpec(memory_space=pltpu.VMEM)


def bias_rows(vectors, width):
    rest = jnp.stack([jnp.pad(v, (0, width - v.size)) for v in vectors])
    rows = []
    for _ in range(3):
        rounded = lax.reduce_precision(rest, 8, 7)
        rows.append(rounded.astype(BF))
        rest = rest - rounded
    rows = jnp.concatenate(rows, axis=0)
    return jnp.pad(rows, ((0, 16 - rows.shape[0]), (0, 0)))


def place_weights_kernel(count, parts, info_ref, *refs):
    owns = refs[:parts]
    pieces = refs[parts : parts + count]
    outs = refs[parts + count :]
    mine = pl.program_id(0) == 0

    @pl.when(mine)
    def _():
        for own, out in zip(owns, outs):
            out[...] = own[...]

    @pl.when(jnp.logical_not(mine))
    def _():
        base = 0
        for out in outs:
            if out.shape[0] < PLANE * 16:
                out[...] = pieces[0][base : base + out.shape[0], :]
                continue
            step = out.shape[0] // PLANE
            for n in range(count):
                start = pl.multiple_of(info_ref[n] * step, 16)
                out[pl.ds(start, step), :] = pieces[n][base : base + step, :]
            base += step


def place_weights(owns, pieces, info):
    count, parts = len(pieces), len(owns)
    others, _, cols = pieces[0].shape
    rows = sum(own.shape[0] if own.shape[0] < PLANE * 16 else own.shape[0] // PLANE for own in owns)

    def piece_index(g, info_ref):
        return (jnp.maximum(g - 1, 0), 0, 0)

    return pl.pallas_call(
        functools.partial(place_weights_kernel, count, parts),
        grid_spec=pltpu.PrefetchScalarGridSpec(
            num_scalar_prefetch=1,
            grid=(others + 1,),
            in_specs=[pl.BlockSpec(own.shape, lambda g, s: (0, 0)) for own in owns]
            + [pl.BlockSpec((None, rows, cols), piece_index)] * count,
            out_specs=[pl.BlockSpec((None, *own.shape), lambda g, s: (g, 0, 0)) for own in owns],
        ),
        out_shape=[struct((others + 1, *own.shape), BF) for own in owns],
        compiler_params=pltpu.CompilerParams(vmem_limit_bytes=VMEM_LIMIT),
        cost_estimate=estimate(3 * parts),
    )(info, *owns, *pieces)


def place_ffn_kernel(count, info_ref, *refs):
    up, down, turned = refs[count:]
    step = refs[0].shape[0] // 2
    for n in range(count):
        start = pl.multiple_of(info_ref[n] * step, 16)
        turned[pl.ds(start, step), :] = refs[n][:step, :].astype(F32)
        down[pl.ds(start, step), :] = refs[n][step:, :].astype(F32)
    up[...] = jnp.transpose(turned[...])


def place_ffn(pieces, info):
    rows, cols = pieces[0].shape
    count = len(pieces)
    hidden = count * rows // 2
    return pl.pallas_call(
        functools.partial(place_ffn_kernel, count),
        in_specs=[SMEM_SPEC] + [VMEM_SPEC] * count,
        out_specs=[VMEM_SPEC] * 2,
        out_shape=[struct((cols, hidden), F32), struct((hidden, cols), F32)],
        scratch_shapes=[pltpu.VMEM((hidden, cols), F32)],
        compiler_params=pltpu.CompilerParams(vmem_limit_bytes=VMEM_LIMIT),
        cost_estimate=estimate(4),
    )(info, *pieces)


def place_attention_kernel(count, cols, width, info_ref, *refs):
    out_qkv, out_o, out_b, vectors, bias = refs[count:]
    step = refs[0].shape[0] // 2
    for n in range(count):
        start = pl.multiple_of(info_ref[n] * step, 16)
        wide = refs[n][:step, :].astype(F32)

        @pl.when(start < cols)
        def _():
            out_qkv[pl.ds(start, step), :] = wide[:, :width]
            bias[pl.ds(start, step), :] = wide[:, width:]

        @pl.when(start >= cols)
        def _():
            out_o[pl.ds(pl.multiple_of(start - cols, 16), step), :] = wide[:, :width]

        @pl.when(start == cols)
        def _():
            groups = width // 128
            for v in range(vectors.shape[0]):
                for j in range(groups):
                    row = v * groups + j
                    vectors[v : v + 1, j * 128 : (j + 1) * 128] = wide[row : row + 1, width:]

        wide = refs[n][step:, :].astype(F32)
        out_qkv[pl.ds(cols + start, step), :] = wide[:, :width]
        bias[pl.ds(cols + start, step), :] = wide[:, width:]
    row = jnp.transpose(bias[...])[0:1, :]
    for j in range(3):
        out_b[j : j + 1, :] = row[:, j * cols : (j + 1) * cols]


def place_attention(pieces, info, cols, width):
    count = len(pieces)
    return pl.pallas_call(
        functools.partial(place_attention_kernel, count, cols, width),
        in_specs=[SMEM_SPEC] + [VMEM_SPEC] * count,
        out_specs=[VMEM_SPEC] * 4,
        out_shape=[
            struct((3 * cols, width), F32),
            struct((cols, width), F32),
            struct((3, cols), F32),
            struct((7, width), F32),
        ],
        scratch_shapes=[pltpu.VMEM((3 * cols, 128), F32)],
        compiler_params=pltpu.CompilerParams(vmem_limit_bytes=VMEM_LIMIT),
        cost_estimate=estimate(3),
    )(info, *pieces)


def phi_of(raw, vectors, head, hd, feats, scale):
    wide = vectors[:, head * hd : (head + 1) * hd].astype(F32)
    half = 0.5 * scale * scale * jnp.sum(wide * wide, axis=-1, keepdims=True)
    part_raw = raw[:, head * feats : (head + 1) * feats]
    return jnp.exp(scale * part_raw - half) * feats ** (-0.5)


def edge_rows(first, last, head):
    lane = lax.broadcasted_iota(jnp.int32, (first.shape[0], 32), 1)
    return jnp.where(lane == head, first, 0.0) + jnp.where(lane == 16 + head, last, 0.0)


def edge_left(value, norm, first, last, head):
    return jnp.concatenate(
        [value * first, value * last, edge_rows(norm * first, norm * last, head)], axis=1
    ).astype(BF)


def edges_of(states, hd):
    norms = states[0][2 * hd :]
    for state in states[1:]:
        norms = norms + state[2 * hd :]
    firsts = jnp.concatenate([s[:hd] for s in states] + [norms[:16]], axis=0).astype(BF)
    lasts = jnp.concatenate([s[hd : 2 * hd] for s in states] + [norms[16:]], axis=0).astype(BF)
    return firsts, lasts


def put_edges(edge_ref, firsts, lasts, level, group):
    for m in range(1, edge_ref.shape[0]):
        place = level ^ m

        @pl.when(place > level)
        def _():
            edge_ref[place, group ^ m] = lasts

        @pl.when(place < level)
        def _():
            edge_ref[place, group ^ m] = firsts


def take_edges(came_ref, match_ref, level):
    left = right = None
    count = came_ref.shape[0] - 1
    for m in range(count):
        wide = came_ref[level ^ (m + 1)].astype(F32)
        a, b = wide * match_ref[m], wide * match_ref[count + m]
        left = a if left is None else left + a
        right = b if right is None else right + b
    return left.astype(BF), right.astype(BF)


def stack_edges(f, l, h, hd, cols):
    return jnp.concatenate(
        [f[h * hd : (h + 1) * hd], l[h * hd : (h + 1) * hd], f[cols:], l[cols:]], axis=0
    )


def with_one(value):
    lane = lax.broadcasted_iota(jnp.int32, value.shape, 1)
    return jnp.concatenate([value, jnp.where(lane == 0, 1.0, 0.0).astype(value.dtype)], axis=1)


def keys_kernel(heads, hd, feats, info_ref, x_ref, w_ref, b_ref, om_ref, ends_ref, *refs):
    *before, kv_ref, phi_ref, edge_ref = refs
    cols = heads * hd
    scale = hd ** (-0.25)
    kv = (dot_nt(x_ref[...], w_ref[...]) + b_ref[...]).astype(BF)
    kv_ref[...] = kv
    raw = dot(kv[:, :cols], om_ref[...])
    first, last = ends_ref[:, 0:1], ends_ref[:, 1:2]
    states = []
    for h in range(heads):
        phi = phi_of(raw, kv, h, hd, feats, scale).astype(BF)
        phi_ref[:, h * feats : (h + 1) * feats] = phi
        value = kv[:, cols + h * hd : cols + (h + 1) * hd].astype(F32)
        states.append(dot_tn(edge_left(value, 1.0, first, last, h), phi))
    firsts, lasts = edges_of(states, hd)
    if not before:
        edge_ref[0] = firsts
        edge_ref[1] = lasts
        return
    group = pl.program_id(0) + 1
    put_edges(edge_ref, firsts, lasts, info_ref[PLANE], group)

    @pl.when(group == 1)
    def _():
        put_edges(edge_ref, before[-1][0], before[-1][1], info_ref[PLANE], 0)


def queries_kernel(heads, hd, feats, x_ref, w_ref, b_ref, om_ref, same_ref, kv_ref, phik_ref, *refs):
    q_ref, phi_ref, nd_ref = refs[-3:]
    cols = heads * hd
    scale = hd ** (-0.25)
    q = (dot_nt(x_ref[...], w_ref[:cols, :]) + b_ref[...]).astype(BF)
    q_ref[...] = q
    raw = dot(q, om_ref[...])
    same = same_ref[...]
    for h in range(heads):
        phi = phi_of(raw, q, h, hd, feats, scale).astype(BF)
        phi_ref[:, h * feats : (h + 1) * feats] = phi
        scores = dot_nt(phi, phik_ref[:, h * feats : (h + 1) * feats]).astype(BF) * same
        value = kv_ref[:, cols + h * hd : cols + (h + 1) * hd]
        nd_ref[:, 2 * h * hd : 2 * (h + 1) * hd] = dot(scores, with_one(value))


def feature_back(dphi, phi, vectors, om, heads, hd, feats, scale):
    lows, sums = [], []
    for h in range(heads):
        grad_raw = dphi[h] * phi[:, h * feats : (h + 1) * feats].astype(F32)
        lows.append((scale * grad_raw).astype(BF))
        total = jnp.sum(grad_raw, axis=-1, keepdims=True)
        sums.append(total * vectors[:, h * hd : (h + 1) * hd].astype(F32))
    through = dot_nt(jnp.concatenate(lows, axis=1), om)
    return through - scale * scale * jnp.concatenate(sums, axis=1)


def put_slices(source_ref, base, sent_refs, kept_ref, info_ref, placed=True):
    step = source_ref.shape[0] // PLANE
    half = PLANE // 2
    for n in range(PLANE):
        if n < half:
            out = kept_ref.at[n]
        else:
            out = sent_refs[n - half] if len(sent_refs) > 1 else sent_refs[0].at[n - half]
        start = pl.multiple_of(jnp.where(placed, info_ref[n], n) * step, 16)
        out[base : base + step, :] = source_ref[pl.ds(start, step), :]


def near_back_kernel(heads, hd, feats, dnd_ref, phiq_ref, kv_ref, phik_ref, same_ref, dphik_ref, dv_ref):
    cols = heads * hd
    same = same_ref[...]
    dvs = []
    for h in range(heads):
        phiq = phiq_ref[:, h * feats : (h + 1) * feats]
        phik = phik_ref[:, h * feats : (h + 1) * feats]
        value = with_one(kv_ref[:, cols + h * hd : cols + (h + 1) * hd])
        dnd = dnd_ref[:, 2 * h * hd : 2 * (h + 1) * hd]
        dscore_t = dot_nt(value, dnd).astype(BF) * same
        score_t = dot_nt(phik, phiq).astype(BF) * same
        dphik_ref[:, h * feats : (h + 1) * feats] = dot(dscore_t, phiq).astype(BF)
        dvs.append(dot(score_t, dnd)[:, :hd])
    dv_ref[...] = jnp.concatenate(dvs, axis=1)


def queries_back_kernel(
    heads, hd, feats, info_ref, dnd_ref, q_ref, phiq_ref, kv_ref, phik_ref, cf_ref, cl_ref, om_ref, same_ref,
    ends_ref, att_ref, x_ref, one_ref, one_sums_ref, two_sums_ref, bup_ref, dq_ref, sent_ref, kept_ref, grad_ref,
):
    cols = heads * hd
    scale = hd ** (-0.25)
    first, last = ends_ref[:, 0:1], ends_ref[:, 1:2]
    same = same_ref[...]
    dphis = []
    for h in range(heads):
        phik = phik_ref[:, h * feats : (h + 1) * feats]
        value = with_one(kv_ref[:, cols + h * hd : cols + (h + 1) * hd])
        dnd = dnd_ref[:, 2 * h * hd : 2 * (h + 1) * hd]
        dscore = dot_nt(dnd, value).astype(BF) * same
        wide = dnd.astype(F32)
        left = edge_left(wide[:, :hd], wide[:, hd : hd + 1], first, last, h)
        stack = stack_edges(cf_ref[...], cl_ref[...], h, hd, cols)
        dphis.append(dot(dscore, phik) + dot(left, stack))
    dq = feature_back(dphis, phiq_ref[...], q_ref[...], om_ref[...], heads, hd, feats, scale)
    dq = dq.astype(BF)
    dq_ref[...] = dq
    grad_ref[:cols, :] = dot_tn(dq, x_ref[...]).astype(BF)
    width = one_ref.shape[1]
    vectors = [one_sums_ref[n : n + 1, :] for n in range(3)] + [two_sums_ref[n : n + 1, :] for n in range(3)]
    vectors = vectors + [bup_ref[...]]
    block = [v[:, n : n + 128] for v in vectors for n in range(0, width, 128)]
    step = grad_ref.shape[0] // PLANE
    block.append(jnp.zeros((step - len(block), 128), F32))
    block = jnp.concatenate(block, axis=0).astype(BF)
    grad_ref[cols:, :width] = dot_tn(att_ref[...], one_ref[...]).astype(BF)
    for n in range(cols, 2 * cols, step):
        grad_ref[n : n + step, width:] = block
    put_slices(grad_ref, 0, [sent_ref], kept_ref, info_ref)


def keys_back_kernel(
    heads, hd, feats, info_ref, match_ref, kv_ref, phik_ref, dphik_ref, dv_ref, came_ref, om_ref, ends_ref, x_ref, *refs
):
    dkv_ref, sent_ref, kept_ref, grad_ref = refs[-4:]
    cols = heads * hd
    scale = hd ** (-0.25)
    first, last = ends_ref[:, 0:1], ends_ref[:, 1:2]
    rf, rl = take_edges(came_ref, match_ref, info_ref[PLANE])
    dphis, dvs = [], []
    for h in range(heads):
        phik = phik_ref[:, h * feats : (h + 1) * feats]
        value = kv_ref[:, cols + h * hd : cols + (h + 1) * hd].astype(F32)
        stack = stack_edges(rf, rl, h, hd, cols)
        dphis.append(
            dphik_ref[:, h * feats : (h + 1) * feats].astype(F32) + dot(edge_left(value, 1.0, first, last, h), stack)
        )
        far = dot_nt(phik, stack[: 2 * hd])
        dvs.append(dv_ref[:, h * hd : (h + 1) * hd] + first * far[:, :hd] + last * far[:, hd:])
    dk = feature_back(dphis, phik_ref[...], kv_ref[:, :cols], om_ref[...], heads, hd, feats, scale)
    dkv = jnp.concatenate([dk] + dvs, axis=1).astype(BF)
    dkv_ref[...] = dkv
    grad_ref[...] = dot_tn(dkv, x_ref[...]).astype(BF)
    put_slices(grad_ref, 0, [sent_ref], kept_ref, info_ref)


def tokens_kernel(grad_ref, w_ref, before_ref, out_ref):
    back = dot(grad_ref[...], w_ref[...])

    @pl.when(pl.program_id(0) == 0)
    def _():
        out_ref[...] = before_ref[...] + back

    @pl.when(pl.program_id(0) > 0)
    def _():
        out_ref[...] += back


def norm_of(hidden):
    average = jnp.mean(hidden, axis=-1, keepdims=True)
    centred = hidden - average
    inverse = lax.rsqrt(jnp.mean(centred * centred, axis=-1, keepdims=True) + EPSILON)
    return centred * inverse, inverse


def norm_back(grad_in, normed, inverse, gain):
    scaled = grad_in * gain
    centred = (
        scaled
        - jnp.mean(scaled, axis=-1, keepdims=True)
        - normed * jnp.mean(scaled * normed, axis=-1, keepdims=True)
    )
    return centred * inverse


def column_sums(arrays, rows):
    sums = [jnp.sum(a, axis=0, keepdims=True) for a in arrays]
    return jnp.concatenate(sums + [jnp.zeros((rows - len(sums), sums[0].shape[1]), F32)], axis=0)


def gelu_both(v):
    gate = 0.5 + 0.5 * lax.erf(v * 0.5**0.5)
    bell = jnp.exp(-0.5 * v * v) * (2.0 * jnp.pi) ** (-0.5)
    return v * gate, gate + v * bell


def ffn_copies(own_up, own_down, pieces, up_ref, down_ref, sems, k):
    if k == 0:
        return [
            pltpu.make_async_copy(own_up, up_ref.at[0], sems.at[0, 0]),
            pltpu.make_async_copy(own_down, down_ref.at[0], sems.at[0, 1]),
        ]
    step = up_ref.shape[1] // PLANE
    base = pieces[0].shape[1] - 2 * step
    copies = []
    for n, piece in enumerate(pieces):
        for part_n, ref in enumerate((up_ref, down_ref)):
            copies.append(
                pltpu.make_async_copy(
                    piece.at[k - 1, pl.ds(base + part_n * step, step)],
                    ref.at[k, pl.ds(n * step, step)],
                    sems.at[k, 2 * n + part_n],
                )
            )
    return copies


def middle_kernel(heads, hd, feats, info_ref, match_ref, phi_ref, nd_ref, came_ref, ends_ref, wo_ref, x_ref, vec_ref, bup_ref, cot_ref, *refs):
    own_up, own_down, *pieces = refs[: 2 + PLANE]
    (
        att_ref, cf_ref, cl_ref, out_ref, gradb_ref, one_out, onelow_ref, sums1_ref, sums2_ref, dnd_ref, edge_ref,
        sent1_ref, sent2_ref, sent3_ref, sent4_ref, kept_ref,
        acc, first_low, normed_one, inverse_one, act_s, slope_s, two, two_low, att_s, den_s, up_s, down_s, grad_s, sems,
    ) = refs[2 + PLANE :]
    sent = [sent1_ref, sent2_ref, sent3_ref, sent4_ref]
    groups = att_s.shape[0]
    stage = pl.program_id(0) // groups
    g = pl.program_id(0) % groups
    cols = heads * hd
    t = acc.shape[0]
    level = info_ref[PLANE]
    final = g == groups - 1

    @pl.when(pl.program_id(0) == 0)
    def _():
        for k in range(groups):
            for copy in ffn_copies(own_up, own_down, pieces, up_s, down_s, sems, k):
                copy.start()

    def first_add(value, start):
        @pl.when(g == 0)
        def _():
            acc[...] = start() + value

        @pl.when(g > 0)
        def _():
            acc[...] += value

    @pl.when(stage == 0)
    def _():
        first, last = ends_ref[:, 0:1], ends_ref[:, 1:2]
        cf, cl = take_edges(came_ref, match_ref, level)
        cf_ref[...] = cf
        cl_ref[...] = cl
        lane = lax.broadcasted_iota(jnp.int32, (t, 128), 1)
        dens = jnp.zeros((t, 128), F32)
        outs = []
        for h in range(heads):
            far = dot_nt(phi_ref[:, h * feats : (h + 1) * feats], stack_edges(cf, cl, h, hd, cols))
            nd = nd_ref[:, 2 * h * hd : 2 * (h + 1) * hd]
            num = nd[:, :hd] + first * far[:, :hd] + last * far[:, hd : 2 * hd]
            den = (
                nd[:, hd : hd + 1]
                + first * far[:, 2 * hd + h : 2 * hd + h + 1]
                + last * far[:, 2 * hd + 16 + h : 2 * hd + 17 + h]
            )
            outs.append(num / den)
            dens = dens + jnp.where(lane == h, den, 0.0)
        att = jnp.concatenate(outs, axis=1).astype(BF)
        att_ref[...] = att
        att_s[g] = att
        den_s[g] = dens
        first_add(dot(att, wo_ref[...]), lambda: x_ref[...].astype(F32) + vec_ref[0:1, :])

        @pl.when(final)
        def _():
            normed, inverse = norm_of(acc[...])
            normed_one[...] = normed
            inverse_one[...] = jnp.broadcast_to(inverse, inverse_one.shape)
            first_low[...] = (normed * vec_ref[1:2, :] + vec_ref[2:3, :]).astype(BF)

    @pl.when(stage == 1)
    def _():
        for k in range(groups):

            @pl.when(g == k)
            def _():
                for copy in ffn_copies(own_up, own_down, pieces, up_s, down_s, sems, k):
                    copy.wait()

        act, slope = gelu_both(dot_nt(first_low[...], up_s[g]) + bup_ref[...])
        act = act.astype(BF)
        act_s[g] = act
        slope_s[g] = slope.astype(BF)
        first_add(
            dot(act, down_s[g]),
            lambda: normed_one[...] * vec_ref[1:2, :] + vec_ref[2:3, :] + vec_ref[3:4, :],
        )

        @pl.when(final)
        def _():
            normed, inverse = norm_of(acc[...])
            gain = vec_ref[4:5, :]
            out_ref[...] = (normed * gain + vec_ref[5:6, :]).astype(BF)
            grad_in = cot_ref[...].astype(F32)
            grad = norm_back(grad_in, normed, inverse, gain)
            two[...] = grad
            two_low[...] = grad.astype(BF)
            sums2_ref[...] = column_sums([grad_in * normed, grad_in, grad], 8)

    @pl.when(stage == 2)
    def _():
        step = up_s.shape[1] // PLANE
        low = two_low[...]
        dpre = dot_nt(low, down_s[g]) * slope_s[g].astype(F32)
        gradb_ref[...] = jnp.sum(dpre, axis=0, keepdims=True)
        pre_low = dpre.astype(BF)
        grad_s[...] = dot_tn(pre_low, first_low[...]).astype(BF)
        put_slices(grad_s, 0, sent, kept_ref, info_ref, g == 0)
        grad_s[...] = dot_tn(act_s[g], low).astype(BF)
        put_slices(grad_s, step, sent, kept_ref, info_ref, g == 0)
        first_add(dot(pre_low, up_s[g]), lambda: two[...])

        @pl.when(final)
        def _():
            grad_in = acc[...]
            normed = normed_one[...]
            one = norm_back(grad_in, normed, inverse_one[:, 0:1], vec_ref[1:2, :])
            one_out[...] = one
            onelow_ref[...] = one.astype(BF)
            sums1_ref[...] = column_sums([grad_in * normed, grad_in, one], 8)

    @pl.when(stage == 3)
    def _():
        first, last = ends_ref[:, 0:1], ends_ref[:, 1:2]
        datt = dot_nt(onelow_ref[...], wo_ref[...])
        lane = lax.broadcasted_iota(jnp.int32, (t, hd), 1)
        atts, dens = att_s[g], den_s[g]
        states = []
        for h in range(heads):
            inverse = 1.0 / dens[:, h : h + 1]
            part_datt = datt[:, h * hd : (h + 1) * hd]
            att = atts[:, h * hd : (h + 1) * hd].astype(F32)
            dnum = part_datt * inverse
            dden = -jnp.sum(part_datt * att, axis=-1, keepdims=True) * inverse
            dnd_ref[:, 2 * h * hd : 2 * (h + 1) * hd] = jnp.concatenate(
                [dnum, jnp.where(lane == 0, dden, 0.0)], axis=1
            ).astype(BF)
            states.append(
                dot_tn(edge_left(dnum, dden, first, last, h), phi_ref[:, h * feats : (h + 1) * feats])
            )
        firsts, lasts = edges_of(states, hd)
        put_edges(edge_ref, firsts, lasts, level, g)


def body(
    rows, heads,
    tokens, segment_ids, w_qkv, b_qkv, w_out, b_out, gain_one, bias_one, w_up, b_up, w_down, b_down,
    gain_two, bias_two, omega, cotangent,
):
    rank = lax.axis_index("rows")
    level = lax.axis_index("heads")
    hd, feats = omega.shape
    _, length, width = tokens.shape
    cols = w_qkv.shape[2]
    nh = cols // hd
    hidden = w_up.shape[1]
    slots = plane_slots(rank)
    me = slots[0]
    info = jnp.stack(slots + [level]).astype(jnp.int32)
    x = tokens[0]

    def slice_of(array):
        step = array.shape[0] // PLANE
        return lax.dynamic_slice_in_dim(array, me * step, step, 0)

    def from_levels(piece):
        return to_levels([piece] * (heads - 1))

    wt = jnp.transpose(w_qkv, (1, 2, 0)).reshape(3 * cols, width)
    own_kv = wt[cols:]
    own_bias = bias_rows([b_qkv.reshape(-1), b_up], width)
    own_qo = jnp.concatenate([wt[:cols], w_out], axis=0)
    own_up = w_up.T
    near = from_levels(jnp.concatenate([slice_of(own_kv), own_bias], axis=0))
    rest = jnp.concatenate([slice_of(own_qo), slice_of(own_up), slice_of(w_down)], axis=0)
    rest = jnp.broadcast_to(rest[None], (heads, *rest.shape))
    own_bias_qkv = b_qkv.reshape(1, -1)

    segments = lax.dynamic_slice_in_dim(segment_ids[0], level * length, length, 0)
    by_level = segment_ids[0].reshape(heads, length)
    firsts, lasts = by_level[:, 0], by_level[:, -1]
    my_first, my_last = segments[0], segments[-1]
    ends = jnp.stack([segments == my_first, segments == my_last], axis=1).astype(F32)
    same = (segments[:, None] == segments[None, :]).astype(BF)
    index = jnp.arange(1, heads) ^ level
    there = index[:, None] == jnp.arange(heads)[None, :]
    index_first = jnp.sum(jnp.where(there, firsts[None], 0), axis=1)
    index_last = jnp.sum(jnp.where(there, lasts[None], 0), axis=1)
    match = jnp.concatenate(
        [(index < level) & (index_last == my_first), (index > level) & (index_first == my_last)]
    ).astype(F32)

    eye = jnp.eye(nh, dtype=BF)
    om = (eye[:, None, :, None] * omega[None, :, None, :]).reshape(cols, nh * feats)
    edge = cols + 16
    dims = (nh, hd, feats)
    t = length
    aug = width + 128
    x_aug = jnp.concatenate([x, jnp.ones((t, 1), BF), jnp.zeros((t, 127), BF)], axis=1)

    half = PLANE // 2
    edge_shape = struct((heads, heads, edge, feats), BF)
    edge_spec = pl.BlockSpec((heads, None, edge, feats), lambda g: (0, g, 0, 0))

    def slot_spec(count, wide):
        return pl.BlockSpec((half, None, count, wide), lambda g: (0, g, 0, 0))

    def slot_shape(count, wide):
        return struct((half, heads, count, wide), BF)

    def of_groups(base, *shape):
        return part(*shape, base=base) if base else whole(*shape)

    def keys(base, count, weights, bias, *before):
        return call(
            functools.partial(keys_kernel, *dims),
            (count,),
            [
                SMEM_SPEC, whole(t, width), of_groups(base, 2 * cols, width), of_groups(base, 1, 2 * cols),
                whole(cols, nh * feats), whole(t, 2),
            ]
            + [ANY_SPEC, ANY_SPEC, whole(2, edge, feats)][: len(before)],
            [
                part(t, 2 * cols, base=base),
                part(t, nh * feats, base=base),
                whole(*edge_shape.shape) if base else whole(2, edge, feats),
            ],
            [
                struct((heads, t, 2 * cols), BF),
                struct((heads, t, nh * feats), BF),
                edge_shape if base else struct((2, edge, feats), BF),
            ],
            (info, x, weights, bias, om, ends, *before),
            us=3 * count,
            aliases={6: 0, 7: 1} if base else None,
        )

    def queries(base, count, weights, bias, kv, phi_k, *before):
        return call(
            functools.partial(queries_kernel, *dims),
            (count,),
            [
                whole(t, width), of_groups(base, 2 * cols, width), of_groups(base, 1, cols),
                whole(cols, nh * feats), whole(t, t),
                part(t, 2 * cols, base=base), part(t, nh * feats, base=base),
            ]
            + [ANY_SPEC] * len(before),
            [
                part(t, cols, base=base), part(t, nh * feats, base=base), part(t, 2 * cols, base=base),
            ],
            [
                struct((heads, t, cols), BF),
                struct((heads, t, nh * feats), BF),
                struct((heads, t, 2 * cols), F32),
            ],
            (x, weights, bias, om, same, kv, phi_k, *before),
            us=3 * count,
            aliases={7 + n: n for n in range(len(before))},
        )

    near_rest = to_heads(after(rest, near))
    near = jnp.stack(near)
    p1 = permute(near, "rows", rows, first_partner)
    p2 = permute(near, "rows", rows, second_partner)
    own_keys = keys(0, 1, after(own_kv, near), own_bias_qkv[:, cols:])
    p3 = permute(after(p1, own_keys), "rows", rows, second_partner)
    own_queries = queries(0, 1, after(own_qo, p1), own_bias_qkv[:, :cols], *own_keys[:2])
    pieces = gather_cores(after([near, p1, p2, p3], own_queries), rows)
    kv_w, bias = place_weights([own_kv, own_bias], pieces, info)
    bias = bias.astype(F32)
    bias = bias[:, 0:2] + (bias[:, 2:4] + bias[:, 4:6])
    bias_qkv = bias[:, 0:1, : 3 * cols]
    bias_q = bias_qkv[:, :, :cols]
    bias_kv = bias_qkv[:, :, cols:]
    at_slot = (jnp.stack(slots)[:, None] == jnp.arange(PLANE)[None, :])[None, :, :, None]
    by_slice = bias[1:, 1, :hidden].reshape(heads - 1, 1, PLANE, hidden // PLANE)
    by_slot = jnp.sum(jnp.where(at_slot, by_slice, 0.0), axis=2).reshape(heads - 1, 1, hidden)
    bias_up = jnp.concatenate([b_up[None, None], by_slot], axis=0)

    own_keys = after(own_keys, own_queries)
    kv, phi_k, edges = keys(1, heads - 1, kv_w, bias_kv, *own_keys)
    came = to_heads(edges)
    near_rest = after(near_rest, edges)
    near_qo, near_ffn = others_first(near_rest, info, 2 * cols // PLANE)
    chips_qo = gather_chips(near_qo, rows)
    (qo_w,) = place_weights([own_qo], gather_cores(chips_qo, rows), info)
    q, phi_q, local = queries(1, heads - 1, qo_w, bias_q, kv, phi_k, *own_queries)
    chips_ffn = gather_chips(after(near_ffn, chips_qo[1:3]), rows, phi_q)
    rest_w = gather_cores(after(chips_ffn, phi_q), rows)
    step = hidden // PLANE
    vec = jnp.pad(
        jnp.stack([b_out, gain_one, bias_one, b_down, gain_two, bias_two]), ((0, 2), (0, 0))
    )

    def staged(shape, *stages, at=0):
        def index(s):
            stage, g = s // heads, s % heads
            group = jnp.where(stage > stages[-1], heads - 1, 0)
            for n in stages:
                group = jnp.where(stage == n, g, group)
            if len(stages) == 2:
                between = (stage > stages[0]) & (stage < stages[1])
                group = jnp.where(between, heads - 1, group)
            return (group, at, 0)

        return pl.BlockSpec((None, *shape), lambda s: index(s))

    def staged_slots(shape, stage):
        spec = staged((1, 1), stage)
        return pl.BlockSpec((shape[0], None, *shape[1:]), lambda s: (0, spec.index_map(s)[0], 0, 0))

    tokens_bf, tokens_f32 = struct((t, width), BF), struct((t, width), F32)
    (
        att, far_f, far_l, layer_output, grad_b_up, grad_one, one_low, sums_one, sums_two, dnd, edges, *sent, kept,
    ) = call(
        functools.partial(middle_kernel, *dims),
        (4 * heads,),
        [
            SMEM_SPEC, SMEM_SPEC, staged((t, nh * feats), 0, 3), staged((t, 2 * cols), 0),
            staged_slots((heads, edge, feats), 0), whole(t, 2), staged((cols, width), 0, 3, at=1), whole(t, width),
            whole(8, width), staged((1, hidden), 1), whole(t, width), *[ANY_SPEC] * (2 + PLANE),
        ],
        [
            staged((t, cols), 0), staged((edge, feats), 0), staged((edge, feats), 0), whole(t, width),
            staged((1, hidden), 2), whole(t, width), whole(t, width), whole(8, width), whole(8, width),
            staged((t, 2 * cols), 3), whole(*edge_shape.shape), *[staged((2 * step, width), 2)] * half,
            staged_slots((half, 2 * step, width), 2),
        ],
        [
            struct((heads, t, cols), BF),
            struct((heads, edge, feats), BF),
            struct((heads, edge, feats), BF),
            tokens_bf,
            struct((heads, 1, hidden), F32),
            tokens_f32,
            tokens_bf,
            struct((8, width), F32),
            struct((8, width), F32),
            struct((heads, t, 2 * cols), BF),
            edge_shape,
            *[struct((heads, 2 * step, width), BF)] * half,
            slot_shape(2 * step, width),
        ],
        (
            info, match, phi_q, local, came, ends, qo_w, x, vec, bias_up, cotangent[0], own_up, w_down, *rest_w,
        ),
        us=50,
        scratch=[
            pltpu.VMEM((t, width), F32),
            pltpu.VMEM((t, width), BF),
            pltpu.VMEM((t, width), F32),
            pltpu.VMEM((t, 128), F32),
            pltpu.VMEM((heads, t, hidden), BF),
            pltpu.VMEM((heads, t, hidden), BF),
            pltpu.VMEM((t, width), F32),
            pltpu.VMEM((t, width), BF),
            pltpu.VMEM((heads, t, cols), BF),
            pltpu.VMEM((heads, t, 128), F32),
            pltpu.VMEM((heads, hidden, width), BF),
            pltpu.VMEM((heads, hidden, width), BF),
            pltpu.VMEM((hidden, width), BF),
            pltpu.SemaphoreType.DMA((heads, 2 * PLANE)),
        ],
        limit=60 * 1024 * 1024,
    )
    by_slot = grad_b_up[1:, 0].reshape(heads - 1, PLANE, 1, step)
    by_slice = jnp.sum(jnp.where(at_slot, by_slot, 0.0), axis=1).reshape(heads - 1, 1, hidden)
    grad_b_up = jnp.concatenate([grad_b_up[:1], by_slice], axis=0)

    back = to_heads(edges)
    ffn = Reduction([a[None] for a in sent], kept, rows)
    ffn_sent = ffn.second()
    slice_rows = 2 * cols // PLANE
    dq, *qo = call(
        functools.partial(queries_back_kernel, *dims),
        (heads,),
        [
            SMEM_SPEC, part(t, 2 * cols), part(t, cols), part(t, nh * feats), part(t, 2 * cols),
            part(t, nh * feats), part(edge, feats), part(edge, feats), whole(cols, nh * feats), whole(t, t),
            whole(t, 2), part(t, cols), whole(t, aug), whole(t, width), whole(8, width),
            whole(8, width), part(1, hidden),
        ],
        [
            part(t, cols), *[slot_spec(slice_rows, aug)] * 2,
        ],
        [
            struct((heads, t, cols), BF),
            *[slot_shape(slice_rows, aug)] * 2,
        ],
        (
            info, after(dnd, ffn_sent), q, phi_q, kv, phi_k, far_f, far_l, om, same, ends, att, x_aug, one_low,
            sums_one, sums_two, grad_b_up,
        ),
        us=20,
        scratch=[pltpu.VMEM((2 * cols, aug), BF)],
    )
    qo = Reduction(qo[:1], qo[1], rows)
    dphi_k, dv = call(
        functools.partial(near_back_kernel, *dims),
        (heads,),
        [part(t, 2 * cols), part(t, nh * feats), part(t, 2 * cols), part(t, nh * feats), whole(t, t)],
        [part(t, nh * feats), part(t, cols)],
        [struct((heads, t, nh * feats), BF), struct((heads, t, cols), F32)],
        (after(dnd, dq), phi_q, kv, phi_k, same),
        us=10,
    )
    qo.second(dv)
    ffn.first(dv)
    back = after(back, dv)

    def keys_back(base, *before):
        slots = pl.BlockSpec((half, None, slice_rows, aug), lambda g: (0, g + base, 0, 0))
        edges = pl.BlockSpec((heads, None, edge, feats), lambda g: (0, g + base, 0, 0))
        return call(
            functools.partial(keys_back_kernel, *dims),
            (heads // 2,),
            [
                SMEM_SPEC, SMEM_SPEC, part(t, 2 * cols, base=base), part(t, nh * feats, base=base),
                part(t, nh * feats, base=base), part(t, cols, base=base), edges, whole(cols, nh * feats),
                whole(t, 2), whole(t, aug),
            ]
            + [ANY_SPEC] * len(before),
            [part(t, 2 * cols, base=base), slots, slots],
            [struct((heads, t, 2 * cols), BF), *[slot_shape(slice_rows, aug)] * 2],
            (info, match, kv, phi_k, dphi_k, dv, back, om, ends, x_aug, *before),
            us=6,
            scratch=[pltpu.VMEM((2 * cols, aug), BF)],
            aliases={10 + n: n for n in range(len(before))},
        )

    before = keys_back(0)
    grad_tokens = call(
        tokens_kernel,
        (heads,),
        [part(t, cols), staged((cols, width), 0), whole(t, width)],
        whole(t, width),
        tokens_f32,
        (dq, qo_w, after(grad_one, before)),
        us=3,
    )
    (ffn_total,) = totals([ffn.parts(grad_tokens)], info, True)
    before = after(before, ffn_total, qo.close, qo.far)
    dkv, *kv_red = keys_back(heads // 2, *before)
    kv_red = Reduction(kv_red[:1], kv_red[1], rows)
    qo_sent = qo.first(dkv)
    kv_sent = kv_red.second(qo_sent)
    grad_tokens = call(
        tokens_kernel,
        (heads,),
        [part(t, 2 * cols), part(2 * cols, width), whole(t, width)],
        whole(t, width),
        tokens_f32,
        (after(dkv, kv_sent), kv_w, grad_tokens),
        us=3,
    )
    kv_sent = kv_red.first(grad_tokens)
    ffn_pieces = plane_gather(sum_levels(after(to_heads(ffn_total), kv_sent)), rows)
    (total,) = totals([qo.parts(), kv_red.parts()], info, True)
    pieces = plane_gather(sum_levels(to_heads(total)), rows)

    out_up, out_down = place_ffn(ffn_pieces, info)
    out_qkv, out_o, out_b, outs = place_attention(pieces, info, cols, width)
    out_qkv = jnp.transpose(out_qkv.reshape(3, cols, width), (2, 0, 1))
    return (
        layer_output[None],
        grad_tokens[None],
        out_qkv,
        out_b,
        out_o,
        outs[2],
        outs[0],
        outs[1],
        out_up,
        outs[6],
        out_down,
        outs[5],
        outs[3],
        outs[4],
    )


def solution(mesh):
    return jax.shard_map(
        functools.partial(body, mesh.shape["rows"], mesh.shape["heads"]),
        mesh=mesh,
        in_specs=(
            P("rows", "heads", None),
            P("rows", None),
            P(None, None, "heads"),
            P(None, "heads"),
            P("heads", None),
            P(),
            P(),
            P(),
            P(None, "heads"),
            P("heads"),
            P("heads", None),
            P(),
            P(),
            P(),
            P(),
            P("rows", "heads", None),
        ),
        out_specs=(
            P("rows", "heads", None),
            P("rows", "heads", None),
            P(None, None, "heads"),
            P(None, "heads"),
            P("heads", None),
            P(),
            P(),
            P(),
            P(None, "heads"),
            P("heads"),
            P("heads", None),
            P(),
            P(),
            P(),
        ),
        check_vma=False,
    )
```

```python
import functools

import jax
import jax.numpy as jnp
from jax import lax
from jax.experimental import pallas as pl
from jax.experimental.pallas import tpu as pltpu
from jax.sharding import PartitionSpec as P

EPSILON = 1e-05
PLANE = 8
VMEM_LIMIT = 48 * 1024 * 1024
BF = jnp.bfloat16
F32 = jnp.float32


def dot(a, b, dims=((1,), (0,))):
    return lax.dot_general(a, b, (dims, ((), ())), preferred_element_type=F32)


def dot_nt(a, b):
    return dot(a, b, ((1,), (1,)))


def dot_tn(a, b):
    return dot(a, b, ((0,), (0,)))


def estimate(us):
    return pl.CostEstimate(flops=int(us * 1e3), bytes_accessed=0, transcendentals=0)


def call_prefetch(kernel, grid, in_specs, out_specs, out_shape, args, us, scratch=()):
    return pl.pallas_call(
        kernel,
        grid_spec=pltpu.PrefetchScalarGridSpec(
            num_scalar_prefetch=1, grid=grid, in_specs=in_specs, out_specs=out_specs, scratch_shapes=list(scratch)
        ),
        out_shape=out_shape,
        compiler_params=pltpu.CompilerParams(vmem_limit_bytes=VMEM_LIMIT),
        cost_estimate=estimate(us),
    )(*args)


def call(kernel, grid, in_specs, out_specs, out_shape, args, us, scratch=(), aliases=None, limit=VMEM_LIMIT):
    return pl.pallas_call(
        kernel,
        grid=grid,
        input_output_aliases=aliases or {},
        in_specs=in_specs,
        out_specs=out_specs,
        out_shape=out_shape,
        scratch_shapes=list(scratch),
        compiler_params=pltpu.CompilerParams(vmem_limit_bytes=limit),
        cost_estimate=estimate(us),
    )(*args)


def whole(*shape):
    return pl.BlockSpec(shape, lambda g: (0,) * len(shape))


def part(*shape, base=0, flip=0):
    return pl.BlockSpec((None, *shape), lambda g: ((g + base) ^ flip,) + (0,) * len(shape))


def other(*shape):
    return pl.BlockSpec((None, *shape), lambda g: (jnp.maximum(g - 1, 0),) + (0,) * len(shape))


ANY_SPEC = pl.BlockSpec(memory_space=pl.ANY)


def struct(shape, dtype):
    return jax.ShapeDtypeStruct(shape, dtype)


def permute(array, axis, size, partner):
    return lax.ppermute(array, axis, [(i, partner(i)) for i in range(size)])


def first_partner(i):
    return i ^ (4 if i & 1 else 2)


def second_partner(i):
    return i ^ (2 if i & 1 else 4)


def core_partner(i):
    return i ^ 1


def after(array, *others):
    return lax.optimization_barrier((array, others))[0]


def gather_chips(piece, rows, *others):
    p1 = permute(piece, "rows", rows, first_partner)
    p2 = permute(piece, "rows", rows, second_partner)
    return [piece, p1, p2, permute(after(p1, *others), "rows", rows, second_partner)]


def gather_cores(own, rows):
    return own + [permute(p, "rows", rows, core_partner) for p in own]


def plane_gather(piece, rows):
    return gather_cores(gather_chips(piece, rows), rows)


def plane_slots(rank):
    me = rank & (PLANE - 1)
    core = rank & 1
    first = jnp.where(core == 1, 4, 2)
    second = jnp.where(core == 1, 2, 4)
    return [
        me,
        me ^ first,
        me ^ second,
        me ^ 6,
        me ^ 1,
        me ^ 1 ^ second,
        me ^ 1 ^ first,
        me ^ 7,
    ]


def to_levels(arrays):
    size = len(arrays) + 1
    return [permute(a, "heads", size, lambda i, m=m: i ^ m) for m, a in enumerate(arrays, 1)]


def sum_kernel(*refs):
    *ins, out = refs
    total = ins[0][...].astype(F32)
    for ref in ins[1:]:
        total = total + ref[...].astype(F32)
    out[...] = total.astype(BF)


def sums(*jobs):
    tail = jobs[0][0][0].shape[1:]
    zeros = (0,) * len(tail)
    counts = [len(job) for job in jobs]

    def kernel(*refs):
        base = 0
        for n, count in enumerate(counts):
            sum_kernel(*refs[base : base + count], refs[-1].at[n])
            base += count

    return call(
        kernel,
        (1,),
        [
            pl.BlockSpec((None, *tail), lambda g, slot=slot: (slot, *zeros)) for job in jobs for _, slot in job
        ],
        whole(len(jobs), *tail),
        struct((len(jobs), *tail), BF),
        [array for job in jobs for array, _ in job],
        us=2,
    )


class Reduction:
    def __init__(self, rows, together=True):
        self.rows = rows
        self.together = together
        self.kept, self.came = [], []

    def cores(self, sent, kept):
        self.kept.append(kept)
        self.came.append([permute(a, "rows", self.rows, core_partner) for a in sent])

    def near(self, n, slot):
        came = self.came[n]
        if len(came) == 1:
            return [(self.kept[n], slot), (came[0], slot)]
        return [(self.kept[n], slot), (came[slot], 0)]

    def second(self, *others):
        self.came = after(self.came, *others)
        jobs = [self.near(n, slot) for n in range(len(self.kept)) for slot in (2, 3)]
        sent = [sums(*jobs)] if self.together else [sums(job) for job in jobs]
        came = [permute(a, "rows", self.rows, second_partner) for a in sent]
        self.close = [(came[0], n) if self.together else (came[n], 0) for n in range(len(jobs))]
        return sent

    def first(self, *others):
        arrays = after([array for array, _ in self.close], *others)
        self.close = [(array, slot) for array, (_, slot) in zip(arrays, self.close)]
        sent = sums(*[[*self.near(n, 1), self.close[2 * n + 1]] for n in range(len(self.kept))])
        self.last = permute(sent, "rows", self.rows, first_partner)
        return sent

    def parts(self, *others):
        last = after(self.last, *others)
        mask = PLANE
        sets = range(len(self.kept))
        while mask < self.rows:
            total = sums(*[[*self.near(n, 0), self.close[2 * n], (last, n)] for n in sets])
            other = permute(total, "rows", self.rows, lambda i, m=mask: i ^ m)
            last = (last.astype(F32) + other.astype(F32)).astype(BF)
            mask *= 2
        return [[*self.near(n, 0), self.close[2 * n], (last, n)] for n in sets]


def total_kernel(sets, stacked, info_ref, *refs):
    outs = refs[4 * sets :]
    groups = refs[0].shape[0]
    base = 0
    for n in range(sets):
        arrays = refs[4 * n : 4 * n + 4]
        rows = arrays[0].shape[1]
        for k in range(groups):
            total = arrays[0][k].astype(F32)
            for array in arrays[1:]:
                total = total + array[k].astype(F32)
            if stacked:
                outs[0][info_ref[PLANE] ^ k, base : base + rows, :] = total.astype(BF)
            else:
                outs[k][base : base + rows, :] = total.astype(BF)
        base += rows


def totals(sets, info, stacked):
    heads, rows, cols = sets[0][0][0].shape[1:]
    specs = [
        pl.BlockSpec((None, heads, rows, cols), lambda g, slot=slot: (slot, 0, 0, 0))
        for pairs in sets
        for _, slot in pairs
    ]
    rows *= len(sets)
    shapes = [struct((heads, rows, cols), BF)] if stacked else [struct((rows, cols), BF)] * heads
    return call(
        functools.partial(total_kernel, len(sets), stacked),
        (1,),
        [SMEM_SPEC] + specs,
        [whole(*shape.shape) for shape in shapes],
        shapes,
        [info] + [array for pairs in sets for array, _ in pairs],
        us=2,
    )


def others_first(array, info):
    heads, *tail = array.shape

    def kernel(info_ref, in_ref, out_ref):
        for k in range(1, heads):
            out_ref[k - 1] = in_ref[info_ref[PLANE] ^ k]

    return call(
        kernel, (1,), [SMEM_SPEC, whole(heads, *tail)], whole(heads - 1, *tail),
        struct((heads - 1, *tail), array.dtype), (info, array), us=2,
    )


def to_heads(array):
    return lax.all_to_all(array, "heads", 0, 0, tiled=True)


def sum_arrays(arrays):
    return sums([(array[None], 0) for array in arrays])[0]


def sum_levels(array):
    return sums([(array, n) for n in range(array.shape[0])])[0]


SMEM_SPEC = pl.BlockSpec(memory_space=pltpu.SMEM)
VMEM_SPEC = pl.BlockSpec(memory_space=pltpu.VMEM)


def bias_rows(vectors, width):
    rest = jnp.stack([jnp.pad(v, (0, width - v.size)) for v in vectors])
    rows = []
    for _ in range(3):
        rounded = lax.reduce_precision(rest, 8, 7)
        rows.append(rounded.astype(BF))
        rest = rest - rounded
    rows = jnp.concatenate(rows, axis=0)
    return jnp.pad(rows, ((0, 16 - rows.shape[0]), (0, 0)))


def place_weights_kernel(count, parts, info_ref, *refs):
    owns = refs[:parts]
    pieces = refs[parts : parts + count]
    outs = refs[parts + count :]
    mine = pl.program_id(0) == 0

    @pl.when(mine)
    def _():
        for own, out in zip(owns, outs):
            out[...] = own[...]

    @pl.when(jnp.logical_not(mine))
    def _():
        base = 0
        for out in outs:
            if out.shape[0] < PLANE * 16:
                out[...] = pieces[0][base : base + out.shape[0], :]
                continue
            step = out.shape[0] // PLANE
            for n in range(count):
                start = pl.multiple_of(info_ref[n] * step, 16)
                out[pl.ds(start, step), :] = pieces[n][base : base + step, :]
            base += step


def place_weights(owns, pieces, info):
    count, parts = len(pieces), len(owns)
    others, _, cols = pieces[0].shape
    rows = sum(own.shape[0] if own.shape[0] < PLANE * 16 else own.shape[0] // PLANE for own in owns)

    def piece_index(g, info_ref):
        return (jnp.maximum(g - 1, 0), 0, 0)

    return pl.pallas_call(
        functools.partial(place_weights_kernel, count, parts),
        grid_spec=pltpu.PrefetchScalarGridSpec(
            num_scalar_prefetch=1,
            grid=(others + 1,),
            in_specs=[pl.BlockSpec(own.shape, lambda g, s: (0, 0)) for own in owns]
            + [pl.BlockSpec((None, rows, cols), piece_index)] * count,
            out_specs=[pl.BlockSpec((None, *own.shape), lambda g, s: (g, 0, 0)) for own in owns],
        ),
        out_shape=[struct((others + 1, *own.shape), BF) for own in owns],
        compiler_params=pltpu.CompilerParams(vmem_limit_bytes=VMEM_LIMIT),
        cost_estimate=estimate(3 * parts),
    )(info, *owns, *pieces)


def place_ffn_kernel(count, info_ref, *refs):
    up, down, turned = refs[count:]
    step = refs[0].shape[0] // 2
    for n in range(count):
        start = pl.multiple_of(info_ref[n] * step, 16)
        turned[pl.ds(start, step), :] = refs[n][:step, :].astype(F32)
        down[pl.ds(start, step), :] = refs[n][step:, :].astype(F32)
    up[...] = jnp.transpose(turned[...])


def place_ffn(pieces, info):
    rows, cols = pieces[0].shape
    count = len(pieces)
    hidden = count * rows // 2
    return pl.pallas_call(
        functools.partial(place_ffn_kernel, count),
        in_specs=[SMEM_SPEC] + [VMEM_SPEC] * count,
        out_specs=[VMEM_SPEC] * 2,
        out_shape=[struct((cols, hidden), F32), struct((hidden, cols), F32)],
        scratch_shapes=[pltpu.VMEM((hidden, cols), F32)],
        compiler_params=pltpu.CompilerParams(vmem_limit_bytes=VMEM_LIMIT),
        cost_estimate=estimate(4),
    )(info, *pieces)


def place_attention_kernel(count, cols, width, info_ref, *refs):
    out_qkv, out_o, out_b, vectors, bias = refs[count:]
    step = refs[0].shape[0] // 2
    for n in range(count):
        start = pl.multiple_of(info_ref[n] * step, 16)
        wide = refs[n][:step, :].astype(F32)

        @pl.when(start < cols)
        def _():
            out_qkv[pl.ds(start, step), :] = wide[:, :width]
            bias[pl.ds(start, step), :] = wide[:, width:]

        @pl.when(start >= cols)
        def _():
            out_o[pl.ds(pl.multiple_of(start - cols, 16), step), :] = wide[:, :width]

        @pl.when(start == cols)
        def _():
            groups = width // 128
            for v in range(vectors.shape[0]):
                for j in range(groups):
                    row = v * groups + j
                    vectors[v : v + 1, j * 128 : (j + 1) * 128] = wide[row : row + 1, width:]

        wide = refs[n][step:, :].astype(F32)
        out_qkv[pl.ds(cols + start, step), :] = wide[:, :width]
        bias[pl.ds(cols + start, step), :] = wide[:, width:]
    row = jnp.transpose(bias[...])[0:1, :]
    for j in range(3):
        out_b[j : j + 1, :] = row[:, j * cols : (j + 1) * cols]


def place_attention(pieces, info, cols, width):
    count = len(pieces)
    return pl.pallas_call(
        functools.partial(place_attention_kernel, count, cols, width),
        in_specs=[SMEM_SPEC] + [VMEM_SPEC] * count,
        out_specs=[VMEM_SPEC] * 4,
        out_shape=[
            struct((3 * cols, width), F32),
            struct((cols, width), F32),
            struct((3, cols), F32),
            struct((7, width), F32),
        ],
        scratch_shapes=[pltpu.VMEM((3 * cols, 128), F32)],
        compiler_params=pltpu.CompilerParams(vmem_limit_bytes=VMEM_LIMIT),
        cost_estimate=estimate(3),
    )(info, *pieces)


def head_sums(values, heads, hd):
    row = lax.broadcasted_iota(jnp.int32, (heads * hd, 128), 0)
    lane = lax.broadcasted_iota(jnp.int32, (heads * hd, 128), 1)
    own = ((row >= lane * hd) & (row < (lane + 1) * hd)).astype(F32).astype(BF)
    high = values.astype(BF)
    low = (values - high.astype(F32)).astype(BF)
    return dot(high, own) + dot(low, own)


def phi_of(raw, halves, head, feats, scale):
    part_raw = raw[:, head * feats : (head + 1) * feats]
    return jnp.exp(scale * part_raw - halves[:, head : head + 1]) * feats ** (-0.5)


def half_norms(vectors, heads, hd, scale):
    wide = vectors.astype(F32)
    return 0.5 * scale * scale * head_sums(wide * wide, heads, hd)


def edge_rows(first, last, head):
    lane = lax.broadcasted_iota(jnp.int32, (first.shape[0], 32), 1)
    return jnp.where(lane == head, first, 0.0) + jnp.where(lane == 16 + head, last, 0.0)


def edge_left(value, norm, first, last, head):
    return jnp.concatenate(
        [value * first, value * last, edge_rows(norm * first, norm * last, head)], axis=1
    ).astype(BF)


def edge_states(values, norms, phi, heads, hd, feats):
    first_values, last_values = values
    cols = heads * hd
    left = jnp.concatenate([first_values, last_values, norms], axis=1).astype(BF)
    state = dot_tn(left, phi)
    row = lax.broadcasted_iota(jnp.int32, (16, feats), 0)
    out = []
    for n in range(2):
        base = 2 * cols + 16 * n
        rows = [state[n * cols + h * hd : n * cols + (h + 1) * hd, h * feats : (h + 1) * feats] for h in range(heads)]
        total = jnp.zeros((16, feats), F32)
        for h in range(heads):
            total = jnp.where(row == h, state[base : base + 16, h * feats : (h + 1) * feats], total)
        out.append(jnp.concatenate([*rows, total], axis=0).astype(BF))
    return out


def put_edges(edge_ref, firsts, lasts, level, group):
    for m in range(1, edge_ref.shape[0]):
        place = level ^ m

        @pl.when(place > level)
        def _():
            edge_ref[place, group ^ m] = lasts

        @pl.when(place < level)
        def _():
            edge_ref[place, group ^ m] = firsts


def take_edges(came_ref, match_ref, level):
    left = right = None
    count = came_ref.shape[0] - 1
    for m in range(count):
        wide = came_ref[level ^ (m + 1)].astype(F32)
        a, b = wide * match_ref[m], wide * match_ref[count + m]
        left = a if left is None else left + a
        right = b if right is None else right + b
    return left.astype(BF), right.astype(BF)


def stack_edges(f, l, h, hd, cols):
    return jnp.concatenate(
        [f[h * hd : (h + 1) * hd], l[h * hd : (h + 1) * hd], f[cols:], l[cols:]], axis=0
    )


def with_one(value):
    lane = lax.broadcasted_iota(jnp.int32, value.shape, 1)
    return jnp.concatenate([value, jnp.where(lane == 0, 1.0, 0.0).astype(value.dtype)], axis=1)


def keys_kernel(heads, hd, feats, info_ref, x_ref, w_ref, b_ref, om_ref, ends_ref, *refs):
    *before, kv_ref, phi_ref, edge_ref = refs
    cols = heads * hd
    scale = hd ** (-0.25)
    kv = (dot_nt(x_ref[...], w_ref[...]) + b_ref[...]).astype(BF)
    kv_ref[...] = kv
    raw = dot(kv[:, :cols], om_ref[...])
    first, last = ends_ref[:, 0:1], ends_ref[:, 1:2]
    halves = half_norms(kv[:, :cols], heads, hd, scale)
    for h in range(heads):
        phi_ref[:, h * feats : (h + 1) * feats] = phi_of(raw, halves, h, feats, scale).astype(BF)
    values = kv[:, cols:].astype(F32)
    lane = lax.broadcasted_iota(jnp.int32, (kv.shape[0], 32), 1)
    firsts, lasts = edge_states(
        (values * first, values * last), jnp.where(lane < 16, first, last), phi_ref[...], heads, hd, feats
    )
    if not before:
        edge_ref[0] = firsts
        edge_ref[1] = lasts
        return
    group = pl.program_id(0) + 1
    put_edges(edge_ref, firsts, lasts, info_ref[PLANE], group)

    @pl.when(group == 1)
    def _():
        put_edges(edge_ref, before[-1][0], before[-1][1], info_ref[PLANE], 0)


def queries_kernel(heads, hd, feats, x_ref, w_ref, b_ref, om_ref, same_ref, kv_ref, phik_ref, *refs):
    q_ref, phi_ref, nd_ref = refs[-3:]
    cols = heads * hd
    scale = hd ** (-0.25)
    q = (dot_nt(x_ref[...], w_ref[:cols, :]) + b_ref[...]).astype(BF)
    q_ref[...] = q
    raw = dot(q, om_ref[...])
    same = same_ref[...]
    halves = half_norms(q, heads, hd, scale)
    for h in range(heads):
        phi = phi_of(raw, halves, h, feats, scale).astype(BF)
        phi_ref[:, h * feats : (h + 1) * feats] = phi
        scores = dot_nt(phi, phik_ref[:, h * feats : (h + 1) * feats]).astype(BF) * same
        value = kv_ref[:, cols + h * hd : cols + (h + 1) * hd]
        nd_ref[:, 2 * h * hd : 2 * (h + 1) * hd] = dot(scores, with_one(value))


def feature_back(dphi, phi, vectors, om, heads, hd, feats, scale):
    cols = heads * hd
    lows = []
    for h in range(heads):
        grad_raw = dphi[h] * phi[:, h * feats : (h + 1) * feats].astype(F32)
        lows.append((scale * grad_raw).astype(BF))
    through = dot_nt(jnp.concatenate(lows, axis=1), om)
    wide = vectors.astype(F32)
    lane = lax.broadcasted_iota(jnp.int32, wide.shape, 1)
    total = through[:, cols : cols + 1]
    for h in range(1, heads):
        total = jnp.where(lane >= h * hd, through[:, cols + h : cols + h + 1], total)
    return through[:, :cols] - scale * total * wide


def weight_grad(grad_ref, rows, left, right):
    width = right.shape[1]
    lane = lax.broadcasted_iota(jnp.int32, (left.shape[0], 128), 1)
    grad_ref[rows, :width] = dot_tn(left, right).astype(BF)
    grad_ref[rows, width:] = dot_tn(left, jnp.where(lane == 0, 1.0, 0.0).astype(BF)).astype(BF)


def put_slices(source_ref, base, sent_refs, kept_ref, info_ref, placed=True):
    step = source_ref.shape[0] // PLANE
    half = PLANE // 2
    for n in range(PLANE):
        if n < half:
            out = kept_ref.at[n]
        else:
            out = sent_refs[n - half] if len(sent_refs) > 1 else sent_refs[0].at[n - half]
        start = pl.multiple_of(jnp.where(placed, info_ref[n], n) * step, 16)
        out[base : base + step, :] = source_ref[pl.ds(start, step), :]


def queries_back_kernel(
    heads, hd, feats, info_ref, dnd_ref, q_ref, phiq_ref, kv_ref, phik_ref, cf_ref, cl_ref, om_ref, same_ref,
    ends_ref, att_ref, x_ref, one_ref, one_sums_ref, two_sums_ref, bup_ref, dq_ref, dphik_ref, dv_ref, sent_ref, kept_ref,
    grad_ref,
):
    cols = heads * hd
    scale = hd ** (-0.25)
    first, last = ends_ref[:, 0:1], ends_ref[:, 1:2]
    same = same_ref[...]
    dphis, dvs = [], []
    for h in range(heads):
        phiq = phiq_ref[:, h * feats : (h + 1) * feats]
        phik = phik_ref[:, h * feats : (h + 1) * feats]
        value = with_one(kv_ref[:, cols + h * hd : cols + (h + 1) * hd])
        dnd = dnd_ref[:, 2 * h * hd : 2 * (h + 1) * hd]
        dscore = dot_nt(dnd, value).astype(BF) * same
        wide = dnd.astype(F32)
        left = edge_left(wide[:, :hd], wide[:, hd : hd + 1], first, last, h)
        stack = stack_edges(cf_ref[...], cl_ref[...], h, hd, cols)
        dphis.append(dot(dscore, phik) + dot(left, stack))
        dscore_t = dot_nt(value, dnd).astype(BF) * same
        score_t = dot_nt(phik, phiq).astype(BF) * same
        dphik_ref[:, h * feats : (h + 1) * feats] = dot(dscore_t, phiq).astype(BF)
        dvs.append(dot(score_t, dnd)[:, :hd])
    dv_ref[...] = jnp.concatenate(dvs, axis=1)
    dq = feature_back(dphis, phiq_ref[...], q_ref[...], om_ref[...], heads, hd, feats, scale)
    dq = dq.astype(BF)
    dq_ref[...] = dq
    weight_grad(grad_ref, slice(0, cols), dq, x_ref[...])
    width = one_ref.shape[1]
    vectors = [one_sums_ref[n : n + 1, :] for n in range(3)] + [two_sums_ref[n : n + 1, :] for n in range(3)]
    vectors = vectors + [bup_ref[...]]
    block = [v[:, n : n + 128] for v in vectors for n in range(0, width, 128)]
    step = grad_ref.shape[0] // PLANE
    block.append(jnp.zeros((step - len(block), 128), F32))
    block = jnp.concatenate(block, axis=0).astype(BF)
    grad_ref[cols:, :width] = dot_tn(att_ref[...], one_ref[...]).astype(BF)
    for n in range(cols, 2 * cols, step):
        grad_ref[n : n + step, width:] = block
    put_slices(grad_ref, 0, [sent_ref], kept_ref, info_ref)


def keys_back_kernel(
    heads, hd, feats, info_ref, match_ref, kv_ref, phik_ref, dphik_ref, dv_ref, came_ref, om_ref, ends_ref, x_ref, *refs
):
    dkv_ref, *sent, kept_ref, grad_ref = refs
    cols = heads * hd
    scale = hd ** (-0.25)
    first, last = ends_ref[:, 0:1], ends_ref[:, 1:2]
    rf, rl = take_edges(came_ref, match_ref, info_ref[PLANE])
    dphis, dvs = [], []
    for h in range(heads):
        phik = phik_ref[:, h * feats : (h + 1) * feats]
        value = kv_ref[:, cols + h * hd : cols + (h + 1) * hd].astype(F32)
        stack = stack_edges(rf, rl, h, hd, cols)
        dphis.append(
            dphik_ref[:, h * feats : (h + 1) * feats].astype(F32) + dot(edge_left(value, 1.0, first, last, h), stack)
        )
        far = dot_nt(phik, stack[: 2 * hd])
        dvs.append(dv_ref[:, h * hd : (h + 1) * hd] + first * far[:, :hd] + last * far[:, hd:])
    dk = feature_back(dphis, phik_ref[...], kv_ref[:, :cols], om_ref[...], heads, hd, feats, scale)
    dkv = jnp.concatenate([dk] + dvs, axis=1).astype(BF)
    dkv_ref[...] = dkv
    weight_grad(grad_ref, slice(0, 2 * cols), dkv, x_ref[...])
    put_slices(grad_ref, 0, sent, kept_ref, info_ref)


def tokens_kernel(cols, dq_ref, dkv_ref, qo_ref, kv_ref, one_ref, out_ref):
    back = dot(dq_ref[...], qo_ref[:cols, :]) + dot(dkv_ref[...], kv_ref[...])

    @pl.when(pl.program_id(0) == 0)
    def _():
        out_ref[...] = one_ref[...] + back

    @pl.when(pl.program_id(0) > 0)
    def _():
        out_ref[...] += back


def norm_of(hidden):
    average = jnp.mean(hidden, axis=-1, keepdims=True)
    centred = hidden - average
    inverse = lax.rsqrt(jnp.mean(centred * centred, axis=-1, keepdims=True) + EPSILON)
    return centred * inverse, inverse


def norm_back(grad_in, normed, inverse, gain):
    scaled = grad_in * gain
    centred = (
        scaled
        - jnp.mean(scaled, axis=-1, keepdims=True)
        - normed * jnp.mean(scaled * normed, axis=-1, keepdims=True)
    )
    return centred * inverse


def column_sums(arrays, rows):
    sums = [jnp.sum(a, axis=0, keepdims=True) for a in arrays]
    return jnp.concatenate(sums + [jnp.zeros((rows - len(sums), sums[0].shape[1]), F32)], axis=0)


def gelu_both(v):
    gate = 0.5 + 0.5 * lax.erf(v * 0.5**0.5)
    bell = jnp.exp(-0.5 * v * v) * (2.0 * jnp.pi) ** (-0.5)
    return v * gate, gate + v * bell


def ffn_copies(own_up, own_down, pieces, up_ref, down_ref, sems, k):
    if k == 0:
        return [
            pltpu.make_async_copy(own_up, up_ref.at[0], sems.at[0, 0]),
            pltpu.make_async_copy(own_down, down_ref.at[0], sems.at[0, 1]),
        ]
    step = up_ref.shape[1] // PLANE
    base = pieces[0].shape[1] - 2 * step
    copies = []
    for n, piece in enumerate(pieces):
        for part_n, ref in enumerate((up_ref, down_ref)):
            copies.append(
                pltpu.make_async_copy(
                    piece.at[k - 1, pl.ds(base + part_n * step, step)],
                    ref.at[k, pl.ds(n * step, step)],
                    sems.at[k, 2 * n + part_n],
                )
            )
    return copies


def middle_kernel(heads, hd, feats, info_ref, match_ref, phi_ref, nd_ref, came_ref, ends_ref, wo_ref, x_ref, vec_ref, bup_ref, cot_ref, *refs):
    own_up, own_down, *pieces = refs[: 2 + PLANE]
    (
        att_ref, cf_ref, cl_ref, out_ref, gradb_ref, one_out, onelow_ref, sums1_ref, sums2_ref, dnd_ref, edge_ref,
        sent1_ref, sent2_ref, sent3_ref, sent4_ref, kept_ref,
        acc, first_low, normed_one, inverse_one, act_s, slope_s, two, two_low, att_s, den_s, up_s, down_s, grad_s, sems,
    ) = refs[2 + PLANE :]
    sent = [sent1_ref, sent2_ref, sent3_ref, sent4_ref]
    groups = att_s.shape[0]
    stage = pl.program_id(0) // groups
    g = pl.program_id(0) % groups
    cols = heads * hd
    t = acc.shape[0]
    level = info_ref[PLANE]
    final = g == groups - 1

    @pl.when(pl.program_id(0) == 0)
    def _():
        for k in range(groups):
            for copy in ffn_copies(own_up, own_down, pieces, up_s, down_s, sems, k):
                copy.start()

    def first_add(value, start):
        @pl.when(g == 0)
        def _():
            acc[...] = start() + value

        @pl.when(g > 0)
        def _():
            acc[...] += value

    @pl.when(stage == 0)
    def _():
        first, last = ends_ref[:, 0:1], ends_ref[:, 1:2]
        cf, cl = take_edges(came_ref, match_ref, level)
        cf_ref[...] = cf
        cl_ref[...] = cl
        lane = lax.broadcasted_iota(jnp.int32, (t, 128), 1)
        dens = jnp.zeros((t, 128), F32)
        outs = []
        for h in range(heads):
            far = dot_nt(phi_ref[:, h * feats : (h + 1) * feats], stack_edges(cf, cl, h, hd, cols))
            nd = nd_ref[:, 2 * h * hd : 2 * (h + 1) * hd]
            num = nd[:, :hd] + first * far[:, :hd] + last * far[:, hd : 2 * hd]
            den = (
                nd[:, hd : hd + 1]
                + first * far[:, 2 * hd + h : 2 * hd + h + 1]
                + last * far[:, 2 * hd + 16 + h : 2 * hd + 17 + h]
            )
            outs.append(num / den)
            dens = dens + jnp.where(lane == h, den, 0.0)
        att = jnp.concatenate(outs, axis=1).astype(BF)
        att_ref[...] = att
        att_s[g] = att
        den_s[g] = dens
        first_add(dot(att, wo_ref[...]), lambda: x_ref[...].astype(F32) + vec_ref[0:1, :])

        @pl.when(final)
        def _():
            normed, inverse = norm_of(acc[...])
            normed_one[...] = normed
            inverse_one[...] = jnp.broadcast_to(inverse, inverse_one.shape)
            first_low[...] = (normed * vec_ref[1:2, :] + vec_ref[2:3, :]).astype(BF)

    @pl.when(stage == 1)
    def _():
        for k in range(groups):

            @pl.when(g == k)
            def _():
                for copy in ffn_copies(own_up, own_down, pieces, up_s, down_s, sems, k):
                    copy.wait()

        act, slope = gelu_both(dot_nt(first_low[...], up_s[g]) + bup_ref[...])
        act = act.astype(BF)
        act_s[g] = act
        slope_s[g] = slope.astype(BF)
        first_add(
            dot(act, down_s[g]),
            lambda: normed_one[...] * vec_ref[1:2, :] + vec_ref[2:3, :] + vec_ref[3:4, :],
        )

        @pl.when(final)
        def _():
            normed, inverse = norm_of(acc[...])
            gain = vec_ref[4:5, :]
            out_ref[...] = (normed * gain + vec_ref[5:6, :]).astype(BF)
            grad_in = cot_ref[...].astype(F32)
            grad = norm_back(grad_in, normed, inverse, gain)
            two[...] = grad
            two_low[...] = grad.astype(BF)
            sums2_ref[...] = column_sums([grad_in * normed, grad_in, grad], 8)

    @pl.when(stage == 2)
    def _():
        step = up_s.shape[1] // PLANE
        low = two_low[...]
        dpre = dot_nt(low, down_s[g]) * slope_s[g].astype(F32)
        gradb_ref[...] = jnp.sum(dpre, axis=0, keepdims=True)
        pre_low = dpre.astype(BF)
        grad_s[...] = dot_tn(pre_low, first_low[...]).astype(BF)
        put_slices(grad_s, 0, sent, kept_ref, info_ref, g == 0)
        grad_s[...] = dot_tn(act_s[g], low).astype(BF)
        put_slices(grad_s, step, sent, kept_ref, info_ref, g == 0)
        first_add(dot(pre_low, up_s[g]), lambda: two[...])

        @pl.when(final)
        def _():
            grad_in = acc[...]
            normed = normed_one[...]
            one = norm_back(grad_in, normed, inverse_one[:, 0:1], vec_ref[1:2, :])
            one_out[...] = one
            onelow_ref[...] = one.astype(BF)
            sums1_ref[...] = column_sums([grad_in * normed, grad_in, one], 8)

    @pl.when(stage == 3)
    def _():
        first, last = ends_ref[:, 0:1], ends_ref[:, 1:2]
        datt = dot_nt(onelow_ref[...], wo_ref[...])
        dens = den_s[g]
        lane = lax.broadcasted_iota(jnp.int32, (t, cols), 1)
        den = dens[:, 0:1]
        for h in range(1, heads):
            den = jnp.where(lane >= h * hd, dens[:, h : h + 1], den)
        dnum = datt / den
        dden = -head_sums(dnum * att_s[g].astype(F32), heads, hd)
        one_lane = lax.broadcasted_iota(jnp.int32, (t, hd), 1) == 0
        for h in range(heads):
            dnd_ref[:, 2 * h * hd : 2 * (h + 1) * hd] = jnp.concatenate(
                [dnum[:, h * hd : (h + 1) * hd], jnp.where(one_lane, dden[:, h : h + 1], 0.0)], axis=1
            ).astype(BF)
        norms = jnp.concatenate([dden[:, :16] * first, dden[:, :16] * last], axis=1)
        firsts, lasts = edge_states((dnum * first, dnum * last), norms, phi_ref[...], heads, hd, feats)
        put_edges(edge_ref, firsts, lasts, level, g)


def body(
    rows, heads,
    tokens, segment_ids, w_qkv, b_qkv, w_out, b_out, gain_one, bias_one, w_up, b_up, w_down, b_down,
    gain_two, bias_two, omega, cotangent,
):
    rank = lax.axis_index("rows")
    level = lax.axis_index("heads")
    hd, feats = omega.shape
    _, length, width = tokens.shape
    cols = w_qkv.shape[2]
    nh = cols // hd
    hidden = w_up.shape[1]
    slots = plane_slots(rank)
    me = slots[0]
    info = jnp.stack(slots + [level]).astype(jnp.int32)
    x = tokens[0]

    def slice_of(array):
        step = array.shape[0] // PLANE
        return lax.dynamic_slice_in_dim(array, me * step, step, 0)

    def from_levels(piece):
        return to_levels([piece] * (heads - 1))

    wt = jnp.transpose(w_qkv, (1, 2, 0)).reshape(3 * cols, width)
    own_kv = wt[cols:]
    own_bias = bias_rows([b_qkv.reshape(-1), b_up], width)
    own_qo = jnp.concatenate([wt[:cols], w_out], axis=0)
    own_up = w_up.T
    near = from_levels(jnp.concatenate([slice_of(own_kv), slice_of(own_qo), own_bias], axis=0))
    rest = jnp.concatenate([slice_of(own_up), slice_of(w_down)], axis=0)
    rest = jnp.broadcast_to(rest[None], (heads, *rest.shape))
    own_bias_qkv = b_qkv.reshape(1, -1)

    segments = lax.dynamic_slice_in_dim(segment_ids[0], level * length, length, 0)
    by_level = segment_ids[0].reshape(heads, length)
    firsts, lasts = by_level[:, 0], by_level[:, -1]
    my_first, my_last = segments[0], segments[-1]
    ends = jnp.stack([segments == my_first, segments == my_last], axis=1).astype(F32)
    same = (segments[:, None] == segments[None, :]).astype(BF)
    index = jnp.arange(1, heads) ^ level
    there = index[:, None] == jnp.arange(heads)[None, :]
    index_first = jnp.sum(jnp.where(there, firsts[None], 0), axis=1)
    index_last = jnp.sum(jnp.where(there, lasts[None], 0), axis=1)
    match = jnp.concatenate(
        [(index < level) & (index_last == my_first), (index > level) & (index_first == my_last)]
    ).astype(F32)

    eye = jnp.eye(nh, dtype=BF)
    om = (eye[:, None, :, None] * omega[None, :, None, :]).reshape(cols, nh * feats)
    om_back = jnp.concatenate(
        [om, jnp.repeat(eye, feats, axis=1), jnp.zeros((16 - nh, nh * feats), BF)], axis=0
    )
    edge = cols + 16
    dims = (nh, hd, feats)
    t = length
    aug = width + 128

    half = PLANE // 2
    edge_shape = struct((heads, heads, edge, feats), BF)
    edge_spec = pl.BlockSpec((heads, None, edge, feats), lambda g: (0, g, 0, 0))

    def slot_spec(count, wide):
        return pl.BlockSpec((half, None, count, wide), lambda g: (0, g, 0, 0))

    def slot_shape(count, wide):
        return struct((half, heads, count, wide), BF)

    def of_groups(base, *shape):
        return part(*shape, base=base) if base else whole(*shape)

    def keys(base, count, weights, bias, *before):
        return call(
            functools.partial(keys_kernel, *dims),
            (count,),
            [
                SMEM_SPEC, whole(t, width), of_groups(base, 2 * cols, width), of_groups(base, 1, 2 * cols),
                whole(cols, nh * feats), whole(t, 2),
            ]
            + [ANY_SPEC, ANY_SPEC, whole(2, edge, feats)][: len(before)],
            [
                part(t, 2 * cols, base=base),
                part(t, nh * feats, base=base),
                whole(*edge_shape.shape) if base else whole(2, edge, feats),
            ],
            [
                struct((heads, t, 2 * cols), BF),
                struct((heads, t, nh * feats), BF),
                edge_shape if base else struct((2, edge, feats), BF),
            ],
            (info, x, weights, bias, om, ends, *before),
            us=3 * count,
            aliases={6: 0, 7: 1} if base else None,
        )

    def queries(base, count, weights, bias, kv, phi_k, *before):
        return call(
            functools.partial(queries_kernel, *dims),
            (count,),
            [
                whole(t, width), of_groups(base, 2 * cols, width), of_groups(base, 1, cols),
                whole(cols, nh * feats), whole(t, t),
                part(t, 2 * cols, base=base), part(t, nh * feats, base=base),
            ]
            + [ANY_SPEC] * len(before),
            [
                part(t, cols, base=base), part(t, nh * feats, base=base), part(t, 2 * cols, base=base),
            ],
            [
                struct((heads, t, cols), BF),
                struct((heads, t, nh * feats), BF),
                struct((heads, t, 2 * cols), F32),
            ],
            (x, weights, bias, om, same, kv, phi_k, *before),
            us=3 * count,
            aliases={7 + n: n for n in range(len(before))},
        )

    near_rest = to_heads(after(rest, near))
    near = jnp.stack(near)
    p1 = permute(near, "rows", rows, first_partner)
    p2 = permute(near, "rows", rows, second_partner)
    own_keys = keys(0, 1, after(own_kv, near), own_bias_qkv[:, cols:])
    p3 = permute(after(p1, own_keys), "rows", rows, second_partner)
    own_queries = queries(0, 1, after(own_qo, p1), own_bias_qkv[:, :cols], *own_keys[:2])
    pieces = gather_cores(after([near, p1, p2, p3], own_queries), rows)
    kv_w, qo_w, bias = place_weights([own_kv, own_qo, own_bias], pieces, info)
    bias = bias.astype(F32)
    bias = bias[:, 0:2] + (bias[:, 2:4] + bias[:, 4:6])
    bias_qkv = bias[:, 0:1, : 3 * cols]
    bias_q = bias_qkv[:, :, :cols]
    bias_kv = bias_qkv[:, :, cols:]
    at_slot = (jnp.stack(slots)[:, None] == jnp.arange(PLANE)[None, :])[None, :, :, None]
    by_slice = bias[1:, 1, :hidden].reshape(heads - 1, 1, PLANE, hidden // PLANE)
    by_slot = jnp.sum(jnp.where(at_slot, by_slice, 0.0), axis=2).reshape(heads - 1, 1, hidden)
    bias_up = jnp.concatenate([b_up[None, None], by_slot], axis=0)

    own_keys = after(own_keys, own_queries)
    kv, phi_k, edges = keys(1, heads - 1, kv_w, bias_kv, *own_keys)
    came = to_heads(edges)
    q, phi_q, local = queries(1, heads - 1, qo_w, bias_q, kv, phi_k, *own_queries)
    chips_ffn = gather_chips(others_first(after(near_rest, edges), info), rows)
    rest_w = gather_cores(after(chips_ffn, phi_q), rows)
    step = hidden // PLANE
    vec = jnp.pad(
        jnp.stack([b_out, gain_one, bias_one, b_down, gain_two, bias_two]), ((0, 2), (0, 0))
    )

    def staged(shape, *stages, at=0):
        def index(s):
            stage, g = s // heads, s % heads
            group = jnp.where(stage > stages[-1], heads - 1, 0)
            for n in stages:
                group = jnp.where(stage == n, g, group)
            if len(stages) == 2:
                between = (stage > stages[0]) & (stage < stages[1])
                group = jnp.where(between, heads - 1, group)
            return (group, at, 0)

        return pl.BlockSpec((None, *shape), lambda s: index(s))

    def staged_slots(shape, stage):
        spec = staged((1, 1), stage)
        return pl.BlockSpec((shape[0], None, *shape[1:]), lambda s: (0, spec.index_map(s)[0], 0, 0))

    tokens_bf, tokens_f32 = struct((t, width), BF), struct((t, width), F32)
    (
        att, far_f, far_l, layer_output, grad_b_up, grad_one, one_low, sums_one, sums_two, dnd, edges, *sent, kept,
    ) = call(
        functools.partial(middle_kernel, *dims),
        (4 * heads,),
        [
            SMEM_SPEC, SMEM_SPEC, staged((t, nh * feats), 0, 3), staged((t, 2 * cols), 0),
            staged_slots((heads, edge, feats), 0), whole(t, 2), staged((cols, width), 0, 3, at=1), whole(t, width),
            whole(8, width), staged((1, hidden), 1), whole(t, width), *[ANY_SPEC] * (2 + PLANE),
        ],
        [
            staged((t, cols), 0), staged((edge, feats), 0), staged((edge, feats), 0), whole(t, width),
            staged((1, hidden), 2), whole(t, width), whole(t, width), whole(8, width), whole(8, width),
            staged((t, 2 * cols), 3), whole(*edge_shape.shape), *[staged((2 * step, width), 2)] * half,
            staged_slots((half, 2 * step, width), 2),
        ],
        [
            struct((heads, t, cols), BF),
            struct((heads, edge, feats), BF),
            struct((heads, edge, feats), BF),
            tokens_bf,
            struct((heads, 1, hidden), F32),
            tokens_f32,
            tokens_bf,
            struct((8, width), F32),
            struct((8, width), F32),
            struct((heads, t, 2 * cols), BF),
            edge_shape,
            *[struct((heads, 2 * step, width), BF)] * half,
            slot_shape(2 * step, width),
        ],
        (
            info, match, phi_q, local, came, ends, qo_w, x, vec, bias_up, cotangent[0], own_up, w_down, *rest_w,
        ),
        us=50,
        scratch=[
            pltpu.VMEM((t, width), F32),
            pltpu.VMEM((t, width), BF),
            pltpu.VMEM((t, width), F32),
            pltpu.VMEM((t, 128), F32),
            pltpu.VMEM((heads, t, hidden), BF),
            pltpu.VMEM((heads, t, hidden), BF),
            pltpu.VMEM((t, width), F32),
            pltpu.VMEM((t, width), BF),
            pltpu.VMEM((heads, t, cols), BF),
            pltpu.VMEM((heads, t, 128), F32),
            pltpu.VMEM((heads, hidden, width), BF),
            pltpu.VMEM((heads, hidden, width), BF),
            pltpu.VMEM((hidden, width), BF),
            pltpu.SemaphoreType.DMA((heads, 2 * PLANE)),
        ],
        limit=60 * 1024 * 1024,
    )
    by_slot = grad_b_up[1:, 0].reshape(heads - 1, PLANE, 1, step)
    by_slice = jnp.sum(jnp.where(at_slot, by_slot, 0.0), axis=1).reshape(heads - 1, 1, hidden)
    grad_b_up = jnp.concatenate([grad_b_up[:1], by_slice], axis=0)

    back = to_heads(edges)
    ffn = Reduction(rows, together=False)
    ffn.cores([a[None] for a in sent], kept)
    ffn_sent = ffn.second()
    slice_rows = 2 * cols // PLANE
    dq, dphi_k, dv, *qo = call(
        functools.partial(queries_back_kernel, *dims),
        (heads,),
        [
            SMEM_SPEC, part(t, 2 * cols), part(t, cols), part(t, nh * feats), part(t, 2 * cols),
            part(t, nh * feats), part(edge, feats), part(edge, feats), whole(cols + 16, nh * feats), whole(t, t),
            whole(t, 2), part(t, cols), whole(t, width), whole(t, width), whole(8, width),
            whole(8, width), part(1, hidden),
        ],
        [
            part(t, cols), part(t, nh * feats), part(t, cols), *[slot_spec(slice_rows, aug)] * 2,
        ],
        [
            struct((heads, t, cols), BF),
            struct((heads, t, nh * feats), BF),
            struct((heads, t, cols), F32),
            *[slot_shape(slice_rows, aug)] * 2,
        ],
        (
            info, after(dnd, ffn_sent), q, phi_q, kv, phi_k, far_f, far_l, om_back, same, ends, att, x, one_low,
            sums_one, sums_two, grad_b_up,
        ),
        us=20,
        scratch=[pltpu.VMEM((2 * cols, aug), BF)],
    )
    red = Reduction(rows)
    red.cores(qo[:1], qo[1])
    back = after(back, ffn.first(dv))
    dkv, *kv_red = call(
        functools.partial(keys_back_kernel, *dims),
        (heads,),
        [
            SMEM_SPEC, SMEM_SPEC, part(t, 2 * cols), part(t, nh * feats), part(t, nh * feats), part(t, cols),
            edge_spec, whole(cols + 16, nh * feats), whole(t, 2), whole(t, width),
        ],
        [part(t, 2 * cols), *[part(slice_rows, aug)] * half, slot_spec(slice_rows, aug)],
        [
            struct((heads, t, 2 * cols), BF),
            *[struct((heads, slice_rows, aug), BF)] * half,
            slot_shape(slice_rows, aug),
        ],
        (info, match, kv, phi_k, dphi_k, dv, back, om_back, ends, x),
        us=12,
        scratch=[pltpu.VMEM((2 * cols, aug), BF)],
    )
    red.cores([a[None] for a in kv_red[:half]], kv_red[half])
    sent = red.second(dkv, ffn.last)
    (ffn_total,) = totals(ffn.parts(sent), info, True)
    grad_tokens = call(
        functools.partial(tokens_kernel, cols),
        (heads,),
        [part(t, cols), part(t, 2 * cols), part(2 * cols, width), part(2 * cols, width), whole(t, width)],
        whole(t, width),
        tokens_f32,
        (dq, after(dkv, ffn_total), qo_w, kv_w, grad_one),
        us=5,
    )
    sent = red.first(grad_tokens)
    ffn_pieces = plane_gather(sum_levels(after(to_heads(ffn_total), sent)), rows)
    own_total, *total = totals(red.parts(), info, False)
    out_up, out_down = place_ffn(ffn_pieces, info)
    chips = gather_chips(sum_arrays([own_total, *to_levels(total)]), rows)
    pieces = gather_cores(after(chips, out_up), rows)

    out_qkv, out_o, out_b, outs = place_attention(pieces, info, cols, width)
    out_qkv = jnp.transpose(out_qkv.reshape(3, cols, width), (2, 0, 1))
    return (
        layer_output[None],
        grad_tokens[None],
        out_qkv,
        out_b,
        out_o,
        outs[2],
        outs[0],
        outs[1],
        out_up,
        outs[6],
        out_down,
        outs[5],
        outs[3],
        outs[4],
    )


def solution(mesh):
    return jax.shard_map(
        functools.partial(body, mesh.shape["rows"], mesh.shape["heads"]),
        mesh=mesh,
        in_specs=(
            P("rows", "heads", None),
            P("rows", None),
            P(None, None, "heads"),
            P(None, "heads"),
            P("heads", None),
            P(),
            P(),
            P(),
            P(None, "heads"),
            P("heads"),
            P("heads", None),
            P(),
            P(),
            P(),
            P(),
            P("rows", "heads", None),
        ),
        out_specs=(
            P("rows", "heads", None),
            P("rows", "heads", None),
            P(None, None, "heads"),
            P(None, "heads"),
            P("heads", None),
            P(),
            P(),
            P(),
            P(None, "heads"),
            P("heads"),
            P("heads", None),
            P(),
            P(),
            P(),
        ),
        check_vma=False,
    )
```

```python
import functools

import jax
import jax.numpy as jnp
from jax import lax
from jax.experimental import pallas as pl
from jax.experimental.pallas import tpu as pltpu
from jax.sharding import PartitionSpec as P

EPSILON = 1e-05
PLANE = 8
VMEM_LIMIT = 48 * 1024 * 1024
BF = jnp.bfloat16
F32 = jnp.float32


def dot(a, b, dims=((1,), (0,))):
    return lax.dot_general(a, b, (dims, ((), ())), preferred_element_type=F32)


def dot_nt(a, b):
    return dot(a, b, ((1,), (1,)))


def dot_tn(a, b):
    return dot(a, b, ((0,), (0,)))


def estimate(us):
    return pl.CostEstimate(flops=int(us * 1e3), bytes_accessed=0, transcendentals=0)


def call_prefetch(kernel, grid, in_specs, out_specs, out_shape, args, us, scratch=()):
    return pl.pallas_call(
        kernel,
        grid_spec=pltpu.PrefetchScalarGridSpec(
            num_scalar_prefetch=1, grid=grid, in_specs=in_specs, out_specs=out_specs, scratch_shapes=list(scratch)
        ),
        out_shape=out_shape,
        compiler_params=pltpu.CompilerParams(vmem_limit_bytes=VMEM_LIMIT),
        cost_estimate=estimate(us),
    )(*args)


def call(kernel, grid, in_specs, out_specs, out_shape, args, us, scratch=(), aliases=None, limit=VMEM_LIMIT):
    return pl.pallas_call(
        kernel,
        grid=grid,
        input_output_aliases=aliases or {},
        in_specs=in_specs,
        out_specs=out_specs,
        out_shape=out_shape,
        scratch_shapes=list(scratch),
        compiler_params=pltpu.CompilerParams(vmem_limit_bytes=limit),
        cost_estimate=estimate(us),
    )(*args)


def whole(*shape):
    return pl.BlockSpec(shape, lambda g: (0,) * len(shape))


def part(*shape, base=0, flip=0):
    return pl.BlockSpec((None, *shape), lambda g: ((g + base) ^ flip,) + (0,) * len(shape))


def other(*shape):
    return pl.BlockSpec((None, *shape), lambda g: (jnp.maximum(g - 1, 0),) + (0,) * len(shape))


ANY_SPEC = pl.BlockSpec(memory_space=pl.ANY)


def struct(shape, dtype):
    return jax.ShapeDtypeStruct(shape, dtype)


def permute(array, axis, size, partner):
    return lax.ppermute(array, axis, [(i, partner(i)) for i in range(size)])


def first_partner(i):
    return i ^ (4 if i & 1 else 2)


def second_partner(i):
    return i ^ (2 if i & 1 else 4)


def core_partner(i):
    return i ^ 1


def after(array, *others):
    return lax.optimization_barrier((array, others))[0]


def gather_chips(piece, rows, *others):
    p1 = permute(piece, "rows", rows, first_partner)
    p2 = permute(piece, "rows", rows, second_partner)
    return [piece, p1, p2, permute(after(p1, *others), "rows", rows, second_partner)]


def gather_cores(own, rows):
    return own + [permute(p, "rows", rows, core_partner) for p in own]


def plane_gather(piece, rows):
    return gather_cores(gather_chips(piece, rows), rows)


def plane_slots(rank):
    me = rank & (PLANE - 1)
    core = rank & 1
    first = jnp.where(core == 1, 4, 2)
    second = jnp.where(core == 1, 2, 4)
    return [
        me,
        me ^ first,
        me ^ second,
        me ^ 6,
        me ^ 1,
        me ^ 1 ^ second,
        me ^ 1 ^ first,
        me ^ 7,
    ]


def to_levels(arrays):
    size = len(arrays) + 1
    return [permute(a, "heads", size, lambda i, m=m: i ^ m) for m, a in enumerate(arrays, 1)]


def sum_kernel(*refs):
    *ins, out = refs
    total = ins[0][...].astype(F32)
    for ref in ins[1:]:
        total = total + ref[...].astype(F32)
    out[...] = total.astype(BF)


def sums(*jobs):
    tail = jobs[0][0][0].shape[1:]
    zeros = (0,) * len(tail)
    counts = [len(job) for job in jobs]

    def kernel(*refs):
        base = 0
        for n, count in enumerate(counts):
            sum_kernel(*refs[base : base + count], refs[-1].at[n])
            base += count

    return call(
        kernel,
        (1,),
        [
            pl.BlockSpec((None, *tail), lambda g, slot=slot: (slot, *zeros)) for job in jobs for _, slot in job
        ],
        whole(len(jobs), *tail),
        struct((len(jobs), *tail), BF),
        [array for job in jobs for array, _ in job],
        us=2,
    )


class Reduction:
    def __init__(self, rows, together=True):
        self.rows = rows
        self.together = together
        self.kept, self.came = [], []

    def cores(self, sent, kept):
        self.kept.append(kept)
        self.came.append([permute(a, "rows", self.rows, core_partner) for a in sent])

    def near(self, n, slot):
        came = self.came[n]
        if len(came) == 1:
            return [(self.kept[n], slot), (came[0], slot)]
        return [(self.kept[n], slot), (came[slot], 0)]

    def second(self, *others):
        self.came = after(self.came, *others)
        jobs = [self.near(n, slot) for n in range(len(self.kept)) for slot in (2, 3)]
        sent = [sums(*jobs)] if self.together else [sums(job) for job in jobs]
        came = [permute(a, "rows", self.rows, second_partner) for a in sent]
        self.close = [(came[0], n) if self.together else (came[n], 0) for n in range(len(jobs))]
        return sent

    def first(self, *others):
        arrays = after([array for array, _ in self.close], *others)
        self.close = [(array, slot) for array, (_, slot) in zip(arrays, self.close)]
        sent = sums(*[[*self.near(n, 1), self.close[2 * n + 1]] for n in range(len(self.kept))])
        self.last = permute(sent, "rows", self.rows, first_partner)
        return sent

    def parts(self, *others):
        last = after(self.last, *others)
        mask = PLANE
        sets = range(len(self.kept))
        while mask < self.rows:
            total = sums(*[[*self.near(n, 0), self.close[2 * n], (last, n)] for n in sets])
            other = permute(total, "rows", self.rows, lambda i, m=mask: i ^ m)
            last = (last.astype(F32) + other.astype(F32)).astype(BF)
            mask *= 2
        return [[*self.near(n, 0), self.close[2 * n], (last, n)] for n in sets]


def total_kernel(sets, stacked, info_ref, *refs):
    outs = refs[4 * sets :]
    groups = refs[0].shape[0]
    base = 0
    for n in range(sets):
        arrays = refs[4 * n : 4 * n + 4]
        rows = arrays[0].shape[1]
        for k in range(groups):
            total = arrays[0][k].astype(F32)
            for array in arrays[1:]:
                total = total + array[k].astype(F32)
            if stacked:
                outs[0][info_ref[PLANE] ^ k, base : base + rows, :] = total.astype(BF)
            else:
                outs[k][base : base + rows, :] = total.astype(BF)
        base += rows


def totals(sets, info, stacked):
    heads, rows, cols = sets[0][0][0].shape[1:]
    specs = [
        pl.BlockSpec((None, heads, rows, cols), lambda g, slot=slot: (slot, 0, 0, 0))
        for pairs in sets
        for _, slot in pairs
    ]
    rows *= len(sets)
    shapes = [struct((heads, rows, cols), BF)] if stacked else [struct((rows, cols), BF)] * heads
    return call(
        functools.partial(total_kernel, len(sets), stacked),
        (1,),
        [SMEM_SPEC] + specs,
        [whole(*shape.shape) for shape in shapes],
        shapes,
        [info] + [array for pairs in sets for array, _ in pairs],
        us=2,
    )


def others_first(array, info):
    heads, *tail = array.shape

    def kernel(info_ref, in_ref, out_ref):
        for k in range(1, heads):
            out_ref[k - 1] = in_ref[info_ref[PLANE] ^ k]

    return call(
        kernel, (1,), [SMEM_SPEC, whole(heads, *tail)], whole(heads - 1, *tail),
        struct((heads - 1, *tail), array.dtype), (info, array), us=2,
    )


def to_heads(array):
    return lax.all_to_all(array, "heads", 0, 0, tiled=True)


def sum_arrays(arrays):
    return sums([(array[None], 0) for array in arrays])[0]


def sum_levels(array):
    return sums([(array, n) for n in range(array.shape[0])])[0]


SMEM_SPEC = pl.BlockSpec(memory_space=pltpu.SMEM)
VMEM_SPEC = pl.BlockSpec(memory_space=pltpu.VMEM)


def bias_rows(vectors, width):
    rest = jnp.stack([jnp.pad(v, (0, width - v.size)) for v in vectors])
    rows = []
    for _ in range(3):
        rounded = lax.reduce_precision(rest, 8, 7)
        rows.append(rounded.astype(BF))
        rest = rest - rounded
    rows = jnp.concatenate(rows, axis=0)
    return jnp.pad(rows, ((0, 16 - rows.shape[0]), (0, 0)))


def place_weights_kernel(count, parts, info_ref, *refs):
    owns = refs[:parts]
    pieces = refs[parts : parts + count]
    outs = refs[parts + count :]
    mine = pl.program_id(0) == 0

    @pl.when(mine)
    def _():
        for own, out in zip(owns, outs):
            out[...] = own[...]

    @pl.when(jnp.logical_not(mine))
    def _():
        base = 0
        for out in outs:
            if out.shape[0] < PLANE * 16:
                out[...] = pieces[0][base : base + out.shape[0], :]
                continue
            step = out.shape[0] // PLANE
            for n in range(count):
                start = pl.multiple_of(info_ref[n] * step, 16)
                out[pl.ds(start, step), :] = pieces[n][base : base + step, :]
            base += step


def place_weights(owns, pieces, info):
    count, parts = len(pieces), len(owns)
    others, _, cols = pieces[0].shape
    rows = sum(own.shape[0] if own.shape[0] < PLANE * 16 else own.shape[0] // PLANE for own in owns)

    def piece_index(g, info_ref):
        return (jnp.maximum(g - 1, 0), 0, 0)

    return pl.pallas_call(
        functools.partial(place_weights_kernel, count, parts),
        grid_spec=pltpu.PrefetchScalarGridSpec(
            num_scalar_prefetch=1,
            grid=(others + 1,),
            in_specs=[pl.BlockSpec(own.shape, lambda g, s: (0, 0)) for own in owns]
            + [pl.BlockSpec((None, rows, cols), piece_index)] * count,
            out_specs=[pl.BlockSpec((None, *own.shape), lambda g, s: (g, 0, 0)) for own in owns],
        ),
        out_shape=[struct((others + 1, *own.shape), BF) for own in owns],
        compiler_params=pltpu.CompilerParams(vmem_limit_bytes=VMEM_LIMIT),
        cost_estimate=estimate(3 * parts),
    )(info, *owns, *pieces)


def place_ffn_kernel(count, info_ref, *refs):
    up, down, turned = refs[count:]
    step = refs[0].shape[0] // 2
    for n in range(count):
        start = pl.multiple_of(info_ref[n] * step, 16)
        turned[pl.ds(start, step), :] = refs[n][:step, :].astype(F32)
        down[pl.ds(start, step), :] = refs[n][step:, :].astype(F32)
    up[...] = jnp.transpose(turned[...])


def place_ffn(pieces, info):
    rows, cols = pieces[0].shape
    count = len(pieces)
    hidden = count * rows // 2
    return pl.pallas_call(
        functools.partial(place_ffn_kernel, count),
        in_specs=[SMEM_SPEC] + [VMEM_SPEC] * count,
        out_specs=[VMEM_SPEC] * 2,
        out_shape=[struct((cols, hidden), F32), struct((hidden, cols), F32)],
        scratch_shapes=[pltpu.VMEM((hidden, cols), F32)],
        compiler_params=pltpu.CompilerParams(vmem_limit_bytes=VMEM_LIMIT),
        cost_estimate=estimate(4),
    )(info, *pieces)


def place_attention_kernel(count, cols, width, info_ref, *refs):
    out_qkv, out_o, out_b, vectors, bias = refs[count:]
    step = refs[0].shape[0] // 2
    for n in range(count):
        start = pl.multiple_of(info_ref[n] * step, 16)
        wide = refs[n][:step, :].astype(F32)

        @pl.when(start < cols)
        def _():
            out_qkv[pl.ds(start, step), :] = wide[:, :width]
            bias[pl.ds(start, step), :] = wide[:, width:]

        @pl.when(start >= cols)
        def _():
            out_o[pl.ds(pl.multiple_of(start - cols, 16), step), :] = wide[:, :width]

        @pl.when(start == cols)
        def _():
            groups = width // 128
            for v in range(vectors.shape[0]):
                for j in range(groups):
                    row = v * groups + j
                    vectors[v : v + 1, j * 128 : (j + 1) * 128] = wide[row : row + 1, width:]

        wide = refs[n][step:, :].astype(F32)
        out_qkv[pl.ds(cols + start, step), :] = wide[:, :width]
        bias[pl.ds(cols + start, step), :] = wide[:, width:]
    row = jnp.transpose(bias[...])[0:1, :]
    for j in range(3):
        out_b[j : j + 1, :] = row[:, j * cols : (j + 1) * cols]


def place_attention(pieces, info, cols, width):
    count = len(pieces)
    return pl.pallas_call(
        functools.partial(place_attention_kernel, count, cols, width),
        in_specs=[SMEM_SPEC] + [VMEM_SPEC] * count,
        out_specs=[VMEM_SPEC] * 4,
        out_shape=[
            struct((3 * cols, width), F32),
            struct((cols, width), F32),
            struct((3, cols), F32),
            struct((7, width), F32),
        ],
        scratch_shapes=[pltpu.VMEM((3 * cols, 128), F32)],
        compiler_params=pltpu.CompilerParams(vmem_limit_bytes=VMEM_LIMIT),
        cost_estimate=estimate(3),
    )(info, *pieces)


def head_sums(values, heads, hd):
    row = lax.broadcasted_iota(jnp.int32, (heads * hd, 128), 0)
    lane = lax.broadcasted_iota(jnp.int32, (heads * hd, 128), 1)
    own = ((row >= lane * hd) & (row < (lane + 1) * hd)).astype(F32).astype(BF)
    high = values.astype(BF)
    low = (values - high.astype(F32)).astype(BF)
    return dot(high, own) + dot(low, own)


def phi_of(raw, halves, head, feats, scale):
    part_raw = raw[:, head * feats : (head + 1) * feats]
    return jnp.exp(scale * part_raw - halves[:, head : head + 1]) * feats ** (-0.5)


def half_norms(vectors, heads, hd, scale):
    wide = vectors.astype(F32)
    return 0.5 * scale * scale * head_sums(wide * wide, heads, hd)


def edge_rows(first, last, head):
    lane = lax.broadcasted_iota(jnp.int32, (first.shape[0], 32), 1)
    return jnp.where(lane == head, first, 0.0) + jnp.where(lane == 16 + head, last, 0.0)


def edge_left(value, norm, first, last, head):
    return jnp.concatenate(
        [value * first, value * last, edge_rows(norm * first, norm * last, head)], axis=1
    ).astype(BF)


def edge_states(values, norms, phi, heads, hd, feats):
    first_values, last_values = values
    cols = heads * hd
    left = jnp.concatenate([first_values, last_values, norms], axis=1).astype(BF)
    state = dot_tn(left, phi)
    row = lax.broadcasted_iota(jnp.int32, (16, feats), 0)
    out = []
    for n in range(2):
        base = 2 * cols + 16 * n
        rows = [state[n * cols + h * hd : n * cols + (h + 1) * hd, h * feats : (h + 1) * feats] for h in range(heads)]
        total = jnp.zeros((16, feats), F32)
        for h in range(heads):
            total = jnp.where(row == h, state[base : base + 16, h * feats : (h + 1) * feats], total)
        out.append(jnp.concatenate([*rows, total], axis=0).astype(BF))
    return out


def put_edges(edge_ref, firsts, lasts, level, group):
    for m in range(1, edge_ref.shape[0]):
        place = level ^ m

        @pl.when(place > level)
        def _():
            edge_ref[place, group ^ m] = lasts

        @pl.when(place < level)
        def _():
            edge_ref[place, group ^ m] = firsts


def take_edges(came_ref, match_ref, level):
    left = right = None
    count = came_ref.shape[0] - 1
    for m in range(count):
        wide = came_ref[level ^ (m + 1)].astype(F32)
        a, b = wide * match_ref[m], wide * match_ref[count + m]
        left = a if left is None else left + a
        right = b if right is None else right + b
    return left.astype(BF), right.astype(BF)


def stack_edges(f, l, h, hd, cols):
    return jnp.concatenate(
        [f[h * hd : (h + 1) * hd], l[h * hd : (h + 1) * hd], f[cols:], l[cols:]], axis=0
    )


def with_one(value):
    lane = lax.broadcasted_iota(jnp.int32, value.shape, 1)
    return jnp.concatenate([value, jnp.where(lane == 0, 1.0, 0.0).astype(value.dtype)], axis=1)


def keys_kernel(heads, hd, feats, info_ref, x_ref, w_ref, b_ref, om_ref, ends_ref, *refs):
    *before, kv_ref, phi_ref, edge_ref = refs
    cols = heads * hd
    scale = hd ** (-0.25)
    kv = (dot_nt(x_ref[...], w_ref[...]) + b_ref[...]).astype(BF)
    kv_ref[...] = kv
    raw = dot(kv[:, :cols], om_ref[...])
    first, last = ends_ref[:, 0:1], ends_ref[:, 1:2]
    halves = half_norms(kv[:, :cols], heads, hd, scale)
    for h in range(heads):
        phi_ref[:, h * feats : (h + 1) * feats] = phi_of(raw, halves, h, feats, scale).astype(BF)
    values = kv[:, cols:].astype(F32)
    lane = lax.broadcasted_iota(jnp.int32, (kv.shape[0], 32), 1)
    firsts, lasts = edge_states(
        (values * first, values * last), jnp.where(lane < 16, first, last), phi_ref[...], heads, hd, feats
    )
    if not before:
        edge_ref[0] = firsts
        edge_ref[1] = lasts
        return
    group = pl.program_id(0) + 1
    put_edges(edge_ref, firsts, lasts, info_ref[PLANE], group)

    @pl.when(group == 1)
    def _():
        put_edges(edge_ref, before[-1][0], before[-1][1], info_ref[PLANE], 0)


def queries_kernel(heads, hd, feats, x_ref, w_ref, b_ref, om_ref, same_ref, kv_ref, phik_ref, *refs):
    q_ref, phi_ref, nd_ref = refs[-3:]
    cols = heads * hd
    scale = hd ** (-0.25)
    q = (dot_nt(x_ref[...], w_ref[:cols, :]) + b_ref[...]).astype(BF)
    q_ref[...] = q
    raw = dot(q, om_ref[...])
    same = same_ref[...]
    halves = half_norms(q, heads, hd, scale)
    for h in range(heads):
        phi = phi_of(raw, halves, h, feats, scale).astype(BF)
        phi_ref[:, h * feats : (h + 1) * feats] = phi
        scores = dot_nt(phi, phik_ref[:, h * feats : (h + 1) * feats]).astype(BF) * same
        value = kv_ref[:, cols + h * hd : cols + (h + 1) * hd]
        nd_ref[:, 2 * h * hd : 2 * (h + 1) * hd] = dot(scores, with_one(value))


def feature_back(dphi, phi, vectors, om, heads, hd, feats, scale):
    cols = heads * hd
    lows = []
    for h in range(heads):
        grad_raw = dphi[h] * phi[:, h * feats : (h + 1) * feats].astype(F32)
        lows.append((scale * grad_raw).astype(BF))
    through = dot_nt(jnp.concatenate(lows, axis=1), om)
    wide = vectors.astype(F32)
    lane = lax.broadcasted_iota(jnp.int32, wide.shape, 1)
    total = through[:, cols : cols + 1]
    for h in range(1, heads):
        total = jnp.where(lane >= h * hd, through[:, cols + h : cols + h + 1], total)
    return through[:, :cols] - scale * total * wide


def weight_grad(grad_ref, rows, left, right):
    width = right.shape[1]
    lane = lax.broadcasted_iota(jnp.int32, (left.shape[0], 128), 1)
    grad_ref[rows, :width] = dot_tn(left, right).astype(BF)
    grad_ref[rows, width:] = dot_tn(left, jnp.where(lane == 0, 1.0, 0.0).astype(BF)).astype(BF)


def put_slices(source_ref, base, sent_refs, kept_ref, info_ref, placed=True):
    step = source_ref.shape[0] // PLANE
    half = PLANE // 2
    for n in range(PLANE):
        if n < half:
            out = kept_ref.at[n]
        else:
            out = sent_refs[n - half] if len(sent_refs) > 1 else sent_refs[0].at[n - half]
        start = pl.multiple_of(jnp.where(placed, info_ref[n], n) * step, 16)
        out[base : base + step, :] = source_ref[pl.ds(start, step), :]


def queries_back_kernel(
    heads, hd, feats, info_ref, dnd_ref, q_ref, phiq_ref, kv_ref, phik_ref, cf_ref, cl_ref, om_ref, same_ref,
    ends_ref, att_ref, x_ref, one_ref, one_sums_ref, two_sums_ref, bup_ref, dq_ref, dphik_ref, dv_ref, sent_ref, kept_ref,
    grad_ref,
):
    cols = heads * hd
    scale = hd ** (-0.25)
    first, last = ends_ref[:, 0:1], ends_ref[:, 1:2]
    same = same_ref[...]
    dphis, dvs = [], []
    for h in range(heads):
        phiq = phiq_ref[:, h * feats : (h + 1) * feats]
        phik = phik_ref[:, h * feats : (h + 1) * feats]
        value = with_one(kv_ref[:, cols + h * hd : cols + (h + 1) * hd])
        dnd = dnd_ref[:, 2 * h * hd : 2 * (h + 1) * hd]
        dscore = dot_nt(dnd, value).astype(BF) * same
        wide = dnd.astype(F32)
        left = edge_left(wide[:, :hd], wide[:, hd : hd + 1], first, last, h)
        stack = stack_edges(cf_ref[...], cl_ref[...], h, hd, cols)
        dphis.append(dot(dscore, phik) + dot(left, stack))
        dscore_t = dot_nt(value, dnd).astype(BF) * same
        score_t = dot_nt(phik, phiq).astype(BF) * same
        dphik_ref[:, h * feats : (h + 1) * feats] = dot(dscore_t, phiq).astype(BF)
        dvs.append(dot(score_t, dnd)[:, :hd])
    dv_ref[...] = jnp.concatenate(dvs, axis=1)
    dq = feature_back(dphis, phiq_ref[...], q_ref[...], om_ref[...], heads, hd, feats, scale)
    dq = dq.astype(BF)
    dq_ref[...] = dq
    weight_grad(grad_ref, slice(0, cols), dq, x_ref[...])
    width = one_ref.shape[1]
    vectors = [one_sums_ref[n : n + 1, :] for n in range(3)] + [two_sums_ref[n : n + 1, :] for n in range(3)]
    vectors = vectors + [bup_ref[...]]
    block = [v[:, n : n + 128] for v in vectors for n in range(0, width, 128)]
    step = grad_ref.shape[0] // PLANE
    block.append(jnp.zeros((step - len(block), 128), F32))
    block = jnp.concatenate(block, axis=0).astype(BF)
    grad_ref[cols:, :width] = dot_tn(att_ref[...], one_ref[...]).astype(BF)
    for n in range(cols, 2 * cols, step):
        grad_ref[n : n + step, width:] = block
    put_slices(grad_ref, 0, [sent_ref], kept_ref, info_ref)


def keys_back_kernel(
    heads, hd, feats, info_ref, match_ref, kv_ref, phik_ref, dphik_ref, dv_ref, came_ref, om_ref, ends_ref, x_ref, *refs
):
    dkv_ref, *sent, kept_ref, grad_ref = refs
    cols = heads * hd
    scale = hd ** (-0.25)
    first, last = ends_ref[:, 0:1], ends_ref[:, 1:2]
    rf, rl = take_edges(came_ref, match_ref, info_ref[PLANE])
    dphis, dvs = [], []
    for h in range(heads):
        phik = phik_ref[:, h * feats : (h + 1) * feats]
        value = kv_ref[:, cols + h * hd : cols + (h + 1) * hd].astype(F32)
        stack = stack_edges(rf, rl, h, hd, cols)
        dphis.append(
            dphik_ref[:, h * feats : (h + 1) * feats].astype(F32) + dot(edge_left(value, 1.0, first, last, h), stack)
        )
        far = dot_nt(phik, stack[: 2 * hd])
        dvs.append(dv_ref[:, h * hd : (h + 1) * hd] + first * far[:, :hd] + last * far[:, hd:])
    dk = feature_back(dphis, phik_ref[...], kv_ref[:, :cols], om_ref[...], heads, hd, feats, scale)
    dkv = jnp.concatenate([dk] + dvs, axis=1).astype(BF)
    dkv_ref[...] = dkv
    weight_grad(grad_ref, slice(0, 2 * cols), dkv, x_ref[...])
    put_slices(grad_ref, 0, sent, kept_ref, info_ref)


def tokens_kernel(cols, dq_ref, dkv_ref, qo_ref, kv_ref, one_ref, out_ref):
    back = dot(dq_ref[...], qo_ref[:cols, :]) + dot(dkv_ref[...], kv_ref[...])

    @pl.when(pl.program_id(0) == 0)
    def _():
        out_ref[...] = one_ref[...] + back

    @pl.when(pl.program_id(0) > 0)
    def _():
        out_ref[...] += back


def norm_of(hidden):
    average = jnp.mean(hidden, axis=-1, keepdims=True)
    centred = hidden - average
    inverse = lax.rsqrt(jnp.mean(centred * centred, axis=-1, keepdims=True) + EPSILON)
    return centred * inverse, inverse


def norm_back(grad_in, normed, inverse, gain):
    scaled = grad_in * gain
    centred = (
        scaled
        - jnp.mean(scaled, axis=-1, keepdims=True)
        - normed * jnp.mean(scaled * normed, axis=-1, keepdims=True)
    )
    return centred * inverse


def column_sums(arrays, rows):
    sums = [jnp.sum(a, axis=0, keepdims=True) for a in arrays]
    return jnp.concatenate(sums + [jnp.zeros((rows - len(sums), sums[0].shape[1]), F32)], axis=0)


def gelu_both(v):
    gate = 0.5 + 0.5 * lax.erf(v * 0.5**0.5)
    bell = jnp.exp(-0.5 * v * v) * (2.0 * jnp.pi) ** (-0.5)
    return v * gate, gate + v * bell


def ffn_copies(own_up, own_down, pieces, up_ref, down_ref, sems, k):
    if k == 0:
        return [
            pltpu.make_async_copy(own_up, up_ref.at[0], sems.at[0, 0]),
            pltpu.make_async_copy(own_down, down_ref.at[0], sems.at[0, 1]),
        ]
    step = up_ref.shape[1] // PLANE
    base = pieces[0].shape[1] - 2 * step
    copies = []
    for n, piece in enumerate(pieces):
        for part_n, ref in enumerate((up_ref, down_ref)):
            copies.append(
                pltpu.make_async_copy(
                    piece.at[k - 1, pl.ds(base + part_n * step, step)],
                    ref.at[k, pl.ds(n * step, step)],
                    sems.at[k, 2 * n + part_n],
                )
            )
    return copies


def middle_kernel(heads, hd, feats, info_ref, match_ref, phi_ref, nd_ref, came_ref, ends_ref, wo_ref, x_ref, vec_ref, bup_ref, cot_ref, *refs):
    own_up, own_down, *pieces = refs[: 2 + PLANE]
    (
        att_ref, cf_ref, cl_ref, out_ref, gradb_ref, one_out, onelow_ref, sums1_ref, sums2_ref, dnd_ref, edge_ref,
        sent1_ref, sent2_ref, sent3_ref, sent4_ref, kept_ref,
        acc, first_low, normed_one, inverse_one, act_s, slope_s, two, two_low, att_s, den_s, up_s, down_s, grad_s, sems,
    ) = refs[2 + PLANE :]
    sent = [sent1_ref, sent2_ref, sent3_ref, sent4_ref]
    groups = att_s.shape[0]
    stage = pl.program_id(0) // groups
    g = pl.program_id(0) % groups
    cols = heads * hd
    t = acc.shape[0]
    level = info_ref[PLANE]
    final = g == groups - 1

    @pl.when(pl.program_id(0) == 0)
    def _():
        for k in range(groups):
            for copy in ffn_copies(own_up, own_down, pieces, up_s, down_s, sems, k):
                copy.start()

    def first_add(value, start):
        @pl.when(g == 0)
        def _():
            acc[...] = start() + value

        @pl.when(g > 0)
        def _():
            acc[...] += value

    @pl.when(stage == 0)
    def _():
        first, last = ends_ref[:, 0:1], ends_ref[:, 1:2]
        cf, cl = take_edges(came_ref, match_ref, level)
        cf_ref[...] = cf
        cl_ref[...] = cl
        lane = lax.broadcasted_iota(jnp.int32, (t, 128), 1)
        dens = jnp.zeros((t, 128), F32)
        outs = []
        for h in range(heads):
            far = dot_nt(phi_ref[:, h * feats : (h + 1) * feats], stack_edges(cf, cl, h, hd, cols))
            nd = nd_ref[:, 2 * h * hd : 2 * (h + 1) * hd]
            num = nd[:, :hd] + first * far[:, :hd] + last * far[:, hd : 2 * hd]
            den = (
                nd[:, hd : hd + 1]
                + first * far[:, 2 * hd + h : 2 * hd + h + 1]
                + last * far[:, 2 * hd + 16 + h : 2 * hd + 17 + h]
            )
            outs.append(num / den)
            dens = dens + jnp.where(lane == h, den, 0.0)
        att = jnp.concatenate(outs, axis=1).astype(BF)
        att_ref[...] = att
        att_s[g] = att
        den_s[g] = dens
        first_add(dot(att, wo_ref[...]), lambda: x_ref[...].astype(F32) + vec_ref[0:1, :])

        @pl.when(final)
        def _():
            normed, inverse = norm_of(acc[...])
            normed_one[...] = normed
            inverse_one[...] = jnp.broadcast_to(inverse, inverse_one.shape)
            first_low[...] = (normed * vec_ref[1:2, :] + vec_ref[2:3, :]).astype(BF)

    @pl.when(stage == 1)
    def _():
        for k in range(groups):

            @pl.when(g == k)
            def _():
                for copy in ffn_copies(own_up, own_down, pieces, up_s, down_s, sems, k):
                    copy.wait()

        act, slope = gelu_both(dot_nt(first_low[...], up_s[g]) + bup_ref[...])
        act = act.astype(BF)
        act_s[g] = act
        slope_s[g] = slope.astype(BF)
        first_add(
            dot(act, down_s[g]),
            lambda: normed_one[...] * vec_ref[1:2, :] + vec_ref[2:3, :] + vec_ref[3:4, :],
        )

        @pl.when(final)
        def _():
            normed, inverse = norm_of(acc[...])
            gain = vec_ref[4:5, :]
            out_ref[...] = (normed * gain + vec_ref[5:6, :]).astype(BF)
            grad_in = cot_ref[...].astype(F32)
            grad = norm_back(grad_in, normed, inverse, gain)
            two[...] = grad
            two_low[...] = grad.astype(BF)
            sums2_ref[...] = column_sums([grad_in * normed, grad_in, grad], 8)

    @pl.when(stage == 2)
    def _():
        step = up_s.shape[1] // PLANE
        low = two_low[...]
        dpre = dot_nt(low, down_s[g]) * slope_s[g].astype(F32)
        gradb_ref[...] = jnp.sum(dpre, axis=0, keepdims=True)
        pre_low = dpre.astype(BF)
        grad_s[...] = dot_tn(pre_low, first_low[...]).astype(BF)
        put_slices(grad_s, 0, sent, kept_ref, info_ref, g == 0)
        grad_s[...] = dot_tn(act_s[g], low).astype(BF)
        put_slices(grad_s, step, sent, kept_ref, info_ref, g == 0)
        first_add(dot(pre_low, up_s[g]), lambda: two[...])

        @pl.when(final)
        def _():
            grad_in = acc[...]
            normed = normed_one[...]
            one = norm_back(grad_in, normed, inverse_one[:, 0:1], vec_ref[1:2, :])
            one_out[...] = one
            onelow_ref[...] = one.astype(BF)
            sums1_ref[...] = column_sums([grad_in * normed, grad_in, one], 8)

    @pl.when(stage == 3)
    def _():
        first, last = ends_ref[:, 0:1], ends_ref[:, 1:2]
        datt = dot_nt(onelow_ref[...], wo_ref[...])
        dens = den_s[g]
        lane = lax.broadcasted_iota(jnp.int32, (t, cols), 1)
        den = dens[:, 0:1]
        for h in range(1, heads):
            den = jnp.where(lane >= h * hd, dens[:, h : h + 1], den)
        dnum = datt / den
        dden = -head_sums(dnum * att_s[g].astype(F32), heads, hd)
        one_lane = lax.broadcasted_iota(jnp.int32, (t, hd), 1) == 0
        for h in range(heads):
            dnd_ref[:, 2 * h * hd : 2 * (h + 1) * hd] = jnp.concatenate(
                [dnum[:, h * hd : (h + 1) * hd], jnp.where(one_lane, dden[:, h : h + 1], 0.0)], axis=1
            ).astype(BF)
        norms = jnp.concatenate([dden[:, :16] * first, dden[:, :16] * last], axis=1)
        firsts, lasts = edge_states((dnum * first, dnum * last), norms, phi_ref[...], heads, hd, feats)
        put_edges(edge_ref, firsts, lasts, level, g)


def body(
    rows, heads,
    tokens, segment_ids, w_qkv, b_qkv, w_out, b_out, gain_one, bias_one, w_up, b_up, w_down, b_down,
    gain_two, bias_two, omega, cotangent,
):
    rank = lax.axis_index("rows")
    level = lax.axis_index("heads")
    hd, feats = omega.shape
    _, length, width = tokens.shape
    cols = w_qkv.shape[2]
    nh = cols // hd
    hidden = w_up.shape[1]
    slots = plane_slots(rank)
    me = slots[0]
    info = jnp.stack(slots + [level]).astype(jnp.int32)
    x = tokens[0]

    def slice_of(array):
        step = array.shape[0] // PLANE
        return lax.dynamic_slice_in_dim(array, me * step, step, 0)

    def from_levels(piece):
        return to_levels([piece] * (heads - 1))

    wt = jnp.transpose(w_qkv, (1, 2, 0)).reshape(3 * cols, width)
    own_kv = wt[cols:]
    own_bias = bias_rows([b_qkv.reshape(-1), b_up], width)
    own_qo = jnp.concatenate([wt[:cols], w_out], axis=0)
    own_up = w_up.T
    rows_of = 2 * cols // PLANE
    kv_slice = lax.dynamic_slice_in_dim(wt, cols + me * rows_of, rows_of, 0)
    q_slice = lax.dynamic_slice_in_dim(wt, jnp.minimum(me, PLANE // 2 - 1) * rows_of, rows_of, 0)
    o_slice = lax.dynamic_slice_in_dim(w_out, jnp.maximum(me - PLANE // 2, 0) * rows_of, rows_of, 0)
    qo_slice = jnp.where(me < PLANE // 2, q_slice, o_slice)
    near = from_levels(jnp.concatenate([kv_slice, qo_slice, own_bias], axis=0))
    rest = jnp.concatenate([slice_of(own_up), slice_of(w_down)], axis=0)
    rest = jnp.broadcast_to(rest[None], (heads, *rest.shape))
    own_bias_qkv = b_qkv.reshape(1, -1)

    segments = lax.dynamic_slice_in_dim(segment_ids[0], level * length, length, 0)
    by_level = segment_ids[0].reshape(heads, length)
    firsts, lasts = by_level[:, 0], by_level[:, -1]
    my_first, my_last = segments[0], segments[-1]
    ends = jnp.stack([segments == my_first, segments == my_last], axis=1).astype(F32)
    same = (segments[:, None] == segments[None, :]).astype(BF)
    index = jnp.arange(1, heads) ^ level
    there = index[:, None] == jnp.arange(heads)[None, :]
    index_first = jnp.sum(jnp.where(there, firsts[None], 0), axis=1)
    index_last = jnp.sum(jnp.where(there, lasts[None], 0), axis=1)
    match = jnp.concatenate(
        [(index < level) & (index_last == my_first), (index > level) & (index_first == my_last)]
    ).astype(F32)

    eye = jnp.eye(nh, dtype=BF)
    om = (eye[:, None, :, None] * omega[None, :, None, :]).reshape(cols, nh * feats)
    om_back = jnp.concatenate(
        [om, jnp.repeat(eye, feats, axis=1), jnp.zeros((16 - nh, nh * feats), BF)], axis=0
    )
    edge = cols + 16
    dims = (nh, hd, feats)
    t = length
    aug = width + 128

    half = PLANE // 2
    edge_shape = struct((heads, heads, edge, feats), BF)
    edge_spec = pl.BlockSpec((heads, None, edge, feats), lambda g: (0, g, 0, 0))

    def slot_spec(count, wide):
        return pl.BlockSpec((half, None, count, wide), lambda g: (0, g, 0, 0))

    def slot_shape(count, wide):
        return struct((half, heads, count, wide), BF)

    def of_groups(base, *shape):
        return part(*shape, base=base) if base else whole(*shape)

    def keys(base, count, weights, bias, *before):
        return call(
            functools.partial(keys_kernel, *dims),
            (count,),
            [
                SMEM_SPEC, whole(t, width), of_groups(base, 2 * cols, width), of_groups(base, 1, 2 * cols),
                whole(cols, nh * feats), whole(t, 2),
            ]
            + [ANY_SPEC, ANY_SPEC, whole(2, edge, feats)][: len(before)],
            [
                part(t, 2 * cols, base=base),
                part(t, nh * feats, base=base),
                whole(*edge_shape.shape) if base else whole(2, edge, feats),
            ],
            [
                struct((heads, t, 2 * cols), BF),
                struct((heads, t, nh * feats), BF),
                edge_shape if base else struct((2, edge, feats), BF),
            ],
            (info, x, weights, bias, om, ends, *before),
            us=3 * count,
            aliases={6: 0, 7: 1} if base else None,
        )

    def queries(base, count, weights, bias, kv, phi_k, *before):
        return call(
            functools.partial(queries_kernel, *dims),
            (count,),
            [
                whole(t, width), of_groups(base, 2 * cols, width), of_groups(base, 1, cols),
                whole(cols, nh * feats), whole(t, t),
                part(t, 2 * cols, base=base), part(t, nh * feats, base=base),
            ]
            + [ANY_SPEC] * len(before),
            [
                part(t, cols, base=base), part(t, nh * feats, base=base), part(t, 2 * cols, base=base),
            ],
            [
                struct((heads, t, cols), BF),
                struct((heads, t, nh * feats), BF),
                struct((heads, t, 2 * cols), F32),
            ],
            (x, weights, bias, om, same, kv, phi_k, *before),
            us=3 * count,
            aliases={7 + n: n for n in range(len(before))},
        )

    near_rest = to_heads(after(rest, near))
    near = jnp.stack(near)
    p1 = permute(near, "rows", rows, first_partner)
    p2 = permute(near, "rows", rows, second_partner)
    own_keys = keys(0, 1, after(own_kv, near), own_bias_qkv[:, cols:])
    p3 = permute(p1, "rows", rows, second_partner)
    own_queries = queries(0, 1, after(own_qo, p1), own_bias_qkv[:, :cols], *own_keys[:2])
    pieces = gather_cores(after([near, p1, p2, p3], own_queries), rows)
    kv_w, qo_w, bias = place_weights([own_kv, own_qo, own_bias], pieces, info)
    bias = bias.astype(F32)
    bias = bias[:, 0:2] + (bias[:, 2:4] + bias[:, 4:6])
    bias_qkv = bias[:, 0:1, : 3 * cols]
    bias_q = bias_qkv[:, :, :cols]
    bias_kv = bias_qkv[:, :, cols:]
    at_slot = (jnp.stack(slots)[:, None] == jnp.arange(PLANE)[None, :])[None, :, :, None]
    by_slice = bias[1:, 1, :hidden].reshape(heads - 1, 1, PLANE, hidden // PLANE)
    by_slot = jnp.sum(jnp.where(at_slot, by_slice, 0.0), axis=2).reshape(heads - 1, 1, hidden)
    bias_up = jnp.concatenate([b_up[None, None], by_slot], axis=0)

    own_keys = after(own_keys, own_queries)
    kv, phi_k, edges = keys(1, heads - 1, kv_w, bias_kv, *own_keys)
    came = to_heads(edges)
    q, phi_q, local = queries(1, heads - 1, qo_w, bias_q, kv, phi_k, *own_queries)
    chips_ffn = gather_chips(others_first(after(near_rest, edges), info), rows)
    rest_w = gather_cores(after(chips_ffn, phi_q), rows)
    step = hidden // PLANE
    vec = jnp.pad(
        jnp.stack([b_out, gain_one, bias_one, b_down, gain_two, bias_two]), ((0, 2), (0, 0))
    )

    def staged(shape, *stages, at=0):
        def index(s):
            stage, g = s // heads, s % heads
            group = jnp.where(stage > stages[-1], heads - 1, 0)
            for n in stages:
                group = jnp.where(stage == n, g, group)
            if len(stages) == 2:
                between = (stage > stages[0]) & (stage < stages[1])
                group = jnp.where(between, heads - 1, group)
            return (group, at, 0)

        return pl.BlockSpec((None, *shape), lambda s: index(s))

    def staged_slots(shape, stage):
        spec = staged((1, 1), stage)
        return pl.BlockSpec((shape[0], None, *shape[1:]), lambda s: (0, spec.index_map(s)[0], 0, 0))

    tokens_bf, tokens_f32 = struct((t, width), BF), struct((t, width), F32)
    (
        att, far_f, far_l, layer_output, grad_b_up, grad_one, one_low, sums_one, sums_two, dnd, edges, *sent, kept,
    ) = call(
        functools.partial(middle_kernel, *dims),
        (4 * heads,),
        [
            SMEM_SPEC, SMEM_SPEC, staged((t, nh * feats), 0, 3), staged((t, 2 * cols), 0),
            staged_slots((heads, edge, feats), 0), whole(t, 2), staged((cols, width), 0, 3, at=1), whole(t, width),
            whole(8, width), staged((1, hidden), 1), whole(t, width), *[ANY_SPEC] * (2 + PLANE),
        ],
        [
            staged((t, cols), 0), staged((edge, feats), 0), staged((edge, feats), 0), whole(t, width),
            staged((1, hidden), 2), whole(t, width), whole(t, width), whole(8, width), whole(8, width),
            staged((t, 2 * cols), 3), whole(*edge_shape.shape), *[staged((2 * step, width), 2)] * half,
            staged_slots((half, 2 * step, width), 2),
        ],
        [
            struct((heads, t, cols), BF),
            struct((heads, edge, feats), BF),
            struct((heads, edge, feats), BF),
            tokens_bf,
            struct((heads, 1, hidden), F32),
            tokens_f32,
            tokens_bf,
            struct((8, width), F32),
            struct((8, width), F32),
            struct((heads, t, 2 * cols), BF),
            edge_shape,
            *[struct((heads, 2 * step, width), BF)] * half,
            slot_shape(2 * step, width),
        ],
        (
            info, match, phi_q, local, came, ends, qo_w, x, vec, bias_up, cotangent[0], own_up, w_down, *rest_w,
        ),
        us=50,
        scratch=[
            pltpu.VMEM((t, width), F32),
            pltpu.VMEM((t, width), BF),
            pltpu.VMEM((t, width), F32),
            pltpu.VMEM((t, 128), F32),
            pltpu.VMEM((heads, t, hidden), BF),
            pltpu.VMEM((heads, t, hidden), BF),
            pltpu.VMEM((t, width), F32),
            pltpu.VMEM((t, width), BF),
            pltpu.VMEM((heads, t, cols), BF),
            pltpu.VMEM((heads, t, 128), F32),
            pltpu.VMEM((heads, hidden, width), BF),
            pltpu.VMEM((heads, hidden, width), BF),
            pltpu.VMEM((hidden, width), BF),
            pltpu.SemaphoreType.DMA((heads, 2 * PLANE)),
        ],
        limit=60 * 1024 * 1024,
    )
    by_slot = grad_b_up[1:, 0].reshape(heads - 1, PLANE, 1, step)
    by_slice = jnp.sum(jnp.where(at_slot, by_slot, 0.0), axis=1).reshape(heads - 1, 1, hidden)
    grad_b_up = jnp.concatenate([grad_b_up[:1], by_slice], axis=0)

    back = to_heads(edges)
    ffn = Reduction(rows, together=False)
    ffn.cores([a[None] for a in sent], kept)
    ffn_sent = ffn.second()
    slice_rows = 2 * cols // PLANE
    dq, dphi_k, dv, *qo = call(
        functools.partial(queries_back_kernel, *dims),
        (heads,),
        [
            SMEM_SPEC, part(t, 2 * cols), part(t, cols), part(t, nh * feats), part(t, 2 * cols),
            part(t, nh * feats), part(edge, feats), part(edge, feats), whole(cols + 16, nh * feats), whole(t, t),
            whole(t, 2), part(t, cols), whole(t, width), whole(t, width), whole(8, width),
            whole(8, width), part(1, hidden),
        ],
        [
            part(t, cols), part(t, nh * feats), part(t, cols), *[slot_spec(slice_rows, aug)] * 2,
        ],
        [
            struct((heads, t, cols), BF),
            struct((heads, t, nh * feats), BF),
            struct((heads, t, cols), F32),
            *[slot_shape(slice_rows, aug)] * 2,
        ],
        (
            info, after(dnd, ffn_sent), q, phi_q, kv, phi_k, far_f, far_l, om_back, same, ends, att, x, one_low,
            sums_one, sums_two, grad_b_up,
        ),
        us=20,
        scratch=[pltpu.VMEM((2 * cols, aug), BF)],
    )
    red = Reduction(rows)
    red.cores(qo[:1], qo[1])
    back = after(back, ffn.first(dv))
    dkv, *kv_red = call(
        functools.partial(keys_back_kernel, *dims),
        (heads,),
        [
            SMEM_SPEC, SMEM_SPEC, part(t, 2 * cols), part(t, nh * feats), part(t, nh * feats), part(t, cols),
            edge_spec, whole(cols + 16, nh * feats), whole(t, 2), whole(t, width),
        ],
        [part(t, 2 * cols), *[part(slice_rows, aug)] * half, slot_spec(slice_rows, aug)],
        [
            struct((heads, t, 2 * cols), BF),
            *[struct((heads, slice_rows, aug), BF)] * half,
            slot_shape(slice_rows, aug),
        ],
        (info, match, kv, phi_k, dphi_k, dv, back, om_back, ends, x),
        us=12,
        scratch=[pltpu.VMEM((2 * cols, aug), BF)],
    )
    red.cores([a[None] for a in kv_red[:half]], kv_red[half])
    sent = red.second(dkv, ffn.last)
    (ffn_total,) = totals(ffn.parts(sent), info, True)
    grad_tokens = call(
        functools.partial(tokens_kernel, cols),
        (heads,),
        [part(t, cols), part(t, 2 * cols), part(2 * cols, width), part(2 * cols, width), whole(t, width)],
        whole(t, width),
        tokens_f32,
        (dq, after(dkv, ffn_total), qo_w, kv_w, grad_one),
        us=5,
    )
    sent = red.first(grad_tokens)
    ffn_pieces = plane_gather(sum_levels(after(to_heads(ffn_total), sent)), rows)
    own_total, *total = totals(red.parts(), info, False)
    out_up, out_down = place_ffn(ffn_pieces, info)
    chips = gather_chips(sum_arrays([own_total, *to_levels(total)]), rows)
    pieces = gather_cores(after(chips, out_up), rows)

    out_qkv, out_o, out_b, outs = place_attention(pieces, info, cols, width)
    out_qkv = jnp.transpose(out_qkv.reshape(3, cols, width), (2, 0, 1))
    return (
        layer_output[None],
        grad_tokens[None],
        out_qkv,
        out_b,
        out_o,
        outs[2],
        outs[0],
        outs[1],
        out_up,
        outs[6],
        out_down,
        outs[5],
        outs[3],
        outs[4],
    )


def solution(mesh):
    return jax.shard_map(
        functools.partial(body, mesh.shape["rows"], mesh.shape["heads"]),
        mesh=mesh,
        in_specs=(
            P("rows", "heads", None),
            P("rows", None),
            P(None, None, "heads"),
            P(None, "heads"),
            P("heads", None),
            P(),
            P(),
            P(),
            P(None, "heads"),
            P("heads"),
            P("heads", None),
            P(),
            P(),
            P(),
            P(),
            P("rows", "heads", None),
        ),
        out_specs=(
            P("rows", "heads", None),
            P("rows", "heads", None),
            P(None, None, "heads"),
            P(None, "heads"),
            P("heads", None),
            P(),
            P(),
            P(),
            P(None, "heads"),
            P("heads"),
            P("heads", None),
            P(),
            P(),
            P(),
        ),
        check_vma=False,
    )
```

```python
import functools

import jax
import jax.numpy as jnp
from jax import lax
from jax.experimental import pallas as pl
from jax.experimental.pallas import tpu as pltpu
from jax.sharding import PartitionSpec as P

EPSILON = 1e-05
PLANE = 8
VMEM_LIMIT = 48 * 1024 * 1024
BF = jnp.bfloat16
F32 = jnp.float32


def dot(a, b, dims=((1,), (0,))):
    return lax.dot_general(a, b, (dims, ((), ())), preferred_element_type=F32)


def dot_nt(a, b):
    return dot(a, b, ((1,), (1,)))


def dot_tn(a, b):
    return dot(a, b, ((0,), (0,)))


def estimate(us):
    return pl.CostEstimate(flops=int(us * 1e3), bytes_accessed=0, transcendentals=0)


def call_prefetch(kernel, grid, in_specs, out_specs, out_shape, args, us, scratch=()):
    return pl.pallas_call(
        kernel,
        grid_spec=pltpu.PrefetchScalarGridSpec(
            num_scalar_prefetch=1, grid=grid, in_specs=in_specs, out_specs=out_specs, scratch_shapes=list(scratch)
        ),
        out_shape=out_shape,
        compiler_params=pltpu.CompilerParams(vmem_limit_bytes=VMEM_LIMIT),
        cost_estimate=estimate(us),
    )(*args)


def call(kernel, grid, in_specs, out_specs, out_shape, args, us, scratch=(), aliases=None, limit=VMEM_LIMIT):
    return pl.pallas_call(
        kernel,
        grid=grid,
        input_output_aliases=aliases or {},
        in_specs=in_specs,
        out_specs=out_specs,
        out_shape=out_shape,
        scratch_shapes=list(scratch),
        compiler_params=pltpu.CompilerParams(vmem_limit_bytes=limit),
        cost_estimate=estimate(us),
    )(*args)


def whole(*shape):
    return pl.BlockSpec(shape, lambda g: (0,) * len(shape))


def part(*shape, base=0, flip=0):
    return pl.BlockSpec((None, *shape), lambda g: ((g + base) ^ flip,) + (0,) * len(shape))


def other(*shape):
    return pl.BlockSpec((None, *shape), lambda g: (jnp.maximum(g - 1, 0),) + (0,) * len(shape))


ANY_SPEC = pl.BlockSpec(memory_space=pl.ANY)


def struct(shape, dtype):
    return jax.ShapeDtypeStruct(shape, dtype)


def permute(array, axis, size, partner):
    return lax.ppermute(array, axis, [(i, partner(i)) for i in range(size)])


def first_partner(i):
    return i ^ (4 if i & 1 else 2)


def second_partner(i):
    return i ^ (2 if i & 1 else 4)


def core_partner(i):
    return i ^ 1


def after(array, *others):
    return lax.optimization_barrier((array, others))[0]


def gather_chips(piece, rows, *others):
    p1 = permute(piece, "rows", rows, first_partner)
    p2 = permute(piece, "rows", rows, second_partner)
    return [piece, p1, p2, permute(after(p1, *others), "rows", rows, second_partner)]


def gather_cores(own, rows):
    return own + [permute(p, "rows", rows, core_partner) for p in own]


def plane_gather(piece, rows):
    return gather_cores(gather_chips(piece, rows), rows)


def plane_slots(rank):
    me = rank & (PLANE - 1)
    core = rank & 1
    first = jnp.where(core == 1, 4, 2)
    second = jnp.where(core == 1, 2, 4)
    return [
        me,
        me ^ first,
        me ^ second,
        me ^ 6,
        me ^ 1,
        me ^ 1 ^ second,
        me ^ 1 ^ first,
        me ^ 7,
    ]


def to_levels(arrays):
    size = len(arrays) + 1
    return [permute(a, "heads", size, lambda i, m=m: i ^ m) for m, a in enumerate(arrays, 1)]


def sum_kernel(*refs):
    *ins, out = refs
    total = ins[0][...].astype(F32)
    for ref in ins[1:]:
        total = total + ref[...].astype(F32)
    out[...] = total.astype(BF)


def sums(*jobs):
    tail = jobs[0][0][0].shape[1:]
    zeros = (0,) * len(tail)
    counts = [len(job) for job in jobs]

    def kernel(*refs):
        base = 0
        for n, count in enumerate(counts):
            sum_kernel(*refs[base : base + count], refs[-1].at[n])
            base += count

    return call(
        kernel,
        (1,),
        [
            pl.BlockSpec((None, *tail), lambda g, slot=slot: (slot, *zeros)) for job in jobs for _, slot in job
        ],
        whole(len(jobs), *tail),
        struct((len(jobs), *tail), BF),
        [array for job in jobs for array, _ in job],
        us=2,
    )


class Reduction:
    def __init__(self, rows, together=True):
        self.rows = rows
        self.together = together
        self.kept, self.came = [], []

    def cores(self, sent, kept):
        self.kept.append(kept)
        self.came.append([permute(a, "rows", self.rows, core_partner) for a in sent])

    def near(self, n, slot):
        came = self.came[n]
        if len(came) == 1:
            return [(self.kept[n], slot), (came[0], slot)]
        return [(self.kept[n], slot), (came[slot], 0)]

    def second(self, *others):
        self.came = after(self.came, *others)
        jobs = [self.near(n, slot) for n in range(len(self.kept)) for slot in (2, 3)]
        sent = [sums(*jobs)] if self.together else [sums(job) for job in jobs]
        came = [permute(a, "rows", self.rows, second_partner) for a in sent]
        self.close = [(came[0], n) if self.together else (came[n], 0) for n in range(len(jobs))]
        return sent

    def first(self, *others):
        arrays = after([array for array, _ in self.close], *others)
        self.close = [(array, slot) for array, (_, slot) in zip(arrays, self.close)]
        sent = sums(*[[*self.near(n, 1), self.close[2 * n + 1]] for n in range(len(self.kept))])
        self.last = permute(sent, "rows", self.rows, first_partner)
        return sent

    def parts(self, *others):
        last = after(self.last, *others)
        mask = PLANE
        sets = range(len(self.kept))
        while mask < self.rows:
            total = sums(*[[*self.near(n, 0), self.close[2 * n], (last, n)] for n in sets])
            other = permute(total, "rows", self.rows, lambda i, m=mask: i ^ m)
            last = (last.astype(F32) + other.astype(F32)).astype(BF)
            mask *= 2
        return [[*self.near(n, 0), self.close[2 * n], (last, n)] for n in sets]


def total_kernel(sets, stacked, info_ref, *refs):
    outs = refs[4 * sets :]
    groups = refs[0].shape[0]
    base = 0
    for n in range(sets):
        arrays = refs[4 * n : 4 * n + 4]
        rows = arrays[0].shape[1]
        for k in range(groups):
            total = arrays[0][k].astype(F32)
            for array in arrays[1:]:
                total = total + array[k].astype(F32)
            if stacked:
                outs[0][info_ref[PLANE] ^ k, base : base + rows, :] = total.astype(BF)
            else:
                outs[k][base : base + rows, :] = total.astype(BF)
        base += rows


def totals(sets, info, stacked):
    heads, rows, cols = sets[0][0][0].shape[1:]
    specs = [
        pl.BlockSpec((None, heads, rows, cols), lambda g, slot=slot: (slot, 0, 0, 0))
        for pairs in sets
        for _, slot in pairs
    ]
    rows *= len(sets)
    shapes = [struct((heads, rows, cols), BF)] if stacked else [struct((rows, cols), BF)] * heads
    return call(
        functools.partial(total_kernel, len(sets), stacked),
        (1,),
        [SMEM_SPEC] + specs,
        [whole(*shape.shape) for shape in shapes],
        shapes,
        [info] + [array for pairs in sets for array, _ in pairs],
        us=2,
    )


def others_first(array, info):
    heads, *tail = array.shape

    def kernel(info_ref, in_ref, out_ref):
        for k in range(1, heads):
            out_ref[k - 1] = in_ref[info_ref[PLANE] ^ k]

    return call(
        kernel, (1,), [SMEM_SPEC, whole(heads, *tail)], whole(heads - 1, *tail),
        struct((heads - 1, *tail), array.dtype), (info, array), us=2,
    )


def to_heads(array):
    return lax.all_to_all(array, "heads", 0, 0, tiled=True)


def sum_arrays(arrays):
    return sums([(array[None], 0) for array in arrays])[0]


def sum_levels(array):
    return sums([(array, n) for n in range(array.shape[0])])[0]


SMEM_SPEC = pl.BlockSpec(memory_space=pltpu.SMEM)
VMEM_SPEC = pl.BlockSpec(memory_space=pltpu.VMEM)


def bias_rows(vectors, width):
    rest = jnp.stack([jnp.pad(v, (0, width - v.size)) for v in vectors])
    rows = []
    for _ in range(3):
        rounded = lax.reduce_precision(rest, 8, 7)
        rows.append(rounded.astype(BF))
        rest = rest - rounded
    rows = jnp.concatenate(rows, axis=0)
    return jnp.pad(rows, ((0, 16 - rows.shape[0]), (0, 0)))


def place_weights_kernel(count, parts, info_ref, *refs):
    owns = refs[:parts]
    pieces = refs[parts : parts + count]
    outs = refs[parts + count :]
    mine = pl.program_id(0) == 0

    @pl.when(mine)
    def _():
        for own, out in zip(owns, outs):
            out[...] = own[...]

    @pl.when(jnp.logical_not(mine))
    def _():
        base = 0
        for out in outs:
            if out.shape[0] < PLANE * 16:
                out[...] = pieces[0][base : base + out.shape[0], :]
                continue
            step = out.shape[0] // PLANE
            for n in range(count):
                start = pl.multiple_of(info_ref[n] * step, 16)
                out[pl.ds(start, step), :] = pieces[n][base : base + step, :]
            base += step


def place_weights(owns, pieces, info):
    count, parts = len(pieces), len(owns)
    others, _, cols = pieces[0].shape
    rows = sum(own.shape[0] if own.shape[0] < PLANE * 16 else own.shape[0] // PLANE for own in owns)

    def piece_index(g, info_ref):
        return (jnp.maximum(g - 1, 0), 0, 0)

    return pl.pallas_call(
        functools.partial(place_weights_kernel, count, parts),
        grid_spec=pltpu.PrefetchScalarGridSpec(
            num_scalar_prefetch=1,
            grid=(others + 1,),
            in_specs=[pl.BlockSpec(own.shape, lambda g, s: (0, 0)) for own in owns]
            + [pl.BlockSpec((None, rows, cols), piece_index)] * count,
            out_specs=[pl.BlockSpec((None, *own.shape), lambda g, s: (g, 0, 0)) for own in owns],
        ),
        out_shape=[struct((others + 1, *own.shape), BF) for own in owns],
        compiler_params=pltpu.CompilerParams(vmem_limit_bytes=VMEM_LIMIT),
        cost_estimate=estimate(3 * parts),
    )(info, *owns, *pieces)


def place_ffn_kernel(count, info_ref, *refs):
    up, down, turned = refs[count:]
    step = refs[0].shape[0] // 2
    for n in range(count):
        start = pl.multiple_of(info_ref[n] * step, 16)
        turned[pl.ds(start, step), :] = refs[n][:step, :].astype(F32)
        down[pl.ds(start, step), :] = refs[n][step:, :].astype(F32)
    up[...] = jnp.transpose(turned[...])


def place_ffn(pieces, info):
    rows, cols = pieces[0].shape
    count = len(pieces)
    hidden = count * rows // 2
    return pl.pallas_call(
        functools.partial(place_ffn_kernel, count),
        in_specs=[SMEM_SPEC] + [VMEM_SPEC] * count,
        out_specs=[VMEM_SPEC] * 2,
        out_shape=[struct((cols, hidden), F32), struct((hidden, cols), F32)],
        scratch_shapes=[pltpu.VMEM((hidden, cols), F32)],
        compiler_params=pltpu.CompilerParams(vmem_limit_bytes=VMEM_LIMIT),
        cost_estimate=estimate(4),
    )(info, *pieces)


def place_attention_kernel(count, cols, width, info_ref, *refs):
    out_qkv, out_o, out_b, vectors, bias = refs[count:]
    step = refs[0].shape[0] // 2
    for n in range(count):
        start = pl.multiple_of(info_ref[n] * step, 16)
        wide = refs[n][:step, :].astype(F32)

        @pl.when(start < cols)
        def _():
            out_qkv[pl.ds(start, step), :] = wide[:, :width]
            bias[pl.ds(start, step), :] = wide[:, width:]

        @pl.when(start >= cols)
        def _():
            out_o[pl.ds(pl.multiple_of(start - cols, 16), step), :] = wide[:, :width]

        @pl.when(start == cols)
        def _():
            groups = width // 128
            for v in range(vectors.shape[0]):
                for j in range(groups):
                    row = v * groups + j
                    vectors[v : v + 1, j * 128 : (j + 1) * 128] = wide[row : row + 1, width:]

        wide = refs[n][step:, :].astype(F32)
        out_qkv[pl.ds(cols + start, step), :] = wide[:, :width]
        bias[pl.ds(cols + start, step), :] = wide[:, width:]
    row = jnp.transpose(bias[...])[0:1, :]
    for j in range(3):
        out_b[j : j + 1, :] = row[:, j * cols : (j + 1) * cols]


def place_attention(pieces, info, cols, width):
    count = len(pieces)
    return pl.pallas_call(
        functools.partial(place_attention_kernel, count, cols, width),
        in_specs=[SMEM_SPEC] + [VMEM_SPEC] * count,
        out_specs=[VMEM_SPEC] * 4,
        out_shape=[
            struct((3 * cols, width), F32),
            struct((cols, width), F32),
            struct((3, cols), F32),
            struct((7, width), F32),
        ],
        scratch_shapes=[pltpu.VMEM((3 * cols, 128), F32)],
        compiler_params=pltpu.CompilerParams(vmem_limit_bytes=VMEM_LIMIT),
        cost_estimate=estimate(3),
    )(info, *pieces)


def head_sums(values, heads, hd):
    row = lax.broadcasted_iota(jnp.int32, (heads * hd, 128), 0)
    lane = lax.broadcasted_iota(jnp.int32, (heads * hd, 128), 1)
    own = ((row >= lane * hd) & (row < (lane + 1) * hd)).astype(F32).astype(BF)
    high = values.astype(BF)
    low = (values - high.astype(F32)).astype(BF)
    return dot(high, own) + dot(low, own)


def phi_of(raw, halves, head, feats, scale):
    part_raw = raw[:, head * feats : (head + 1) * feats]
    return jnp.exp(scale * part_raw - halves[:, head : head + 1]) * feats ** (-0.5)


def half_norms(vectors, heads, hd, scale):
    wide = vectors.astype(F32)
    return 0.5 * scale * scale * head_sums(wide * wide, heads, hd)


def edge_rows(first, last, head):
    lane = lax.broadcasted_iota(jnp.int32, (first.shape[0], 32), 1)
    return jnp.where(lane == head, first, 0.0) + jnp.where(lane == 16 + head, last, 0.0)


def edge_left(value, norm, first, last, head):
    return jnp.concatenate(
        [value * first, value * last, edge_rows(norm * first, norm * last, head)], axis=1
    ).astype(BF)


def edge_states(values, norms, phi, heads, hd, feats):
    first_values, last_values = values
    cols = heads * hd
    left = jnp.concatenate([first_values, last_values, norms], axis=1).astype(BF)
    state = dot_tn(left, phi)
    row = lax.broadcasted_iota(jnp.int32, (16, feats), 0)
    out = []
    for n in range(2):
        base = 2 * cols + 16 * n
        rows = [state[n * cols + h * hd : n * cols + (h + 1) * hd, h * feats : (h + 1) * feats] for h in range(heads)]
        total = jnp.zeros((16, feats), F32)
        for h in range(heads):
            total = jnp.where(row == h, state[base : base + 16, h * feats : (h + 1) * feats], total)
        out.append(jnp.concatenate([*rows, total], axis=0).astype(BF))
    return out


def put_edges(edge_ref, firsts, lasts, level, group):
    for m in range(1, edge_ref.shape[0]):
        place = level ^ m

        @pl.when(place > level)
        def _():
            edge_ref[place, group ^ m] = lasts

        @pl.when(place < level)
        def _():
            edge_ref[place, group ^ m] = firsts


def take_edges(came_ref, match_ref, level):
    left = right = None
    count = came_ref.shape[0] - 1
    for m in range(count):
        wide = came_ref[level ^ (m + 1)].astype(F32)
        a, b = wide * match_ref[m], wide * match_ref[count + m]
        left = a if left is None else left + a
        right = b if right is None else right + b
    return left.astype(BF), right.astype(BF)


def stack_edges(f, l, h, hd, cols):
    return jnp.concatenate(
        [f[h * hd : (h + 1) * hd], l[h * hd : (h + 1) * hd], f[cols:], l[cols:]], axis=0
    )


def with_one(value):
    lane = lax.broadcasted_iota(jnp.int32, value.shape, 1)
    return jnp.concatenate([value, jnp.where(lane == 0, 1.0, 0.0).astype(value.dtype)], axis=1)


def keys_kernel(heads, hd, feats, info_ref, x_ref, w_ref, b_ref, om_ref, ends_ref, *refs):
    *before, kv_ref, phi_ref, edge_ref = refs
    cols = heads * hd
    scale = hd ** (-0.25)
    kv = (dot_nt(x_ref[...], w_ref[...]) + b_ref[...]).astype(BF)
    kv_ref[...] = kv
    raw = dot(kv[:, :cols], om_ref[...])
    first, last = ends_ref[:, 0:1], ends_ref[:, 1:2]
    halves = half_norms(kv[:, :cols], heads, hd, scale)
    for h in range(heads):
        phi_ref[:, h * feats : (h + 1) * feats] = phi_of(raw, halves, h, feats, scale).astype(BF)
    values = kv[:, cols:].astype(F32)
    lane = lax.broadcasted_iota(jnp.int32, (kv.shape[0], 32), 1)
    firsts, lasts = edge_states(
        (values * first, values * last), jnp.where(lane < 16, first, last), phi_ref[...], heads, hd, feats
    )
    if not before:
        edge_ref[0] = firsts
        edge_ref[1] = lasts
        return
    group = pl.program_id(0) + 1
    put_edges(edge_ref, firsts, lasts, info_ref[PLANE], group)

    @pl.when(group == 1)
    def _():
        put_edges(edge_ref, before[-1][0], before[-1][1], info_ref[PLANE], 0)


def queries_kernel(heads, hd, feats, x_ref, w_ref, b_ref, om_ref, same_ref, kv_ref, phik_ref, *refs):
    q_ref, phi_ref, nd_ref = refs[-3:]
    cols = heads * hd
    scale = hd ** (-0.25)
    q = (dot_nt(x_ref[...], w_ref[:cols, :]) + b_ref[...]).astype(BF)
    q_ref[...] = q
    raw = dot(q, om_ref[...])
    same = same_ref[...]
    halves = half_norms(q, heads, hd, scale)
    for h in range(heads):
        phi = phi_of(raw, halves, h, feats, scale).astype(BF)
        phi_ref[:, h * feats : (h + 1) * feats] = phi
        scores = dot_nt(phi, phik_ref[:, h * feats : (h + 1) * feats]).astype(BF) * same
        value = kv_ref[:, cols + h * hd : cols + (h + 1) * hd]
        nd_ref[:, 2 * h * hd : 2 * (h + 1) * hd] = dot(scores, with_one(value))


def feature_back(dphi, phi, vectors, om, heads, hd, feats, scale):
    cols = heads * hd
    lows = []
    for h in range(heads):
        grad_raw = dphi[h] * phi[:, h * feats : (h + 1) * feats].astype(F32)
        lows.append((scale * grad_raw).astype(BF))
    through = dot_nt(jnp.concatenate(lows, axis=1), om)
    wide = vectors.astype(F32)
    lane = lax.broadcasted_iota(jnp.int32, wide.shape, 1)
    total = through[:, cols : cols + 1]
    for h in range(1, heads):
        total = jnp.where(lane >= h * hd, through[:, cols + h : cols + h + 1], total)
    return through[:, :cols] - scale * total * wide


def weight_grad(grad_ref, rows, left, right):
    width = right.shape[1]
    lane = lax.broadcasted_iota(jnp.int32, (left.shape[0], 128), 1)
    grad_ref[rows, :width] = dot_tn(left, right).astype(BF)
    grad_ref[rows, width:] = dot_tn(left, jnp.where(lane == 0, 1.0, 0.0).astype(BF)).astype(BF)


def put_slices(source_ref, base, sent_refs, kept_ref, info_ref, placed=True):
    step = source_ref.shape[0] // PLANE
    half = PLANE // 2
    for n in range(PLANE):
        if n < half:
            out = kept_ref.at[n]
        else:
            out = sent_refs[n - half] if len(sent_refs) > 1 else sent_refs[0].at[n - half]
        start = pl.multiple_of(jnp.where(placed, info_ref[n], n) * step, 16)
        out[base : base + step, :] = source_ref[pl.ds(start, step), :]


def queries_back_kernel(
    heads, hd, feats, info_ref, dnd_ref, q_ref, phiq_ref, kv_ref, phik_ref, cf_ref, cl_ref, om_ref, same_ref,
    ends_ref, att_ref, x_ref, one_ref, one_sums_ref, two_sums_ref, bup_ref, dq_ref, dphik_ref, dv_ref, sent_ref, kept_ref,
    grad_ref,
):
    cols = heads * hd
    scale = hd ** (-0.25)
    first, last = ends_ref[:, 0:1], ends_ref[:, 1:2]
    same = same_ref[...]
    dphis, dvs = [], []
    for h in range(heads):
        phiq = phiq_ref[:, h * feats : (h + 1) * feats]
        phik = phik_ref[:, h * feats : (h + 1) * feats]
        value = with_one(kv_ref[:, cols + h * hd : cols + (h + 1) * hd])
        dnd = dnd_ref[:, 2 * h * hd : 2 * (h + 1) * hd]
        dscore = dot_nt(dnd, value).astype(BF) * same
        wide = dnd.astype(F32)
        left = edge_left(wide[:, :hd], wide[:, hd : hd + 1], first, last, h)
        stack = stack_edges(cf_ref[...], cl_ref[...], h, hd, cols)
        dphis.append(dot(dscore, phik) + dot(left, stack))
        dscore_t = dot_nt(value, dnd).astype(BF) * same
        score_t = dot_nt(phik, phiq).astype(BF) * same
        dphik_ref[:, h * feats : (h + 1) * feats] = dot(dscore_t, phiq).astype(BF)
        dvs.append(dot(score_t, dnd)[:, :hd])
    dv_ref[...] = jnp.concatenate(dvs, axis=1)
    dq = feature_back(dphis, phiq_ref[...], q_ref[...], om_ref[...], heads, hd, feats, scale)
    dq = dq.astype(BF)
    dq_ref[...] = dq
    weight_grad(grad_ref, slice(0, cols), dq, x_ref[...])
    width = one_ref.shape[1]
    vectors = [one_sums_ref[n : n + 1, :] for n in range(3)] + [two_sums_ref[n : n + 1, :] for n in range(3)]
    vectors = vectors + [bup_ref[...]]
    block = [v[:, n : n + 128] for v in vectors for n in range(0, width, 128)]
    step = grad_ref.shape[0] // PLANE
    block.append(jnp.zeros((step - len(block), 128), F32))
    block = jnp.concatenate(block, axis=0).astype(BF)
    grad_ref[cols:, :width] = dot_tn(att_ref[...], one_ref[...]).astype(BF)
    for n in range(cols, 2 * cols, step):
        grad_ref[n : n + step, width:] = block
    put_slices(grad_ref, 0, [sent_ref], kept_ref, info_ref)


def keys_back_kernel(
    heads, hd, feats, info_ref, match_ref, kv_ref, phik_ref, dphik_ref, dv_ref, came_ref, om_ref, ends_ref, x_ref, *refs
):
    dkv_ref, *sent, kept_ref, grad_ref = refs
    cols = heads * hd
    scale = hd ** (-0.25)
    first, last = ends_ref[:, 0:1], ends_ref[:, 1:2]
    rf, rl = take_edges(came_ref, match_ref, info_ref[PLANE])
    dphis, dvs = [], []
    for h in range(heads):
        phik = phik_ref[:, h * feats : (h + 1) * feats]
        value = kv_ref[:, cols + h * hd : cols + (h + 1) * hd].astype(F32)
        stack = stack_edges(rf, rl, h, hd, cols)
        dphis.append(
            dphik_ref[:, h * feats : (h + 1) * feats].astype(F32) + dot(edge_left(value, 1.0, first, last, h), stack)
        )
        far = dot_nt(phik, stack[: 2 * hd])
        dvs.append(dv_ref[:, h * hd : (h + 1) * hd] + first * far[:, :hd] + last * far[:, hd:])
    dk = feature_back(dphis, phik_ref[...], kv_ref[:, :cols], om_ref[...], heads, hd, feats, scale)
    dkv = jnp.concatenate([dk] + dvs, axis=1).astype(BF)
    dkv_ref[...] = dkv
    weight_grad(grad_ref, slice(0, 2 * cols), dkv, x_ref[...])
    put_slices(grad_ref, 0, sent, kept_ref, info_ref)


def tokens_kernel(cols, dq_ref, dkv_ref, qo_ref, kv_ref, one_ref, out_ref):
    back = dot(dq_ref[...], qo_ref[:cols, :]) + dot(dkv_ref[...], kv_ref[...])

    @pl.when(pl.program_id(0) == 0)
    def _():
        out_ref[...] = one_ref[...] + back

    @pl.when(pl.program_id(0) > 0)
    def _():
        out_ref[...] += back


def norm_of(hidden):
    average = jnp.mean(hidden, axis=-1, keepdims=True)
    centred = hidden - average
    inverse = lax.rsqrt(jnp.mean(centred * centred, axis=-1, keepdims=True) + EPSILON)
    return centred * inverse, inverse


def norm_back(grad_in, normed, inverse, gain):
    scaled = grad_in * gain
    centred = (
        scaled
        - jnp.mean(scaled, axis=-1, keepdims=True)
        - normed * jnp.mean(scaled * normed, axis=-1, keepdims=True)
    )
    return centred * inverse


def column_sums(arrays, rows):
    sums = [jnp.sum(a, axis=0, keepdims=True) for a in arrays]
    return jnp.concatenate(sums + [jnp.zeros((rows - len(sums), sums[0].shape[1]), F32)], axis=0)


def gelu_both(v):
    gate = 0.5 + 0.5 * lax.erf(v * 0.5**0.5)
    bell = jnp.exp(-0.5 * v * v) * (2.0 * jnp.pi) ** (-0.5)
    return v * gate, gate + v * bell


def ffn_copies(own_up, own_down, pieces, up_ref, down_ref, sems, k):
    if k == 0:
        return [
            pltpu.make_async_copy(own_up, up_ref.at[0], sems.at[0, 0]),
            pltpu.make_async_copy(own_down, down_ref.at[0], sems.at[0, 1]),
        ]
    step = up_ref.shape[1] // PLANE
    base = pieces[0].shape[1] - 2 * step
    copies = []
    for n, piece in enumerate(pieces):
        for part_n, ref in enumerate((up_ref, down_ref)):
            copies.append(
                pltpu.make_async_copy(
                    piece.at[k - 1, pl.ds(base + part_n * step, step)],
                    ref.at[k, pl.ds(n * step, step)],
                    sems.at[k, 2 * n + part_n],
                )
            )
    return copies


def middle_kernel(heads, hd, feats, info_ref, match_ref, phi_ref, nd_ref, came_ref, ends_ref, wo_ref, x_ref, vec_ref, bup_ref, cot_ref, *refs):
    own_up, own_down, *pieces = refs[: 2 + PLANE]
    (
        att_ref, cf_ref, cl_ref, out_ref, gradb_ref, one_out, onelow_ref, sums1_ref, sums2_ref, dnd_ref, edge_ref,
        sent1_ref, sent2_ref, sent3_ref, sent4_ref, kept_ref,
        acc, first_low, normed_one, inverse_one, act_s, slope_s, two, two_low, att_s, den_s, up_s, down_s, grad_s, sems,
    ) = refs[2 + PLANE :]
    sent = [sent1_ref, sent2_ref, sent3_ref, sent4_ref]
    groups = att_s.shape[0]
    stage = pl.program_id(0) // groups
    g = pl.program_id(0) % groups
    cols = heads * hd
    t = acc.shape[0]
    level = info_ref[PLANE]
    final = g == groups - 1

    @pl.when(pl.program_id(0) == 0)
    def _():
        for k in range(groups):
            for copy in ffn_copies(own_up, own_down, pieces, up_s, down_s, sems, k):
                copy.start()

    def first_add(value, start):
        @pl.when(g == 0)
        def _():
            acc[...] = start() + value

        @pl.when(g > 0)
        def _():
            acc[...] += value

    @pl.when(stage == 0)
    def _():
        first, last = ends_ref[:, 0:1], ends_ref[:, 1:2]
        cf, cl = take_edges(came_ref, match_ref, level)
        cf_ref[...] = cf
        cl_ref[...] = cl
        lane = lax.broadcasted_iota(jnp.int32, (t, 128), 1)
        dens = jnp.zeros((t, 128), F32)
        outs = []
        for h in range(heads):
            far = dot_nt(phi_ref[:, h * feats : (h + 1) * feats], stack_edges(cf, cl, h, hd, cols))
            nd = nd_ref[:, 2 * h * hd : 2 * (h + 1) * hd]
            num = nd[:, :hd] + first * far[:, :hd] + last * far[:, hd : 2 * hd]
            den = (
                nd[:, hd : hd + 1]
                + first * far[:, 2 * hd + h : 2 * hd + h + 1]
                + last * far[:, 2 * hd + 16 + h : 2 * hd + 17 + h]
            )
            outs.append(num / den)
            dens = dens + jnp.where(lane == h, den, 0.0)
        att = jnp.concatenate(outs, axis=1).astype(BF)
        att_ref[...] = att
        att_s[g] = att
        den_s[g] = dens
        first_add(dot(att, wo_ref[...]), lambda: x_ref[...].astype(F32) + vec_ref[0:1, :])

        @pl.when(final)
        def _():
            normed, inverse = norm_of(acc[...])
            normed_one[...] = normed
            inverse_one[...] = jnp.broadcast_to(inverse, inverse_one.shape)
            first_low[...] = (normed * vec_ref[1:2, :] + vec_ref[2:3, :]).astype(BF)

    @pl.when(stage == 1)
    def _():
        for k in range(groups):

            @pl.when(g == k)
            def _():
                for copy in ffn_copies(own_up, own_down, pieces, up_s, down_s, sems, k):
                    copy.wait()

        act, slope = gelu_both(dot_nt(first_low[...], up_s[g]) + bup_ref[...])
        act = act.astype(BF)
        act_s[g] = act
        slope_s[g] = slope.astype(BF)
        first_add(
            dot(act, down_s[g]),
            lambda: normed_one[...] * vec_ref[1:2, :] + vec_ref[2:3, :] + vec_ref[3:4, :],
        )

        @pl.when(final)
        def _():
            normed, inverse = norm_of(acc[...])
            gain = vec_ref[4:5, :]
            out_ref[...] = (normed * gain + vec_ref[5:6, :]).astype(BF)
            grad_in = cot_ref[...].astype(F32)
            grad = norm_back(grad_in, normed, inverse, gain)
            two[...] = grad
            two_low[...] = grad.astype(BF)
            sums2_ref[...] = column_sums([grad_in * normed, grad_in, grad], 8)

    @pl.when(stage == 2)
    def _():
        step = up_s.shape[1] // PLANE
        low = two_low[...]
        dpre = dot_nt(low, down_s[g]) * slope_s[g].astype(F32)
        gradb_ref[...] = jnp.sum(dpre, axis=0, keepdims=True)
        pre_low = dpre.astype(BF)
        grad_s[...] = dot_tn(pre_low, first_low[...]).astype(BF)
        put_slices(grad_s, 0, sent, kept_ref, info_ref, g == 0)
        grad_s[...] = dot_tn(act_s[g], low).astype(BF)
        put_slices(grad_s, step, sent, kept_ref, info_ref, g == 0)
        first_add(dot(pre_low, up_s[g]), lambda: two[...])

        @pl.when(final)
        def _():
            grad_in = acc[...]
            normed = normed_one[...]
            one = norm_back(grad_in, normed, inverse_one[:, 0:1], vec_ref[1:2, :])
            one_out[...] = one
            onelow_ref[...] = one.astype(BF)
            sums1_ref[...] = column_sums([grad_in * normed, grad_in, one], 8)

    @pl.when(stage == 3)
    def _():
        first, last = ends_ref[:, 0:1], ends_ref[:, 1:2]
        datt = dot_nt(onelow_ref[...], wo_ref[...])
        dens = den_s[g]
        lane = lax.broadcasted_iota(jnp.int32, (t, cols), 1)
        den = dens[:, 0:1]
        for h in range(1, heads):
            den = jnp.where(lane >= h * hd, dens[:, h : h + 1], den)
        dnum = datt / den
        dden = -head_sums(dnum * att_s[g].astype(F32), heads, hd)
        one_lane = lax.broadcasted_iota(jnp.int32, (t, hd), 1) == 0
        for h in range(heads):
            dnd_ref[:, 2 * h * hd : 2 * (h + 1) * hd] = jnp.concatenate(
                [dnum[:, h * hd : (h + 1) * hd], jnp.where(one_lane, dden[:, h : h + 1], 0.0)], axis=1
            ).astype(BF)
        norms = jnp.concatenate([dden[:, :16] * first, dden[:, :16] * last], axis=1)
        firsts, lasts = edge_states((dnum * first, dnum * last), norms, phi_ref[...], heads, hd, feats)
        put_edges(edge_ref, firsts, lasts, level, g)


def body(
    rows, heads,
    tokens, segment_ids, w_qkv, b_qkv, w_out, b_out, gain_one, bias_one, w_up, b_up, w_down, b_down,
    gain_two, bias_two, omega, cotangent,
):
    rank = lax.axis_index("rows")
    level = lax.axis_index("heads")
    hd, feats = omega.shape
    _, length, width = tokens.shape
    cols = w_qkv.shape[2]
    nh = cols // hd
    hidden = w_up.shape[1]
    slots = plane_slots(rank)
    me = slots[0]
    info = jnp.stack(slots + [level]).astype(jnp.int32)
    x = tokens[0]

    def slice_of(array):
        step = array.shape[0] // PLANE
        return lax.dynamic_slice_in_dim(array, me * step, step, 0)

    def from_levels(piece):
        return to_levels([piece] * (heads - 1))

    wt = jnp.transpose(w_qkv, (1, 2, 0)).reshape(3 * cols, width)
    own_kv = wt[cols:]
    own_bias = bias_rows([b_qkv.reshape(-1), b_up], width)
    own_qo = jnp.concatenate([wt[:cols], w_out], axis=0)
    own_up = w_up.T
    rows_of = 2 * cols // PLANE
    kv_slice = lax.dynamic_slice_in_dim(wt, cols + me * rows_of, rows_of, 0)
    q_slice = lax.dynamic_slice_in_dim(wt, jnp.minimum(me, PLANE // 2 - 1) * rows_of, rows_of, 0)
    o_slice = lax.dynamic_slice_in_dim(w_out, jnp.maximum(me - PLANE // 2, 0) * rows_of, rows_of, 0)
    qo_slice = jnp.where(me < PLANE // 2, q_slice, o_slice)
    near = from_levels(jnp.concatenate([kv_slice, qo_slice, own_bias], axis=0))
    rest = jnp.concatenate([slice_of(own_up), slice_of(w_down)], axis=0)
    rest = jnp.broadcast_to(rest[None], (heads, *rest.shape))
    own_bias_qkv = b_qkv.reshape(1, -1)

    segments = lax.dynamic_slice_in_dim(segment_ids[0], level * length, length, 0)
    by_level = segment_ids[0].reshape(heads, length)
    firsts, lasts = by_level[:, 0], by_level[:, -1]
    my_first, my_last = segments[0], segments[-1]
    ends = jnp.stack([segments == my_first, segments == my_last], axis=1).astype(F32)
    same = (segments[:, None] == segments[None, :]).astype(BF)
    index = jnp.arange(1, heads) ^ level
    there = index[:, None] == jnp.arange(heads)[None, :]
    index_first = jnp.sum(jnp.where(there, firsts[None], 0), axis=1)
    index_last = jnp.sum(jnp.where(there, lasts[None], 0), axis=1)
    match = jnp.concatenate(
        [(index < level) & (index_last == my_first), (index > level) & (index_first == my_last)]
    ).astype(F32)

    eye = jnp.eye(nh, dtype=BF)
    om = (eye[:, None, :, None] * omega[None, :, None, :]).reshape(cols, nh * feats)
    om_back = jnp.concatenate(
        [om, jnp.repeat(eye, feats, axis=1), jnp.zeros((16 - nh, nh * feats), BF)], axis=0
    )
    edge = cols + 16
    dims = (nh, hd, feats)
    t = length
    aug = width + 128

    half = PLANE // 2
    edge_shape = struct((heads, heads, edge, feats), BF)
    edge_spec = pl.BlockSpec((heads, None, edge, feats), lambda g: (0, g, 0, 0))

    def slot_spec(count, wide):
        return pl.BlockSpec((half, None, count, wide), lambda g: (0, g, 0, 0))

    def slot_shape(count, wide):
        return struct((half, heads, count, wide), BF)

    def of_groups(base, *shape):
        return part(*shape, base=base) if base else whole(*shape)

    def keys(base, count, weights, bias, *before):
        return call(
            functools.partial(keys_kernel, *dims),
            (count,),
            [
                SMEM_SPEC, whole(t, width), of_groups(base, 2 * cols, width), of_groups(base, 1, 2 * cols),
                whole(cols, nh * feats), whole(t, 2),
            ]
            + [ANY_SPEC, ANY_SPEC, whole(2, edge, feats)][: len(before)],
            [
                part(t, 2 * cols, base=base),
                part(t, nh * feats, base=base),
                whole(*edge_shape.shape) if base else whole(2, edge, feats),
            ],
            [
                struct((heads, t, 2 * cols), BF),
                struct((heads, t, nh * feats), BF),
                edge_shape if base else struct((2, edge, feats), BF),
            ],
            (info, x, weights, bias, om, ends, *before),
            us=3 * count,
            aliases={6: 0, 7: 1} if base else None,
        )

    def queries(base, count, weights, bias, kv, phi_k, *before):
        return call(
            functools.partial(queries_kernel, *dims),
            (count,),
            [
                whole(t, width), of_groups(base, 2 * cols, width), of_groups(base, 1, cols),
                whole(cols, nh * feats), whole(t, t),
                part(t, 2 * cols, base=base), part(t, nh * feats, base=base),
            ]
            + [ANY_SPEC] * len(before),
            [
                part(t, cols, base=base), part(t, nh * feats, base=base), part(t, 2 * cols, base=base),
            ],
            [
                struct((heads, t, cols), BF),
                struct((heads, t, nh * feats), BF),
                struct((heads, t, 2 * cols), F32),
            ],
            (x, weights, bias, om, same, kv, phi_k, *before),
            us=3 * count,
            aliases={7 + n: n for n in range(len(before))},
        )

    near_rest = to_heads(after(rest, near))
    near = jnp.stack(near)
    p1 = permute(near, "rows", rows, first_partner)
    p2 = permute(near, "rows", rows, second_partner)
    own_keys = keys(0, 1, after(own_kv, near), own_bias_qkv[:, cols:])
    p3 = permute(p1, "rows", rows, second_partner)
    own_queries = queries(0, 1, after(own_qo, p1), own_bias_qkv[:, :cols], *own_keys[:2])
    pieces = gather_cores([near, p1, p2, after(p3, own_queries)], rows)
    kv_w, qo_w, bias = place_weights([own_kv, own_qo, own_bias], pieces, info)
    bias = bias.astype(F32)
    bias = bias[:, 0:2] + (bias[:, 2:4] + bias[:, 4:6])
    bias_qkv = bias[:, 0:1, : 3 * cols]
    bias_q = bias_qkv[:, :, :cols]
    bias_kv = bias_qkv[:, :, cols:]
    at_slot = (jnp.stack(slots)[:, None] == jnp.arange(PLANE)[None, :])[None, :, :, None]
    by_slice = bias[1:, 1, :hidden].reshape(heads - 1, 1, PLANE, hidden // PLANE)
    by_slot = jnp.sum(jnp.where(at_slot, by_slice, 0.0), axis=2).reshape(heads - 1, 1, hidden)
    bias_up = jnp.concatenate([b_up[None, None], by_slot], axis=0)

    own_keys = after(own_keys, own_queries)
    kv, phi_k, edges = keys(1, heads - 1, kv_w, bias_kv, *own_keys)
    came = to_heads(edges)
    q, phi_q, local = queries(1, heads - 1, qo_w, bias_q, kv, phi_k, *own_queries)
    chips_ffn = gather_chips(others_first(after(near_rest, edges), info), rows)
    rest_w = gather_cores(after(chips_ffn, phi_q), rows)
    step = hidden // PLANE
    vec = jnp.pad(
        jnp.stack([b_out, gain_one, bias_one, b_down, gain_two, bias_two]), ((0, 2), (0, 0))
    )

    def staged(shape, *stages, at=0):
        def index(s):
            stage, g = s // heads, s % heads
            group = jnp.where(stage > stages[-1], heads - 1, 0)
            for n in stages:
                group = jnp.where(stage == n, g, group)
            if len(stages) == 2:
                between = (stage > stages[0]) & (stage < stages[1])
                group = jnp.where(between, heads - 1, group)
            return (group, at, 0)

        return pl.BlockSpec((None, *shape), lambda s: index(s))

    def staged_slots(shape, stage):
        spec = staged((1, 1), stage)
        return pl.BlockSpec((shape[0], None, *shape[1:]), lambda s: (0, spec.index_map(s)[0], 0, 0))

    tokens_bf, tokens_f32 = struct((t, width), BF), struct((t, width), F32)
    (
        att, far_f, far_l, layer_output, grad_b_up, grad_one, one_low, sums_one, sums_two, dnd, edges, *sent, kept,
    ) = call(
        functools.partial(middle_kernel, *dims),
        (4 * heads,),
        [
            SMEM_SPEC, SMEM_SPEC, staged((t, nh * feats), 0, 3), staged((t, 2 * cols), 0),
            staged_slots((heads, edge, feats), 0), whole(t, 2), staged((cols, width), 0, 3, at=1), whole(t, width),
            whole(8, width), staged((1, hidden), 1), whole(t, width), *[ANY_SPEC] * (2 + PLANE),
        ],
        [
            staged((t, cols), 0), staged((edge, feats), 0), staged((edge, feats), 0), whole(t, width),
            staged((1, hidden), 2), whole(t, width), whole(t, width), whole(8, width), whole(8, width),
            staged((t, 2 * cols), 3), whole(*edge_shape.shape), *[staged((2 * step, width), 2)] * half,
            staged_slots((half, 2 * step, width), 2),
        ],
        [
            struct((heads, t, cols), BF),
            struct((heads, edge, feats), BF),
            struct((heads, edge, feats), BF),
            tokens_bf,
            struct((heads, 1, hidden), F32),
            tokens_f32,
            tokens_bf,
            struct((8, width), F32),
            struct((8, width), F32),
            struct((heads, t, 2 * cols), BF),
            edge_shape,
            *[struct((heads, 2 * step, width), BF)] * half,
            slot_shape(2 * step, width),
        ],
        (
            info, match, phi_q, local, came, ends, qo_w, x, vec, bias_up, cotangent[0], own_up, w_down, *rest_w,
        ),
        us=50,
        scratch=[
            pltpu.VMEM((t, width), F32),
            pltpu.VMEM((t, width), BF),
            pltpu.VMEM((t, width), F32),
            pltpu.VMEM((t, 128), F32),
            pltpu.VMEM((heads, t, hidden), BF),
            pltpu.VMEM((heads, t, hidden), BF),
            pltpu.VMEM((t, width), F32),
            pltpu.VMEM((t, width), BF),
            pltpu.VMEM((heads, t, cols), BF),
            pltpu.VMEM((heads, t, 128), F32),
            pltpu.VMEM((heads, hidden, width), BF),
            pltpu.VMEM((heads, hidden, width), BF),
            pltpu.VMEM((hidden, width), BF),
            pltpu.SemaphoreType.DMA((heads, 2 * PLANE)),
        ],
        limit=60 * 1024 * 1024,
    )
    by_slot = grad_b_up[1:, 0].reshape(heads - 1, PLANE, 1, step)
    by_slice = jnp.sum(jnp.where(at_slot, by_slot, 0.0), axis=1).reshape(heads - 1, 1, hidden)
    grad_b_up = jnp.concatenate([grad_b_up[:1], by_slice], axis=0)

    back = to_heads(edges)
    ffn = Reduction(rows, together=False)
    ffn.cores([a[None] for a in sent], kept)
    ffn_sent = ffn.second()
    slice_rows = 2 * cols // PLANE
    dq, dphi_k, dv, *qo = call(
        functools.partial(queries_back_kernel, *dims),
        (heads,),
        [
            SMEM_SPEC, part(t, 2 * cols), part(t, cols), part(t, nh * feats), part(t, 2 * cols),
            part(t, nh * feats), part(edge, feats), part(edge, feats), whole(cols + 16, nh * feats), whole(t, t),
            whole(t, 2), part(t, cols), whole(t, width), whole(t, width), whole(8, width),
            whole(8, width), part(1, hidden),
        ],
        [
            part(t, cols), part(t, nh * feats), part(t, cols), *[slot_spec(slice_rows, aug)] * 2,
        ],
        [
            struct((heads, t, cols), BF),
            struct((heads, t, nh * feats), BF),
            struct((heads, t, cols), F32),
            *[slot_shape(slice_rows, aug)] * 2,
        ],
        (
            info, after(dnd, ffn_sent), q, phi_q, kv, phi_k, far_f, far_l, om_back, same, ends, att, x, one_low,
            sums_one, sums_two, grad_b_up,
        ),
        us=20,
        scratch=[pltpu.VMEM((2 * cols, aug), BF)],
    )
    red = Reduction(rows)
    red.cores(qo[:1], qo[1])
    back = after(back, ffn.first(dv))
    dkv, *kv_red = call(
        functools.partial(keys_back_kernel, *dims),
        (heads,),
        [
            SMEM_SPEC, SMEM_SPEC, part(t, 2 * cols), part(t, nh * feats), part(t, nh * feats), part(t, cols),
            edge_spec, whole(cols + 16, nh * feats), whole(t, 2), whole(t, width),
        ],
        [part(t, 2 * cols), *[part(slice_rows, aug)] * half, slot_spec(slice_rows, aug)],
        [
            struct((heads, t, 2 * cols), BF),
            *[struct((heads, slice_rows, aug), BF)] * half,
            slot_shape(slice_rows, aug),
        ],
        (info, match, kv, phi_k, dphi_k, dv, back, om_back, ends, x),
        us=12,
        scratch=[pltpu.VMEM((2 * cols, aug), BF)],
    )
    red.cores([a[None] for a in kv_red[:half]], kv_red[half])
    sent = red.second(dkv, ffn.last)
    (ffn_total,) = totals(ffn.parts(sent), info, True)
    grad_tokens = call(
        functools.partial(tokens_kernel, cols),
        (heads,),
        [part(t, cols), part(t, 2 * cols), part(2 * cols, width), part(2 * cols, width), whole(t, width)],
        whole(t, width),
        tokens_f32,
        (dq, after(dkv, ffn_total), qo_w, kv_w, grad_one),
        us=5,
    )
    sent = red.first(grad_tokens)
    ffn_pieces = plane_gather(sum_levels(after(to_heads(ffn_total), sent)), rows)
    own_total, *total = totals(red.parts(), info, False)
    out_up, out_down = place_ffn(ffn_pieces, info)
    chips = gather_chips(sum_arrays([own_total, *to_levels(total)]), rows)
    pieces = gather_cores(after(chips, out_up), rows)

    out_qkv, out_o, out_b, outs = place_attention(pieces, info, cols, width)
    out_qkv = jnp.transpose(out_qkv.reshape(3, cols, width), (2, 0, 1))
    return (
        layer_output[None],
        grad_tokens[None],
        out_qkv,
        out_b,
        out_o,
        outs[2],
        outs[0],
        outs[1],
        out_up,
        outs[6],
        out_down,
        outs[5],
        outs[3],
        outs[4],
    )


def solution(mesh):
    return jax.shard_map(
        functools.partial(body, mesh.shape["rows"], mesh.shape["heads"]),
        mesh=mesh,
        in_specs=(
            P("rows", "heads", None),
            P("rows", None),
            P(None, None, "heads"),
            P(None, "heads"),
            P("heads", None),
            P(),
            P(),
            P(),
            P(None, "heads"),
            P("heads"),
            P("heads", None),
            P(),
            P(),
            P(),
            P(),
            P("rows", "heads", None),
        ),
        out_specs=(
            P("rows", "heads", None),
            P("rows", "heads", None),
            P(None, None, "heads"),
            P(None, "heads"),
            P("heads", None),
            P(),
            P(),
            P(),
            P(None, "heads"),
            P("heads"),
            P("heads", None),
            P(),
            P(),
            P(),
        ),
        check_vma=False,
    )
```

```python
import functools

import jax
import jax.numpy as jnp
from jax import lax
from jax.experimental import pallas as pl
from jax.experimental.pallas import tpu as pltpu
from jax.sharding import PartitionSpec as P

EPSILON = 1e-05
PLANE = 8
VMEM_LIMIT = 48 * 1024 * 1024
BF = jnp.bfloat16
F32 = jnp.float32


def dot(a, b, dims=((1,), (0,))):
    return lax.dot_general(a, b, (dims, ((), ())), preferred_element_type=F32)


def dot_nt(a, b):
    return dot(a, b, ((1,), (1,)))


def dot_tn(a, b):
    return dot(a, b, ((0,), (0,)))


def estimate(us):
    return pl.CostEstimate(flops=int(us * 1e3), bytes_accessed=0, transcendentals=0)


def call_prefetch(kernel, grid, in_specs, out_specs, out_shape, args, us, scratch=()):
    return pl.pallas_call(
        kernel,
        grid_spec=pltpu.PrefetchScalarGridSpec(
            num_scalar_prefetch=1, grid=grid, in_specs=in_specs, out_specs=out_specs, scratch_shapes=list(scratch)
        ),
        out_shape=out_shape,
        compiler_params=pltpu.CompilerParams(vmem_limit_bytes=VMEM_LIMIT),
        cost_estimate=estimate(us),
    )(*args)


def call(kernel, grid, in_specs, out_specs, out_shape, args, us, scratch=(), aliases=None, limit=VMEM_LIMIT):
    return pl.pallas_call(
        kernel,
        grid=grid,
        input_output_aliases=aliases or {},
        in_specs=in_specs,
        out_specs=out_specs,
        out_shape=out_shape,
        scratch_shapes=list(scratch),
        compiler_params=pltpu.CompilerParams(vmem_limit_bytes=limit),
        cost_estimate=estimate(us),
    )(*args)


def whole(*shape):
    return pl.BlockSpec(shape, lambda g: (0,) * len(shape))


def part(*shape, base=0, flip=0):
    return pl.BlockSpec((None, *shape), lambda g: ((g + base) ^ flip,) + (0,) * len(shape))


def other(*shape):
    return pl.BlockSpec((None, *shape), lambda g: (jnp.maximum(g - 1, 0),) + (0,) * len(shape))


ANY_SPEC = pl.BlockSpec(memory_space=pl.ANY)


def struct(shape, dtype):
    return jax.ShapeDtypeStruct(shape, dtype)


def permute(array, axis, size, partner):
    return lax.ppermute(array, axis, [(i, partner(i)) for i in range(size)])


def first_partner(i):
    return i ^ (4 if i & 1 else 2)


def second_partner(i):
    return i ^ (2 if i & 1 else 4)


def core_partner(i):
    return i ^ 1


def after(array, *others):
    return lax.optimization_barrier((array, others))[0]


def gather_chips(piece, rows, *others):
    p1 = permute(piece, "rows", rows, first_partner)
    p2 = permute(piece, "rows", rows, second_partner)
    return [piece, p1, p2, permute(after(p1, *others), "rows", rows, second_partner)]


def gather_cores(own, rows):
    return own + [permute(p, "rows", rows, core_partner) for p in own]


def plane_gather(piece, rows):
    return gather_cores(gather_chips(piece, rows), rows)


def plane_slots(rank):
    me = rank & (PLANE - 1)
    core = rank & 1
    first = jnp.where(core == 1, 4, 2)
    second = jnp.where(core == 1, 2, 4)
    return [
        me,
        me ^ first,
        me ^ second,
        me ^ 6,
        me ^ 1,
        me ^ 1 ^ second,
        me ^ 1 ^ first,
        me ^ 7,
    ]


def to_levels(arrays):
    size = len(arrays) + 1
    return [permute(a, "heads", size, lambda i, m=m: i ^ m) for m, a in enumerate(arrays, 1)]


def sum_kernel(*refs):
    *ins, out = refs
    total = ins[0][...].astype(F32)
    for ref in ins[1:]:
        total = total + ref[...].astype(F32)
    out[...] = total.astype(BF)


def sums(*jobs):
    tail = jobs[0][0][0].shape[1:]
    zeros = (0,) * len(tail)
    counts = [len(job) for job in jobs]

    def kernel(*refs):
        base = 0
        for n, count in enumerate(counts):
            sum_kernel(*refs[base : base + count], refs[-1].at[n])
            base += count

    return call(
        kernel,
        (1,),
        [
            pl.BlockSpec((None, *tail), lambda g, slot=slot: (slot, *zeros)) for job in jobs for _, slot in job
        ],
        whole(len(jobs), *tail),
        struct((len(jobs), *tail), BF),
        [array for job in jobs for array, _ in job],
        us=2,
    )


class Reduction:
    def __init__(self, rows, together=True):
        self.rows = rows
        self.together = together
        self.kept, self.came = [], []

    def cores(self, sent, kept):
        self.kept.append(kept)
        self.came.append([permute(a, "rows", self.rows, core_partner) for a in sent])

    def near(self, n, slot):
        came = self.came[n]
        if len(came) == 1:
            return [(self.kept[n], slot), (came[0], slot)]
        return [(self.kept[n], slot), (came[slot], 0)]

    def second(self, *others):
        self.came = after(self.came, *others)
        jobs = [self.near(n, slot) for n in range(len(self.kept)) for slot in (2, 3)]
        sent = [sums(*jobs)] if self.together else [sums(job) for job in jobs]
        came = [permute(a, "rows", self.rows, second_partner) for a in sent]
        self.close = [(came[0], n) if self.together else (came[n], 0) for n in range(len(jobs))]
        return sent

    def first(self, *others):
        arrays = after([array for array, _ in self.close], *others)
        self.close = [(array, slot) for array, (_, slot) in zip(arrays, self.close)]
        sent = sums(*[[*self.near(n, 1), self.close[2 * n + 1]] for n in range(len(self.kept))])
        self.last = permute(sent, "rows", self.rows, first_partner)
        return sent

    def parts(self, *others):
        last = after(self.last, *others)
        mask = PLANE
        sets = range(len(self.kept))
        while mask < self.rows:
            total = sums(*[[*self.near(n, 0), self.close[2 * n], (last, n)] for n in sets])
            other = permute(total, "rows", self.rows, lambda i, m=mask: i ^ m)
            last = (last.astype(F32) + other.astype(F32)).astype(BF)
            mask *= 2
        return [[*self.near(n, 0), self.close[2 * n], (last, n)] for n in sets]


def total_kernel(sets, stacked, info_ref, *refs):
    outs = refs[4 * sets :]
    groups = refs[0].shape[0]
    base = 0
    for n in range(sets):
        arrays = refs[4 * n : 4 * n + 4]
        rows = arrays[0].shape[1]
        for k in range(groups):
            total = arrays[0][k].astype(F32)
            for array in arrays[1:]:
                total = total + array[k].astype(F32)
            if stacked:
                outs[0][info_ref[PLANE] ^ k, base : base + rows, :] = total.astype(BF)
            else:
                outs[k][base : base + rows, :] = total.astype(BF)
        base += rows


def totals(sets, info, stacked):
    heads, rows, cols = sets[0][0][0].shape[1:]
    specs = [
        pl.BlockSpec((None, heads, rows, cols), lambda g, slot=slot: (slot, 0, 0, 0))
        for pairs in sets
        for _, slot in pairs
    ]
    rows *= len(sets)
    shapes = [struct((heads, rows, cols), BF)] if stacked else [struct((rows, cols), BF)] * heads
    return call(
        functools.partial(total_kernel, len(sets), stacked),
        (1,),
        [SMEM_SPEC] + specs,
        [whole(*shape.shape) for shape in shapes],
        shapes,
        [info] + [array for pairs in sets for array, _ in pairs],
        us=2,
    )


def others_first(array, info):
    heads, *tail = array.shape

    def kernel(info_ref, in_ref, out_ref):
        for k in range(1, heads):
            out_ref[k - 1] = in_ref[info_ref[PLANE] ^ k]

    return call(
        kernel, (1,), [SMEM_SPEC, whole(heads, *tail)], whole(heads - 1, *tail),
        struct((heads - 1, *tail), array.dtype), (info, array), us=2,
    )


def to_heads(array):
    return lax.all_to_all(array, "heads", 0, 0, tiled=True)


def sum_arrays(arrays):
    return sums([(array[None], 0) for array in arrays])[0]


def sum_levels(array):
    return sums([(array, n) for n in range(array.shape[0])])[0]


SMEM_SPEC = pl.BlockSpec(memory_space=pltpu.SMEM)
VMEM_SPEC = pl.BlockSpec(memory_space=pltpu.VMEM)


def bias_rows(vectors, width):
    rest = jnp.stack([jnp.pad(v, (0, width - v.size)) for v in vectors])
    rows = []
    for _ in range(3):
        rounded = lax.reduce_precision(rest, 8, 7)
        rows.append(rounded.astype(BF))
        rest = rest - rounded
    rows = jnp.concatenate(rows, axis=0)
    return jnp.pad(rows, ((0, 16 - rows.shape[0]), (0, 0)))


def place_weights_kernel(count, parts, info_ref, *refs):
    owns = refs[:parts]
    pieces = refs[parts : parts + count]
    outs = refs[parts + count :]
    mine = pl.program_id(0) == 0

    @pl.when(mine)
    def _():
        for own, out in zip(owns, outs):
            out[...] = own[...]

    @pl.when(jnp.logical_not(mine))
    def _():
        base = 0
        for out in outs:
            if out.shape[0] < PLANE * 16:
                out[...] = pieces[0][base : base + out.shape[0], :]
                continue
            step = out.shape[0] // PLANE
            for n in range(count):
                start = pl.multiple_of(info_ref[n] * step, 16)
                out[pl.ds(start, step), :] = pieces[n][base : base + step, :]
            base += step


def place_weights(owns, pieces, info):
    count, parts = len(pieces), len(owns)
    others, _, cols = pieces[0].shape
    rows = sum(own.shape[0] if own.shape[0] < PLANE * 16 else own.shape[0] // PLANE for own in owns)

    def piece_index(g, info_ref):
        return (jnp.maximum(g - 1, 0), 0, 0)

    return pl.pallas_call(
        functools.partial(place_weights_kernel, count, parts),
        grid_spec=pltpu.PrefetchScalarGridSpec(
            num_scalar_prefetch=1,
            grid=(others + 1,),
            in_specs=[pl.BlockSpec(own.shape, lambda g, s: (0, 0)) for own in owns]
            + [pl.BlockSpec((None, rows, cols), piece_index)] * count,
            out_specs=[pl.BlockSpec((None, *own.shape), lambda g, s: (g, 0, 0)) for own in owns],
        ),
        out_shape=[struct((others + 1, *own.shape), BF) for own in owns],
        compiler_params=pltpu.CompilerParams(vmem_limit_bytes=VMEM_LIMIT),
        cost_estimate=estimate(3 * parts),
    )(info, *owns, *pieces)


def place_ffn_kernel(count, info_ref, *refs):
    up, down, turned = refs[count:]
    step = refs[0].shape[0] // 2
    for n in range(count):
        start = pl.multiple_of(info_ref[n] * step, 16)
        turned[pl.ds(start, step), :] = refs[n][:step, :].astype(F32)
        down[pl.ds(start, step), :] = refs[n][step:, :].astype(F32)
    up[...] = jnp.transpose(turned[...])


def place_ffn(pieces, info):
    rows, cols = pieces[0].shape
    count = len(pieces)
    hidden = count * rows // 2
    return pl.pallas_call(
        functools.partial(place_ffn_kernel, count),
        in_specs=[SMEM_SPEC] + [VMEM_SPEC] * count,
        out_specs=[VMEM_SPEC] * 2,
        out_shape=[struct((cols, hidden), F32), struct((hidden, cols), F32)],
        scratch_shapes=[pltpu.VMEM((hidden, cols), F32)],
        compiler_params=pltpu.CompilerParams(vmem_limit_bytes=VMEM_LIMIT),
        cost_estimate=estimate(4),
    )(info, *pieces)


def place_attention_kernel(count, cols, width, info_ref, *refs):
    out_qkv, out_o, out_b, vectors, bias = refs[count:]
    step = refs[0].shape[0] // 2
    for n in range(count):
        start = pl.multiple_of(info_ref[n] * step, 16)
        wide = refs[n][:step, :].astype(F32)

        @pl.when(start < cols)
        def _():
            out_qkv[pl.ds(start, step), :] = wide[:, :width]
            bias[pl.ds(start, step), :] = wide[:, width:]

        @pl.when(start >= cols)
        def _():
            out_o[pl.ds(pl.multiple_of(start - cols, 16), step), :] = wide[:, :width]

        @pl.when(start == cols)
        def _():
            groups = width // 128
            for v in range(vectors.shape[0]):
                for j in range(groups):
                    row = v * groups + j
                    vectors[v : v + 1, j * 128 : (j + 1) * 128] = wide[row : row + 1, width:]

        wide = refs[n][step:, :].astype(F32)
        out_qkv[pl.ds(cols + start, step), :] = wide[:, :width]
        bias[pl.ds(cols + start, step), :] = wide[:, width:]
    row = jnp.transpose(bias[...])[0:1, :]
    for j in range(3):
        out_b[j : j + 1, :] = row[:, j * cols : (j + 1) * cols]


def place_attention(pieces, info, cols, width):
    count = len(pieces)
    return pl.pallas_call(
        functools.partial(place_attention_kernel, count, cols, width),
        in_specs=[SMEM_SPEC] + [VMEM_SPEC] * count,
        out_specs=[VMEM_SPEC] * 4,
        out_shape=[
            struct((3 * cols, width), F32),
            struct((cols, width), F32),
            struct((3, cols), F32),
            struct((7, width), F32),
        ],
        scratch_shapes=[pltpu.VMEM((3 * cols, 128), F32)],
        compiler_params=pltpu.CompilerParams(vmem_limit_bytes=VMEM_LIMIT),
        cost_estimate=estimate(3),
    )(info, *pieces)


def head_sums(values, heads, hd):
    row = lax.broadcasted_iota(jnp.int32, (heads * hd, 128), 0)
    lane = lax.broadcasted_iota(jnp.int32, (heads * hd, 128), 1)
    own = ((row >= lane * hd) & (row < (lane + 1) * hd)).astype(F32).astype(BF)
    high = values.astype(BF)
    low = (values - high.astype(F32)).astype(BF)
    return dot(high, own) + dot(low, own)


def phi_of(raw, halves, head, feats, scale):
    part_raw = raw[:, head * feats : (head + 1) * feats]
    return jnp.exp(scale * part_raw - halves[:, head : head + 1]) * feats ** (-0.5)


def half_norms(vectors, heads, hd, scale):
    wide = vectors.astype(F32)
    return 0.5 * scale * scale * head_sums(wide * wide, heads, hd)


def edge_rows(first, last, head):
    lane = lax.broadcasted_iota(jnp.int32, (first.shape[0], 32), 1)
    return jnp.where(lane == head, first, 0.0) + jnp.where(lane == 16 + head, last, 0.0)


def edge_left(value, norm, first, last, head):
    return jnp.concatenate(
        [value * first, value * last, edge_rows(norm * first, norm * last, head)], axis=1
    ).astype(BF)


def edge_states(values, norms, phi, heads, hd, feats):
    first_values, last_values = values
    cols = heads * hd
    left = jnp.concatenate([first_values, last_values, norms], axis=1).astype(BF)
    state = dot_tn(left, phi)
    row = lax.broadcasted_iota(jnp.int32, (16, feats), 0)
    out = []
    for n in range(2):
        base = 2 * cols + 16 * n
        rows = [state[n * cols + h * hd : n * cols + (h + 1) * hd, h * feats : (h + 1) * feats] for h in range(heads)]
        total = jnp.zeros((16, feats), F32)
        for h in range(heads):
            total = jnp.where(row == h, state[base : base + 16, h * feats : (h + 1) * feats], total)
        out.append(jnp.concatenate([*rows, total], axis=0).astype(BF))
    return out


def put_edges(edge_ref, firsts, lasts, level, group):
    for m in range(1, edge_ref.shape[0]):
        place = level ^ m

        @pl.when(place > level)
        def _():
            edge_ref[place, group ^ m] = lasts

        @pl.when(place < level)
        def _():
            edge_ref[place, group ^ m] = firsts


def take_edges(came_ref, match_ref, level):
    left = right = None
    count = came_ref.shape[0] - 1
    for m in range(count):
        wide = came_ref[level ^ (m + 1)].astype(F32)
        a, b = wide * match_ref[m], wide * match_ref[count + m]
        left = a if left is None else left + a
        right = b if right is None else right + b
    return left.astype(BF), right.astype(BF)


def stack_edges(f, l, h, hd, cols):
    return jnp.concatenate(
        [f[h * hd : (h + 1) * hd], l[h * hd : (h + 1) * hd], f[cols:], l[cols:]], axis=0
    )


def with_one(value):
    lane = lax.broadcasted_iota(jnp.int32, value.shape, 1)
    return jnp.concatenate([value, jnp.where(lane == 0, 1.0, 0.0).astype(value.dtype)], axis=1)


def keys_kernel(heads, hd, feats, info_ref, x_ref, w_ref, b_ref, om_ref, ends_ref, *refs):
    *before, kv_ref, phi_ref, edge_ref = refs
    cols = heads * hd
    scale = hd ** (-0.25)
    kv = (dot_nt(x_ref[...], w_ref[...]) + b_ref[...]).astype(BF)
    kv_ref[...] = kv
    raw = dot(kv[:, :cols], om_ref[...])
    first, last = ends_ref[:, 0:1], ends_ref[:, 1:2]
    halves = half_norms(kv[:, :cols], heads, hd, scale)
    for h in range(heads):
        phi_ref[:, h * feats : (h + 1) * feats] = phi_of(raw, halves, h, feats, scale).astype(BF)
    values = kv[:, cols:].astype(F32)
    lane = lax.broadcasted_iota(jnp.int32, (kv.shape[0], 32), 1)
    firsts, lasts = edge_states(
        (values * first, values * last), jnp.where(lane < 16, first, last), phi_ref[...], heads, hd, feats
    )
    if not before:
        edge_ref[0] = firsts
        edge_ref[1] = lasts
        return
    group = pl.program_id(0) + 1
    put_edges(edge_ref, firsts, lasts, info_ref[PLANE], group)

    @pl.when(group == 1)
    def _():
        put_edges(edge_ref, before[-1][0], before[-1][1], info_ref[PLANE], 0)


def queries_kernel(heads, hd, feats, x_ref, w_ref, b_ref, om_ref, same_ref, kv_ref, phik_ref, *refs):
    q_ref, phi_ref, nd_ref = refs[-3:]
    cols = heads * hd
    scale = hd ** (-0.25)
    q = (dot_nt(x_ref[...], w_ref[:cols, :]) + b_ref[...]).astype(BF)
    q_ref[...] = q
    raw = dot(q, om_ref[...])
    same = same_ref[...]
    halves = half_norms(q, heads, hd, scale)
    for h in range(heads):
        phi = phi_of(raw, halves, h, feats, scale).astype(BF)
        phi_ref[:, h * feats : (h + 1) * feats] = phi
        scores = dot_nt(phi, phik_ref[:, h * feats : (h + 1) * feats]).astype(BF) * same
        value = kv_ref[:, cols + h * hd : cols + (h + 1) * hd]
        nd_ref[:, 2 * h * hd : 2 * (h + 1) * hd] = dot(scores, with_one(value))


def feature_back(dphi, phi, vectors, om, heads, hd, feats, scale):
    cols = heads * hd
    lows = []
    for h in range(heads):
        grad_raw = dphi[h] * phi[:, h * feats : (h + 1) * feats].astype(F32)
        lows.append((scale * grad_raw).astype(BF))
    through = dot_nt(jnp.concatenate(lows, axis=1), om)
    wide = vectors.astype(F32)
    lane = lax.broadcasted_iota(jnp.int32, wide.shape, 1)
    total = through[:, cols : cols + 1]
    for h in range(1, heads):
        total = jnp.where(lane >= h * hd, through[:, cols + h : cols + h + 1], total)
    return through[:, :cols] - scale * total * wide


def weight_grad(grad_ref, rows, left, right):
    width = right.shape[1]
    lane = lax.broadcasted_iota(jnp.int32, (left.shape[0], 128), 1)
    grad_ref[rows, :width] = dot_tn(left, right).astype(BF)
    grad_ref[rows, width:] = dot_tn(left, jnp.where(lane == 0, 1.0, 0.0).astype(BF)).astype(BF)


def put_slices(source_ref, base, sent_refs, kept_ref, info_ref, placed=True):
    step = source_ref.shape[0] // PLANE
    half = PLANE // 2
    for n in range(PLANE):
        if n < half:
            out = kept_ref.at[n]
        else:
            out = sent_refs[n - half] if len(sent_refs) > 1 else sent_refs[0].at[n - half]
        start = pl.multiple_of(jnp.where(placed, info_ref[n], n) * step, 16)
        out[base : base + step, :] = source_ref[pl.ds(start, step), :]


def queries_back_kernel(
    heads, hd, feats, info_ref, dnd_ref, q_ref, phiq_ref, kv_ref, phik_ref, cf_ref, cl_ref, om_ref, same_ref,
    ends_ref, att_ref, x_ref, one_ref, one_sums_ref, two_sums_ref, bup_ref, dq_ref, dphik_ref, dv_ref, sent_ref, kept_ref,
    grad_ref,
):
    cols = heads * hd
    scale = hd ** (-0.25)
    first, last = ends_ref[:, 0:1], ends_ref[:, 1:2]
    same = same_ref[...]
    dphis, dvs = [], []
    for h in range(heads):
        phiq = phiq_ref[:, h * feats : (h + 1) * feats]
        phik = phik_ref[:, h * feats : (h + 1) * feats]
        value = with_one(kv_ref[:, cols + h * hd : cols + (h + 1) * hd])
        dnd = dnd_ref[:, 2 * h * hd : 2 * (h + 1) * hd]
        dscore = dot_nt(dnd, value).astype(BF) * same
        wide = dnd.astype(F32)
        left = edge_left(wide[:, :hd], wide[:, hd : hd + 1], first, last, h)
        stack = stack_edges(cf_ref[...], cl_ref[...], h, hd, cols)
        dphis.append(dot(dscore, phik) + dot(left, stack))
        dscore_t = dot_nt(value, dnd).astype(BF) * same
        score_t = dot_nt(phik, phiq).astype(BF) * same
        dphik_ref[:, h * feats : (h + 1) * feats] = dot(dscore_t, phiq).astype(BF)
        dvs.append(dot(score_t, dnd)[:, :hd])
    dv_ref[...] = jnp.concatenate(dvs, axis=1)
    dq = feature_back(dphis, phiq_ref[...], q_ref[...], om_ref[...], heads, hd, feats, scale)
    dq = dq.astype(BF)
    dq_ref[...] = dq
    weight_grad(grad_ref, slice(0, cols), dq, x_ref[...])
    width = one_ref.shape[1]
    vectors = [one_sums_ref[n : n + 1, :] for n in range(3)] + [two_sums_ref[n : n + 1, :] for n in range(3)]
    vectors = vectors + [bup_ref[...]]
    block = [v[:, n : n + 128] for v in vectors for n in range(0, width, 128)]
    step = grad_ref.shape[0] // PLANE
    block.append(jnp.zeros((step - len(block), 128), F32))
    block = jnp.concatenate(block, axis=0).astype(BF)
    grad_ref[cols:, :width] = dot_tn(att_ref[...], one_ref[...]).astype(BF)
    for n in range(cols, 2 * cols, step):
        grad_ref[n : n + step, width:] = block
    put_slices(grad_ref, 0, [sent_ref], kept_ref, info_ref)


def keys_back_kernel(
    heads, hd, feats, info_ref, match_ref, kv_ref, phik_ref, dphik_ref, dv_ref, came_ref, om_ref, ends_ref, x_ref, *refs
):
    dkv_ref, *sent, kept_ref, grad_ref = refs
    cols = heads * hd
    scale = hd ** (-0.25)
    first, last = ends_ref[:, 0:1], ends_ref[:, 1:2]
    rf, rl = take_edges(came_ref, match_ref, info_ref[PLANE])
    dphis, dvs = [], []
    for h in range(heads):
        phik = phik_ref[:, h * feats : (h + 1) * feats]
        value = kv_ref[:, cols + h * hd : cols + (h + 1) * hd].astype(F32)
        stack = stack_edges(rf, rl, h, hd, cols)
        dphis.append(
            dphik_ref[:, h * feats : (h + 1) * feats].astype(F32) + dot(edge_left(value, 1.0, first, last, h), stack)
        )
        far = dot_nt(phik, stack[: 2 * hd])
        dvs.append(dv_ref[:, h * hd : (h + 1) * hd] + first * far[:, :hd] + last * far[:, hd:])
    dk = feature_back(dphis, phik_ref[...], kv_ref[:, :cols], om_ref[...], heads, hd, feats, scale)
    dkv = jnp.concatenate([dk] + dvs, axis=1).astype(BF)
    dkv_ref[...] = dkv
    weight_grad(grad_ref, slice(0, 2 * cols), dkv, x_ref[...])
    put_slices(grad_ref, 0, sent, kept_ref, info_ref)


def tokens_kernel(cols, dq_ref, dkv_ref, qo_ref, kv_ref, one_ref, out_ref):
    back = dot(dq_ref[...], qo_ref[:cols, :]) + dot(dkv_ref[...], kv_ref[...])

    @pl.when(pl.program_id(0) == 0)
    def _():
        out_ref[...] = one_ref[...] + back

    @pl.when(pl.program_id(0) > 0)
    def _():
        out_ref[...] += back


def norm_of(hidden):
    average = jnp.mean(hidden, axis=-1, keepdims=True)
    centred = hidden - average
    inverse = lax.rsqrt(jnp.mean(centred * centred, axis=-1, keepdims=True) + EPSILON)
    return centred * inverse, inverse


def norm_back(grad_in, normed, inverse, gain):
    scaled = grad_in * gain
    centred = (
        scaled
        - jnp.mean(scaled, axis=-1, keepdims=True)
        - normed * jnp.mean(scaled * normed, axis=-1, keepdims=True)
    )
    return centred * inverse


def column_sums(arrays, rows):
    sums = [jnp.sum(a, axis=0, keepdims=True) for a in arrays]
    return jnp.concatenate(sums + [jnp.zeros((rows - len(sums), sums[0].shape[1]), F32)], axis=0)


def gelu_both(v):
    gate = 0.5 + 0.5 * lax.erf(v * 0.5**0.5)
    bell = jnp.exp(-0.5 * v * v) * (2.0 * jnp.pi) ** (-0.5)
    return v * gate, gate + v * bell


def ffn_copies(own_up, own_down, pieces, up_ref, down_ref, sems, k):
    if k == 0:
        return [
            pltpu.make_async_copy(own_up, up_ref.at[0], sems.at[0, 0]),
            pltpu.make_async_copy(own_down, down_ref.at[0], sems.at[0, 1]),
        ]
    step = up_ref.shape[1] // PLANE
    base = pieces[0].shape[1] - 2 * step
    copies = []
    for n, piece in enumerate(pieces):
        for part_n, ref in enumerate((up_ref, down_ref)):
            copies.append(
                pltpu.make_async_copy(
                    piece.at[k - 1, pl.ds(base + part_n * step, step)],
                    ref.at[k, pl.ds(n * step, step)],
                    sems.at[k, 2 * n + part_n],
                )
            )
    return copies


def middle_kernel(heads, hd, feats, info_ref, match_ref, phi_ref, nd_ref, came_ref, ends_ref, wo_ref, x_ref, vec_ref, bup_ref, cot_ref, *refs):
    own_up, own_down, *pieces = refs[: 2 + PLANE]
    (
        att_ref, cf_ref, cl_ref, out_ref, gradb_ref, one_out, onelow_ref, sums1_ref, sums2_ref, dnd_ref, edge_ref,
        sent1_ref, sent2_ref, sent3_ref, sent4_ref, kept_ref,
        acc, first_low, normed_one, inverse_one, act_s, slope_s, two, two_low, att_s, den_s, up_s, down_s, grad_s, sems,
    ) = refs[2 + PLANE :]
    sent = [sent1_ref, sent2_ref, sent3_ref, sent4_ref]
    groups = att_s.shape[0]
    stage = pl.program_id(0) // groups
    g = pl.program_id(0) % groups
    cols = heads * hd
    t = acc.shape[0]
    level = info_ref[PLANE]
    final = g == groups - 1

    @pl.when(pl.program_id(0) == 0)
    def _():
        for k in range(groups):
            for copy in ffn_copies(own_up, own_down, pieces, up_s, down_s, sems, k):
                copy.start()

    def first_add(value, start):
        @pl.when(g == 0)
        def _():
            acc[...] = start() + value

        @pl.when(g > 0)
        def _():
            acc[...] += value

    @pl.when(stage == 0)
    def _():
        first, last = ends_ref[:, 0:1], ends_ref[:, 1:2]
        cf, cl = take_edges(came_ref, match_ref, level)
        cf_ref[...] = cf
        cl_ref[...] = cl
        lane = lax.broadcasted_iota(jnp.int32, (t, 128), 1)
        dens = jnp.zeros((t, 128), F32)
        outs = []
        for h in range(heads):
            far = dot_nt(phi_ref[:, h * feats : (h + 1) * feats], stack_edges(cf, cl, h, hd, cols))
            nd = nd_ref[:, 2 * h * hd : 2 * (h + 1) * hd]
            num = nd[:, :hd] + first * far[:, :hd] + last * far[:, hd : 2 * hd]
            den = (
                nd[:, hd : hd + 1]
                + first * far[:, 2 * hd + h : 2 * hd + h + 1]
                + last * far[:, 2 * hd + 16 + h : 2 * hd + 17 + h]
            )
            outs.append(num / den)
            dens = dens + jnp.where(lane == h, den, 0.0)
        att = jnp.concatenate(outs, axis=1).astype(BF)
        att_ref[...] = att
        att_s[g] = att
        den_s[g] = dens
        first_add(dot(att, wo_ref[...]), lambda: x_ref[...].astype(F32) + vec_ref[0:1, :])

        @pl.when(final)
        def _():
            normed, inverse = norm_of(acc[...])
            normed_one[...] = normed
            inverse_one[...] = jnp.broadcast_to(inverse, inverse_one.shape)
            first_low[...] = (normed * vec_ref[1:2, :] + vec_ref[2:3, :]).astype(BF)

    @pl.when(stage == 1)
    def _():
        for k in range(groups):

            @pl.when(g == k)
            def _():
                for copy in ffn_copies(own_up, own_down, pieces, up_s, down_s, sems, k):
                    copy.wait()

        act, slope = gelu_both(dot_nt(first_low[...], up_s[g]) + bup_ref[...])
        act = act.astype(BF)
        act_s[g] = act
        slope_s[g] = slope.astype(BF)
        first_add(
            dot(act, down_s[g]),
            lambda: normed_one[...] * vec_ref[1:2, :] + vec_ref[2:3, :] + vec_ref[3:4, :],
        )

        @pl.when(final)
        def _():
            normed, inverse = norm_of(acc[...])
            gain = vec_ref[4:5, :]
            out_ref[...] = (normed * gain + vec_ref[5:6, :]).astype(BF)
            grad_in = cot_ref[...].astype(F32)
            grad = norm_back(grad_in, normed, inverse, gain)
            two[...] = grad
            two_low[...] = grad.astype(BF)
            sums2_ref[...] = column_sums([grad_in * normed, grad_in, grad], 8)

    @pl.when(stage == 2)
    def _():
        step = up_s.shape[1] // PLANE
        low = two_low[...]
        dpre = dot_nt(low, down_s[g]) * slope_s[g].astype(F32)
        gradb_ref[...] = jnp.sum(dpre, axis=0, keepdims=True)
        pre_low = dpre.astype(BF)
        grad_s[...] = dot_tn(pre_low, first_low[...]).astype(BF)
        put_slices(grad_s, 0, sent, kept_ref, info_ref, g == 0)
        grad_s[...] = dot_tn(act_s[g], low).astype(BF)
        put_slices(grad_s, step, sent, kept_ref, info_ref, g == 0)
        first_add(dot(pre_low, up_s[g]), lambda: two[...])

        @pl.when(final)
        def _():
            grad_in = acc[...]
            normed = normed_one[...]
            one = norm_back(grad_in, normed, inverse_one[:, 0:1], vec_ref[1:2, :])
            one_out[...] = one
            onelow_ref[...] = one.astype(BF)
            sums1_ref[...] = column_sums([grad_in * normed, grad_in, one], 8)

    @pl.when(stage == 3)
    def _():
        first, last = ends_ref[:, 0:1], ends_ref[:, 1:2]
        datt = dot_nt(onelow_ref[...], wo_ref[...])
        dens = den_s[g]
        lane = lax.broadcasted_iota(jnp.int32, (t, cols), 1)
        den = dens[:, 0:1]
        for h in range(1, heads):
            den = jnp.where(lane >= h * hd, dens[:, h : h + 1], den)
        dnum = datt / den
        dden = -head_sums(dnum * att_s[g].astype(F32), heads, hd)
        one_lane = lax.broadcasted_iota(jnp.int32, (t, hd), 1) == 0
        for h in range(heads):
            dnd_ref[:, 2 * h * hd : 2 * (h + 1) * hd] = jnp.concatenate(
                [dnum[:, h * hd : (h + 1) * hd], jnp.where(one_lane, dden[:, h : h + 1], 0.0)], axis=1
            ).astype(BF)
        norms = jnp.concatenate([dden[:, :16] * first, dden[:, :16] * last], axis=1)
        firsts, lasts = edge_states((dnum * first, dnum * last), norms, phi_ref[...], heads, hd, feats)
        put_edges(edge_ref, firsts, lasts, level, g)


def body(
    rows, heads,
    tokens, segment_ids, w_qkv, b_qkv, w_out, b_out, gain_one, bias_one, w_up, b_up, w_down, b_down,
    gain_two, bias_two, omega, cotangent,
):
    rank = lax.axis_index("rows")
    level = lax.axis_index("heads")
    hd, feats = omega.shape
    _, length, width = tokens.shape
    cols = w_qkv.shape[2]
    nh = cols // hd
    hidden = w_up.shape[1]
    slots = plane_slots(rank)
    me = slots[0]
    info = jnp.stack(slots + [level]).astype(jnp.int32)
    x = tokens[0]

    def slice_of(array):
        step = array.shape[0] // PLANE
        return lax.dynamic_slice_in_dim(array, me * step, step, 0)

    def from_levels(piece):
        return to_levels([piece] * (heads - 1))

    wt = jnp.transpose(w_qkv, (1, 2, 0)).reshape(3 * cols, width)
    own_kv = wt[cols:]
    own_bias = bias_rows([b_qkv.reshape(-1), b_up], width)
    own_qo = jnp.concatenate([wt[:cols], w_out], axis=0)
    own_up = w_up.T
    rows_of = 2 * cols // PLANE
    kv_slice = lax.dynamic_slice_in_dim(wt, cols + me * rows_of, rows_of, 0)
    q_slice = lax.dynamic_slice_in_dim(wt, jnp.minimum(me, PLANE // 2 - 1) * rows_of, rows_of, 0)
    o_slice = lax.dynamic_slice_in_dim(w_out, jnp.maximum(me - PLANE // 2, 0) * rows_of, rows_of, 0)
    qo_slice = jnp.where(me < PLANE // 2, q_slice, o_slice)
    near = from_levels(jnp.concatenate([kv_slice, qo_slice, own_bias], axis=0))
    rest = jnp.concatenate([slice_of(own_up), slice_of(w_down)], axis=0)
    rest = jnp.broadcast_to(rest[None], (heads, *rest.shape))
    own_bias_qkv = b_qkv.reshape(1, -1)

    segments = lax.dynamic_slice_in_dim(segment_ids[0], level * length, length, 0)
    by_level = segment_ids[0].reshape(heads, length)
    firsts, lasts = by_level[:, 0], by_level[:, -1]
    my_first, my_last = segments[0], segments[-1]
    ends = jnp.stack([segments == my_first, segments == my_last], axis=1).astype(F32)
    same = (segments[:, None] == segments[None, :]).astype(BF)
    index = jnp.arange(1, heads) ^ level
    there = index[:, None] == jnp.arange(heads)[None, :]
    index_first = jnp.sum(jnp.where(there, firsts[None], 0), axis=1)
    index_last = jnp.sum(jnp.where(there, lasts[None], 0), axis=1)
    match = jnp.concatenate(
        [(index < level) & (index_last == my_first), (index > level) & (index_first == my_last)]
    ).astype(F32)

    eye = jnp.eye(nh, dtype=BF)
    om = (eye[:, None, :, None] * omega[None, :, None, :]).reshape(cols, nh * feats)
    om_back = jnp.concatenate(
        [om, jnp.repeat(eye, feats, axis=1), jnp.zeros((16 - nh, nh * feats), BF)], axis=0
    )
    edge = cols + 16
    dims = (nh, hd, feats)
    t = length
    aug = width + 128

    half = PLANE // 2
    edge_shape = struct((heads, heads, edge, feats), BF)
    edge_spec = pl.BlockSpec((heads, None, edge, feats), lambda g: (0, g, 0, 0))

    def slot_spec(count, wide):
        return pl.BlockSpec((half, None, count, wide), lambda g: (0, g, 0, 0))

    def slot_shape(count, wide):
        return struct((half, heads, count, wide), BF)

    def of_groups(base, *shape):
        return part(*shape, base=base) if base else whole(*shape)

    def keys(base, count, weights, bias, *before):
        return call(
            functools.partial(keys_kernel, *dims),
            (count,),
            [
                SMEM_SPEC, whole(t, width), of_groups(base, 2 * cols, width), of_groups(base, 1, 2 * cols),
                whole(cols, nh * feats), whole(t, 2),
            ]
            + [ANY_SPEC, ANY_SPEC, whole(2, edge, feats)][: len(before)],
            [
                part(t, 2 * cols, base=base),
                part(t, nh * feats, base=base),
                whole(*edge_shape.shape) if base else whole(2, edge, feats),
            ],
            [
                struct((heads, t, 2 * cols), BF),
                struct((heads, t, nh * feats), BF),
                edge_shape if base else struct((2, edge, feats), BF),
            ],
            (info, x, weights, bias, om, ends, *before),
            us=3 * count,
            aliases={6: 0, 7: 1} if base else None,
        )

    def queries(base, count, weights, bias, kv, phi_k, *before):
        return call(
            functools.partial(queries_kernel, *dims),
            (count,),
            [
                whole(t, width), of_groups(base, 2 * cols, width), of_groups(base, 1, cols),
                whole(cols, nh * feats), whole(t, t),
                part(t, 2 * cols, base=base), part(t, nh * feats, base=base),
            ]
            + [ANY_SPEC] * len(before),
            [
                part(t, cols, base=base), part(t, nh * feats, base=base), part(t, 2 * cols, base=base),
            ],
            [
                struct((heads, t, cols), BF),
                struct((heads, t, nh * feats), BF),
                struct((heads, t, 2 * cols), F32),
            ],
            (x, weights, bias, om, same, kv, phi_k, *before),
            us=3 * count,
            aliases={7 + n: n for n in range(len(before))},
        )

    near_rest = to_heads(after(rest, near))
    near = jnp.stack(near)
    p1 = permute(near, "rows", rows, first_partner)
    p2 = permute(near, "rows", rows, second_partner)
    own_keys = keys(0, 1, after(own_kv, near), own_bias_qkv[:, cols:])
    p3 = permute(p1, "rows", rows, second_partner)
    own_queries = queries(0, 1, after(own_qo, p1), own_bias_qkv[:, :cols], *own_keys[:2])
    pieces = gather_cores([near, p1, p2, after(p3, own_queries)], rows)
    kv_w, qo_w, bias = place_weights([own_kv, own_qo, own_bias], pieces, info)
    bias = bias.astype(F32)
    bias = bias[:, 0:2] + (bias[:, 2:4] + bias[:, 4:6])
    bias_qkv = bias[:, 0:1, : 3 * cols]
    bias_q = bias_qkv[:, :, :cols]
    bias_kv = bias_qkv[:, :, cols:]
    at_slot = (jnp.stack(slots)[:, None] == jnp.arange(PLANE)[None, :])[None, :, :, None]
    by_slice = bias[1:, 1, :hidden].reshape(heads - 1, 1, PLANE, hidden // PLANE)
    by_slot = jnp.sum(jnp.where(at_slot, by_slice, 0.0), axis=2).reshape(heads - 1, 1, hidden)
    bias_up = jnp.concatenate([b_up[None, None], by_slot], axis=0)

    own_keys = after(own_keys, own_queries)
    kv, phi_k, edges = keys(1, heads - 1, kv_w, bias_kv, *own_keys)
    came = to_heads(edges)
    q, phi_q, local = queries(1, heads - 1, qo_w, bias_q, kv, phi_k, *own_queries)
    chips_ffn = gather_chips(others_first(after(near_rest, edges), info), rows)
    rest_w = gather_cores([*chips_ffn[:3], after(chips_ffn[3], phi_q)], rows)
    step = hidden // PLANE
    vec = jnp.pad(
        jnp.stack([b_out, gain_one, bias_one, b_down, gain_two, bias_two]), ((0, 2), (0, 0))
    )

    def staged(shape, *stages, at=0):
        def index(s):
            stage, g = s // heads, s % heads
            group = jnp.where(stage > stages[-1], heads - 1, 0)
            for n in stages:
                group = jnp.where(stage == n, g, group)
            if len(stages) == 2:
                between = (stage > stages[0]) & (stage < stages[1])
                group = jnp.where(between, heads - 1, group)
            return (group, at, 0)

        return pl.BlockSpec((None, *shape), lambda s: index(s))

    def staged_slots(shape, stage):
        spec = staged((1, 1), stage)
        return pl.BlockSpec((shape[0], None, *shape[1:]), lambda s: (0, spec.index_map(s)[0], 0, 0))

    tokens_bf, tokens_f32 = struct((t, width), BF), struct((t, width), F32)
    (
        att, far_f, far_l, layer_output, grad_b_up, grad_one, one_low, sums_one, sums_two, dnd, edges, *sent, kept,
    ) = call(
        functools.partial(middle_kernel, *dims),
        (4 * heads,),
        [
            SMEM_SPEC, SMEM_SPEC, staged((t, nh * feats), 0, 3), staged((t, 2 * cols), 0),
            staged_slots((heads, edge, feats), 0), whole(t, 2), staged((cols, width), 0, 3, at=1), whole(t, width),
            whole(8, width), staged((1, hidden), 1), whole(t, width), *[ANY_SPEC] * (2 + PLANE),
        ],
        [
            staged((t, cols), 0), staged((edge, feats), 0), staged((edge, feats), 0), whole(t, width),
            staged((1, hidden), 2), whole(t, width), whole(t, width), whole(8, width), whole(8, width),
            staged((t, 2 * cols), 3), whole(*edge_shape.shape), *[staged((2 * step, width), 2)] * half,
            staged_slots((half, 2 * step, width), 2),
        ],
        [
            struct((heads, t, cols), BF),
            struct((heads, edge, feats), BF),
            struct((heads, edge, feats), BF),
            tokens_bf,
            struct((heads, 1, hidden), F32),
            tokens_f32,
            tokens_bf,
            struct((8, width), F32),
            struct((8, width), F32),
            struct((heads, t, 2 * cols), BF),
            edge_shape,
            *[struct((heads, 2 * step, width), BF)] * half,
            slot_shape(2 * step, width),
        ],
        (
            info, match, phi_q, local, came, ends, qo_w, x, vec, bias_up, cotangent[0], own_up, w_down, *rest_w,
        ),
        us=50,
        scratch=[
            pltpu.VMEM((t, width), F32),
            pltpu.VMEM((t, width), BF),
            pltpu.VMEM((t, width), F32),
            pltpu.VMEM((t, 128), F32),
            pltpu.VMEM((heads, t, hidden), BF),
            pltpu.VMEM((heads, t, hidden), BF),
            pltpu.VMEM((t, width), F32),
            pltpu.VMEM((t, width), BF),
            pltpu.VMEM((heads, t, cols), BF),
            pltpu.VMEM((heads, t, 128), F32),
            pltpu.VMEM((heads, hidden, width), BF),
            pltpu.VMEM((heads, hidden, width), BF),
            pltpu.VMEM((hidden, width), BF),
            pltpu.SemaphoreType.DMA((heads, 2 * PLANE)),
        ],
        limit=60 * 1024 * 1024,
    )
    by_slot = grad_b_up[1:, 0].reshape(heads - 1, PLANE, 1, step)
    by_slice = jnp.sum(jnp.where(at_slot, by_slot, 0.0), axis=1).reshape(heads - 1, 1, hidden)
    grad_b_up = jnp.concatenate([grad_b_up[:1], by_slice], axis=0)

    back = to_heads(edges)
    ffn = Reduction(rows, together=False)
    ffn.cores([a[None] for a in sent], kept)
    ffn_sent = ffn.second()
    slice_rows = 2 * cols // PLANE
    dq, dphi_k, dv, *qo = call(
        functools.partial(queries_back_kernel, *dims),
        (heads,),
        [
            SMEM_SPEC, part(t, 2 * cols), part(t, cols), part(t, nh * feats), part(t, 2 * cols),
            part(t, nh * feats), part(edge, feats), part(edge, feats), whole(cols + 16, nh * feats), whole(t, t),
            whole(t, 2), part(t, cols), whole(t, width), whole(t, width), whole(8, width),
            whole(8, width), part(1, hidden),
        ],
        [
            part(t, cols), part(t, nh * feats), part(t, cols), *[slot_spec(slice_rows, aug)] * 2,
        ],
        [
            struct((heads, t, cols), BF),
            struct((heads, t, nh * feats), BF),
            struct((heads, t, cols), F32),
            *[slot_shape(slice_rows, aug)] * 2,
        ],
        (
            info, after(dnd, ffn_sent), q, phi_q, kv, phi_k, far_f, far_l, om_back, same, ends, att, x, one_low,
            sums_one, sums_two, grad_b_up,
        ),
        us=20,
        scratch=[pltpu.VMEM((2 * cols, aug), BF)],
    )
    red = Reduction(rows)
    red.cores(qo[:1], qo[1])
    back = after(back, ffn.first(dv))
    dkv, *kv_red = call(
        functools.partial(keys_back_kernel, *dims),
        (heads,),
        [
            SMEM_SPEC, SMEM_SPEC, part(t, 2 * cols), part(t, nh * feats), part(t, nh * feats), part(t, cols),
            edge_spec, whole(cols + 16, nh * feats), whole(t, 2), whole(t, width),
        ],
        [part(t, 2 * cols), *[part(slice_rows, aug)] * half, slot_spec(slice_rows, aug)],
        [
            struct((heads, t, 2 * cols), BF),
            *[struct((heads, slice_rows, aug), BF)] * half,
            slot_shape(slice_rows, aug),
        ],
        (info, match, kv, phi_k, dphi_k, dv, back, om_back, ends, x),
        us=12,
        scratch=[pltpu.VMEM((2 * cols, aug), BF)],
    )
    red.cores([a[None] for a in kv_red[:half]], kv_red[half])
    sent = red.second(dkv, ffn.last)
    (ffn_total,) = totals(ffn.parts(sent), info, True)
    grad_tokens = call(
        functools.partial(tokens_kernel, cols),
        (heads,),
        [part(t, cols), part(t, 2 * cols), part(2 * cols, width), part(2 * cols, width), whole(t, width)],
        whole(t, width),
        tokens_f32,
        (dq, after(dkv, ffn_total), qo_w, kv_w, grad_one),
        us=5,
    )
    sent = red.first(grad_tokens)
    ffn_pieces = plane_gather(sum_levels(after(to_heads(ffn_total), sent)), rows)
    own_total, *total = totals(red.parts(), info, False)
    out_up, out_down = place_ffn(ffn_pieces, info)
    chips = gather_chips(sum_arrays([own_total, *to_levels(total)]), rows)
    pieces = gather_cores(after(chips, out_up), rows)

    out_qkv, out_o, out_b, outs = place_attention(pieces, info, cols, width)
    out_qkv = jnp.transpose(out_qkv.reshape(3, cols, width), (2, 0, 1))
    return (
        layer_output[None],
        grad_tokens[None],
        out_qkv,
        out_b,
        out_o,
        outs[2],
        outs[0],
        outs[1],
        out_up,
        outs[6],
        out_down,
        outs[5],
        outs[3],
        outs[4],
    )


def solution(mesh):
    return jax.shard_map(
        functools.partial(body, mesh.shape["rows"], mesh.shape["heads"]),
        mesh=mesh,
        in_specs=(
            P("rows", "heads", None),
            P("rows", None),
            P(None, None, "heads"),
            P(None, "heads"),
            P("heads", None),
            P(),
            P(),
            P(),
            P(None, "heads"),
            P("heads"),
            P("heads", None),
            P(),
            P(),
            P(),
            P(),
            P("rows", "heads", None),
        ),
        out_specs=(
            P("rows", "heads", None),
            P("rows", "heads", None),
            P(None, None, "heads"),
            P(None, "heads"),
            P("heads", None),
            P(),
            P(),
            P(),
            P(None, "heads"),
            P("heads"),
            P("heads", None),
            P(),
            P(),
            P(),
        ),
        check_vma=False,
    )
```
